32 devices in a mesh: section: 4 (over y, x), seq: 8 (over z, core).
Axes of the slice: x: 2, y: 2, z: 4, core: 2. Of those that a mesh axis runs over, the one named last changes fastest.
Arguments:
- inputs: bfloat16 [4, 512, 2048], P(None, 'seq'), may hold values from -6 to 6
- doc_starts: int32 [4, 2], replicated, may hold values from 1 to 511, as said below
- valid_mask: int32 [4, 512], P(None, 'seq'), may hold values 0 or 1
- cotangent: bfloat16 [4, 512, 2048], P(None, 'seq'), may hold values from -6 to 6
- prev_state: bfloat16 [4, 2, 2560], replicated, may hold values from -6 to 6
- prev_inputs: bfloat16 [4, 2, 3, 2560], replicated, may hold values from -6 to 6
- rec_gain: bfloat16 [2, 2048], P(None, 'seq'), may hold values from 0.25 to 1.75
- in_weight: bfloat16 [2, 2048, 2560], P(None, 'seq'), may hold values from -0.125 to 0.125
- side_weight: bfloat16 [2, 2048, 2560], P(None, 'seq'), may hold values from -0.125 to 0.125
- out_weight: bfloat16 [2, 2560, 2048], P(None, 'seq'), may hold values from -0.3125 to 0.3125
- rate_blocks: bfloat16 [2, 10, 256, 256], P(None, None, 'seq'), may hold values from -0.375 to 0.375
- inflow_blocks: bfloat16 [2, 10, 256, 256], P(None, None, 'seq'), may hold values from -0.375 to 0.375
- rate_bias: bfloat16 [2, 2560], P(None, 'seq'), may hold values from -4 to 4
- inflow_bias: bfloat16 [2, 2560], P(None, 'seq'), may hold values from -4 to 4
- conv_taps: bfloat16 [2, 4, 2560], P(None, None, 'seq'), may hold values from -3 to 3
- conv_bias: bfloat16 [2, 2560], P(None, 'seq'), may hold values from -3 to 3
- lru_param: bfloat16 [2, 2560], P(None, 'seq'), may hold values from 4 to 11
- mlp_gain: bfloat16 [2, 2048], P(None, 'seq'), may hold values from 0.25 to 1.75
- gate_weight: bfloat16 [2, 2048, 6144], P(None, 'seq'), may hold values from -0.125 to 0.125
- up_weight: bfloat16 [2, 2048, 6144], P(None, 'seq'), may hold values from -0.125 to 0.125
- down_weight: bfloat16 [2, 6144, 2048], P(None, 'seq'), may hold values from -0.15625 to 0.15625
Outputs:
- outputs: bfloat16 [4, 512, 2048], P('section', 'seq')
- input_grad: bfloat16 [4, 512, 2048], P('section', 'seq')
- rec_gain_grad: float32 [2, 2048], P(None, 'seq')
- in_weight_grad: float32 [2, 2048, 2560], P(None, 'seq')
- side_weight_grad: float32 [2, 2048, 2560], P(None, 'seq')
- out_weight_grad: float32 [2, 2560, 2048], P(None, 'seq')
- rate_blocks_grad: float32 [2, 10, 256, 256], P(None, None, 'seq')
- inflow_blocks_grad: float32 [2, 10, 256, 256], P(None, None, 'seq')
- rate_bias_grad: float32 [2, 2560], P(None, 'seq')
- inflow_bias_grad: float32 [2, 2560], P(None, 'seq')
- conv_taps_grad: float32 [2, 4, 2560], P(None, None, 'seq')
- conv_bias_grad: float32 [2, 2560], P(None, 'seq')
- lru_param_grad: float32 [2, 2560], P(None, 'seq')
- mlp_gain_grad: float32 [2, 2048], P(None, 'seq')
- gate_weight_grad: float32 [2, 2048, 6144], P(None, 'seq')
- up_weight_grad: float32 [2, 2048, 6144], P(None, 'seq')
- down_weight_grad: float32 [2, 6144, 2048], P(None, 'seq')
The draws below stay inside these ranges and needn't reach their ends.
Inputs may be any that keep to these rules, and one draw needn't show every extreme that they name: `doc_starts`: each row holds two document starts in increasing order: the first on the stream's first 64 tokens, the second on its last 64 tokens; tokens before the first start continue the document of prev_state and prev_inputs.
All inputs are finite; a program needn't handle non-finite values. No bound on the sum of `valid_mask` on one device may be relied on, other than what follows from the above.
Results may differ from the reference program's by a relative error of at most 0.022.
Values may be sent and summed in bfloat16 or wider, within the bound.
A program may use at most 512 MiB of HBM per device.

```python
import jax
import jax.numpy as jnp
from jax import lax

D = 2048
W = 2560
FF = 6144
BLOCKS = 10
BW = 256
CONV = 4
LAYERS = 2
TOK_DEV = 64
MICRO = 4
TOKENS = 512


def draw_doc_starts(key, part):
    key = jax.random.fold_in(key, 7)
    head_key, tail_key = jax.random.split(key)
    head_start = jax.random.randint(head_key, (MICRO, 1), 1, TOK_DEV)
    tail_start = jax.random.randint(tail_key, (MICRO, 1), TOKENS - TOK_DEV, TOKENS)
    return jnp.concatenate([head_start, tail_start], axis=1).astype(jnp.int32)


def draw_lru_param(key, part):
    key = jax.random.fold_in(key, 11)
    pick_key, slow_key, fast_key = jax.random.split(key, 3)
    slow_share = 0.5
    slow_pick = jax.random.uniform(pick_key, (LAYERS, W)) < slow_share
    slow_rate = jnp.exp(jax.random.uniform(slow_key, (LAYERS, W), minval=jnp.log(0.5 / TOKENS), maxval=jnp.log(2.0 / TOKENS)))
    fast_rate = jnp.exp(jax.random.uniform(fast_key, (LAYERS, W), minval=jnp.log(0.04), maxval=jnp.log(0.12)))
    rate_value = jnp.where(slow_pick, slow_rate, fast_rate)
    return (-jnp.log(jnp.expm1(rate_value / 8.0))).astype(jnp.bfloat16)


def with_ends(values, rng, smallest, top_value):
    place = [jax.random.randint(jax.random.fold_in(rng, axis), (), 0, length) for axis, length in enumerate(values.shape)]
    widest = values.shape.index(max(values.shape))
    next_to = place[:widest] + [(place[widest] + 1) % values.shape[widest]] + place[widest + 1:]
    return values.at[tuple(place)].set(smallest).at[tuple(next_to)].set(top_value)


def steps_of(rng, shape, cuts, smallest, largest):
    gain, own = 1.0, jax.random.fold_in(rng, 6)
    for position, parts in cuts:
        heights = jnp.exp(jax.random.uniform(jax.random.fold_in(own, position), (parts,), jnp.float32, smallest / len(cuts), largest / len(cuts)))
        gain = gain * jnp.repeat(heights, shape[position] // parts).reshape([-1 if axis == position else 1 for axis in range(len(shape))])
    return gain


def bell_draw(rng, shape, scale, most, pieces=(), held_as=jnp.bfloat16):
    values = jax.random.normal(rng, shape, jnp.float32) * scale
    if len(pieces) > 0:
        values = steps_of(rng, shape, pieces, -0.22, 0.18) * values
    return jnp.clip(values, min=-most, max=most).astype(held_as)


def setup_inputs(seed: int = 0) -> dict:
    key_list = jax.random.split(jax.random.key(seed), 22)
    return {
        "inputs": bell_draw(key_list[0], (MICRO, TOKENS, D), 1.0, 6.0, ((1, 8),)),
        "doc_starts": draw_doc_starts(jax.random.fold_in(key_list[21], 71), 0),
        "valid_mask": with_ends((jax.random.randint(key_list[2], (MICRO, TOKENS), 0, 4) < 3).astype(jnp.int32), jax.random.fold_in(key_list[2], 1), 0, 1),
        "cotangent": bell_draw(key_list[3], (MICRO, TOKENS, D), 1.0, 6.0, ((1, 8),)),
        "prev_state": bell_draw(key_list[4], (MICRO, LAYERS, W), 1.0, 6.0),
        "prev_inputs": bell_draw(key_list[5], (MICRO, LAYERS, 3, W), 1.0, 6.0),
        "rec_gain": jnp.clip(1.0 + 0.15 * jax.random.normal(key_list[6], (LAYERS, D), jnp.float32), 0.25, 1.75).astype(jnp.bfloat16),
        "in_weight": bell_draw(key_list[7], (LAYERS, D, W), D ** -0.5, 0.125, ((1, 8),)),
        "side_weight": bell_draw(key_list[8], (LAYERS, D, W), D ** -0.5, 0.125, ((1, 8),)),
        "out_weight": bell_draw(key_list[9], (LAYERS, W, D), (W // 8) ** -0.5, 0.3125, ((1, 8),)),
        "rate_blocks": bell_draw(key_list[10], (LAYERS, BLOCKS, BW, BW), BW ** -0.5, 0.375, ((2, 8),)),
        "inflow_blocks": bell_draw(key_list[11], (LAYERS, BLOCKS, BW, BW), BW ** -0.5, 0.375, ((2, 8),)),
        "rate_bias": bell_draw(key_list[12], (LAYERS, W), 1.0, 4.0, ((1, 8),)),
        "inflow_bias": bell_draw(key_list[13], (LAYERS, W), 1.0, 4.0, ((1, 8),)),
        "conv_taps": bell_draw(key_list[14], (LAYERS, CONV, W), CONV ** -0.5, 3.0, ((2, 8),)),
        "conv_bias": bell_draw(key_list[15], (LAYERS, W), 0.5, 3.0, ((1, 8),)),
        "lru_param": draw_lru_param(jax.random.fold_in(key_list[21], 71), 0),
        "mlp_gain": jnp.clip(1.0 + 0.15 * jax.random.normal(key_list[17], (LAYERS, D), jnp.float32), 0.25, 1.75).astype(jnp.bfloat16),
        "gate_weight": bell_draw(key_list[18], (LAYERS, D, FF), D ** -0.5, 0.125, ((1, 8),)),
        "up_weight": bell_draw(key_list[19], (LAYERS, D, FF), D ** -0.5, 0.125, ((1, 8),)),
        "down_weight": bell_draw(key_list[20], (LAYERS, FF, D), (FF // 4) ** -0.5, 0.15625, ((1, 8),)),
    }


@jax.custom_vjp
def low(v):
    return lax.optimization_barrier(v.astype(jnp.bfloat16)).astype(jnp.float32)

@jax.custom_vjp
def low_back(v):
    return v

def low_keep(v):
    return (low(v), None)

def low_pass(kept, grad):
    return (grad,)

def back_keep(v):
    return (v, None)

def back_low(kept, grad):
    return (low(grad),)
low.defvjp(low_keep, low_pass)
low_back.defvjp(back_keep, back_low)
epsilon = 1e-06
rate_scale = 8.0

def matmul(first_rows, second_rows):
    return jnp.dot(first_rows, second_rows, precision=lax.Precision.HIGHEST, preferred_element_type=jnp.float32)

def rms_scale(values, gain_row):
    factor = lax.rsqrt(lax.optimization_barrier(jnp.mean(values * values, axis=-1, keepdims=True)) + epsilon)
    return values * factor * gain_row

def lru_terms(pre_rate, pre_inflow, mixed_rows, lru_wide, resets):
    rate_gate = jax.nn.sigmoid(pre_rate)
    inflow = jax.nn.sigmoid(pre_inflow)
    log_decay = -rate_scale * rate_gate * jax.nn.softplus(-lru_wide)
    keep_state = 1.0 - resets[:, None]
    decays = jnp.exp(log_decay) * keep_state
    factor = resets[:, None] + keep_state * jnp.sqrt(-jnp.expm1(2.0 * log_decay))
    return (decays, factor * inflow * mixed_rows)

def block_product(values, blocks):
    shaped = values.reshape(values.shape[0], blocks.shape[0], blocks.shape[1])
    result = jnp.einsum('tbi,bij->tbj', shaped, blocks, precision=lax.Precision.HIGHEST)
    return result.reshape(values.shape[0], -1)

def shifted(values, amount):
    return jnp.concatenate([jnp.zeros((amount,), values.dtype), values[:-amount]])

def stream_masks(starts):
    places = jnp.arange(TOKENS, dtype=jnp.int32)
    resets = jnp.any(places[:, None] == starts[None, :], axis=1).astype(jnp.float32)
    first_keep = 1.0 - resets
    second_keep = first_keep * (1.0 - shifted(resets, 1))
    third_keep = second_keep * (1.0 - shifted(resets, 2))
    return (resets, (first_keep, second_keep, third_keep))

def linear_scan(decays, drives, state_init):

    def advance(carried, entry_item):
        fresh = entry_item[0] * carried + entry_item[1]
        return (fresh, fresh)
    return lax.scan(jax.checkpoint(advance), state_init, (decays, drives))[1]

def recurrent_block(x_wide, params, state_init, rim_init, resets, keep_rows):
    gain_row, in_weight, side_weight, out_weight, rate_blocks, inflow_blocks, rate_bias, inflow_bias, conv_taps, conv_bias, lru_param = params
    first_keep, second_keep, third_keep = keep_rows
    normed = low(rms_scale(x_wide, gain_row))
    inner_rows = low_back(low(matmul(normed, in_weight)))
    branch_pre = low_back(matmul(normed, side_weight))
    side_gate = jax.nn.gelu(branch_pre)
    extended = jnp.concatenate([rim_init, inner_rows], axis=0)
    mixed_rows = conv_bias + conv_taps[0] * extended[3:] + conv_taps[1] * extended[2:-1] * first_keep[:, None] + conv_taps[2] * extended[1:-2] * second_keep[:, None] + conv_taps[3] * extended[:-3] * third_keep[:, None]
    mixed_rows = low_back(mixed_rows)
    mixed_low = low(mixed_rows)
    pre_rate = low_back(block_product(mixed_low, rate_blocks) + rate_bias)
    pre_inflow = low_back(block_product(mixed_low, inflow_blocks) + inflow_bias)
    decays, drives = lru_terms(pre_rate, pre_inflow, mixed_rows, lru_param, resets)
    states = linear_scan(decays, drives, state_init)
    gated_rows = low(states * side_gate)
    return low_back(matmul(gated_rows, out_weight))

def mlp_block(x_wide, params):
    gain_row, gate_weight, up_weight, down_weight = params
    normed = low(rms_scale(x_wide, gain_row))
    gate_pre = low_back(matmul(normed, gate_weight))
    up_pre = low_back(matmul(normed, up_weight))
    hidden = low(jax.nn.gelu(gate_pre) * up_pre)
    return low_back(matmul(hidden, down_weight))

def forward(inputs, rec_params, mlp_params, prev_state, prev_inputs, doc_starts):
    finished = []
    for batch_index in range(MICRO):
        resets, keep_rows = stream_masks(doc_starts[batch_index])
        stream = inputs[batch_index]
        for layer_index in range(LAYERS):
            rec_layer = tuple((param_all[layer_index] for param_all in rec_params))
            mlp_layer = tuple((param_all[layer_index] for param_all in mlp_params))
            branch = recurrent_block(stream, rec_layer, prev_state[batch_index, layer_index], prev_inputs[batch_index, layer_index], resets, keep_rows)
            stream = low_back(low(stream + branch))
            branch = mlp_block(stream, mlp_layer)
            if layer_index + 1 < LAYERS:
                stream = low_back(low(stream + branch))
            else:
                stream = low(stream + branch)
        finished.append(stream)
    return jnp.stack(finished)

def reference(inputs, doc_starts, valid_mask, cotangent, prev_state, prev_inputs, rec_gain, in_weight, side_weight, out_weight, rate_blocks, inflow_blocks, rate_bias, inflow_bias, conv_taps, conv_bias, lru_param, mlp_gain, gate_weight, up_weight, down_weight):
    rec_params = tuple((param_all.astype(jnp.float32) for param_all in (rec_gain, in_weight, side_weight, out_weight, rate_blocks, inflow_blocks, rate_bias, inflow_bias, conv_taps, conv_bias, lru_param)))
    mlp_params = tuple((param_all.astype(jnp.float32) for param_all in (mlp_gain, gate_weight, up_weight, down_weight)))
    states_wide = prev_state.astype(jnp.float32)
    rims_wide = prev_inputs.astype(jnp.float32)

    def run_all(stream_in, rec_all, mlp_all):
        return forward(stream_in, rec_all, mlp_all, states_wide, rims_wide, doc_starts)
    results, pullback = jax.vjp(run_all, inputs.astype(jnp.float32), rec_params, mlp_params)
    masked = cotangent.astype(jnp.float32) * valid_mask[:, :, None].astype(jnp.float32)
    input_grad, rec_grads, mlp_grads = pullback(masked)
    return (results.astype(jnp.bfloat16), input_grad.astype(jnp.bfloat16), rec_grads[0], rec_grads[1], rec_grads[2], rec_grads[3], rec_grads[4], rec_grads[5], rec_grads[6], rec_grads[7], rec_grads[8], rec_grads[9], rec_grads[10], mlp_grads[0], mlp_grads[1], mlp_grads[2], mlp_grads[3])
```

```python
from functools import partial

import jax
import jax.numpy as jnp
import numpy as np
from jax import lax
from jax.experimental import pallas as pl
from jax.experimental.pallas import tpu as pltpu
from jax.sharding import PartitionSpec as P


epsilon = 1e-06
rate_scale = 8.0
MESH = pl.DeviceIdType.MESH
VMEM_LIMIT = 60 * 1024 * 1024
f32 = jnp.float32
bf16 = jnp.bfloat16


def line_place():
    place = lax.axis_index("seq")
    chip = place // 2
    core = place % 2
    return place, chip, core, chip * 2 + 1 - core


def enter(chips, mate):
    _, chip, core, _ = line_place()
    barrier = pltpu.get_barrier_semaphore()
    pl.semaphore_signal(barrier, inc=1, device_id={"seq": mate}, device_id_type=MESH)
    for k in range(1, chips):
        peer = ((chip + k) % chips) * 2 + core
        pl.semaphore_signal(barrier, inc=1, device_id={"seq": peer}, device_id_type=MESH)
    pl.semaphore_wait(barrier, chips)


def exchange_body(mode, count, refs):
    chips = count // 2
    has_sum = mode != "start"
    has_gather = mode != "last"
    refs = list(refs)
    take = refs.pop
    part_ref = take(0) if has_sum else None
    x_ref = take(0)
    dy_ref = take(0) if mode in ("back", "last") else None
    gain_ref = take(0)
    out_ref = take(0) if has_gather else None
    rows_ref = take(0) if has_sum else None
    dgain_ref = take(0) if mode in ("back", "last") else None
    if has_sum:
        pair_ref, staged_ref, landed_ref, pair_sem, sum_sem = (take(0) for _ in range(5))
    if has_gather:
        gather_sem, mate_sem = (take(0) for _ in range(2))
    place, chip, core, mate = line_place()
    enter(chips, mate)

    if has_sum:
        pair_copies = []
        for k in list(range(1, chips)) + [0]:
            to_chip = (chip + k) % chips
            copy = pltpu.make_async_remote_copy(
                src_ref=part_ref.at[to_chip * 2 + 1 - core],
                dst_ref=pair_ref.at[k],
                send_sem=pair_sem.at[0, k],
                recv_sem=pair_sem.at[1, k],
                device_id={"seq": mate},
                device_id_type=MESH,
            )
            copy.start()
            pair_copies.append((k, copy))
        sum_copies = []
        total = None
        for k, copy in pair_copies:
            to_chip = (chip + k) % chips
            copy.wait_recv()
            both = part_ref[to_chip * 2 + core].astype(f32) + pair_ref[k].astype(f32)
            if k == 0:
                total = both
            else:
                staged_ref[k] = both.astype(bf16)
                send = pltpu.make_async_remote_copy(
                    src_ref=staged_ref.at[k],
                    dst_ref=landed_ref.at[k],
                    send_sem=sum_sem.at[0, k],
                    recv_sem=sum_sem.at[1, k],
                    device_id={"seq": to_chip * 2 + core},
                    device_id_type=MESH,
                )
                send.start()
                sum_copies.append((k, send))
        for k, send in sum_copies:
            send.wait_recv()
            total = total + landed_ref[k].astype(f32)

    gain = gain_ref[...]
    x_wide = x_ref[...].astype(f32)
    if mode in ("start", "forward"):
        if mode == "forward":
            x_low = (x_wide + total).astype(bf16)
            rows_ref[...] = x_low
            x_wide = x_low.astype(f32)
        scale = lax.rsqrt(jnp.mean(x_wide * x_wide, axis=-1, keepdims=True) + epsilon)
        sent = (x_wide * scale * gain).astype(bf16)
    else:
        scale = lax.rsqrt(jnp.mean(x_wide * x_wide, axis=-1, keepdims=True) + epsilon)
        scaled = total * gain
        inner_mean = jnp.mean(scaled * x_wide, axis=-1, keepdims=True)
        back = scale * scaled - x_wide * (scale * scale * scale * inner_mean)
        dgain_ref[...] = jnp.sum(total * x_wide * scale, axis=0, keepdims=True)
        sent = (dy_ref[...].astype(f32) + back).astype(bf16)
        rows_ref[...] = sent

    if has_gather:
        out_ref[place] = sent
        sends = []
        for k in range(1, chips):
            copy = pltpu.make_async_remote_copy(
                src_ref=out_ref.at[place],
                dst_ref=out_ref.at[place],
                send_sem=gather_sem.at[0, k],
                recv_sem=gather_sem.at[1, k],
                device_id={"seq": ((chip + k) % chips) * 2 + core},
                device_id_type=MESH,
            )
            copy.start()
            sends.append(copy)
        mates = []

        def to_mate(slot, k):
            copy = pltpu.make_async_remote_copy(
                src_ref=out_ref.at[slot],
                dst_ref=out_ref.at[slot],
                send_sem=mate_sem.at[0, k],
                recv_sem=mate_sem.at[1, k],
                device_id={"seq": mate},
                device_id_type=MESH,
            )
            copy.start()
            mates.append(copy)

        to_mate(place, 0)
        for k in range(1, chips):
            sends[k - 1].wait_recv()
            to_mate(((chip + chips - k) % chips) * 2 + core, k)
        for copy in mates:
            copy.wait()
        for copy in sends:
            copy.wait_send()
    if has_sum:
        for _, copy in pair_copies:
            copy.wait_send()
        for _, send in sum_copies:
            send.wait_send()


def exchange(mode, collective_id, part, x, dy, gain):
    rows, width = x.shape
    count = lax.axis_size("seq")
    chips = count // 2
    has_sum = mode != "start"
    has_gather = mode != "last"
    backward = mode in ("back", "last")
    operands = ([part.reshape(count, rows, width)] if has_sum else []) + [x]
    operands += ([dy] if backward else []) + [gain.astype(f32).reshape(1, width)]
    shapes = []
    if has_gather:
        shapes.append(jax.ShapeDtypeStruct((count, rows, width), bf16))
    if has_sum:
        shapes.append(jax.ShapeDtypeStruct((rows, width), bf16))
    if backward:
        shapes.append(jax.ShapeDtypeStruct((1, width), f32))
    scratch = []
    if has_sum:
        scratch += [pltpu.VMEM((chips, rows, width), bf16)] * 3
        scratch += [pltpu.SemaphoreType.DMA((2, chips))] * 2
    if has_gather:
        scratch += [pltpu.SemaphoreType.DMA((2, chips))] * 2
    whole = pl.BlockSpec(memory_space=pltpu.VMEM)
    outs = pl.pallas_call(
        lambda *refs: exchange_body(mode, count, refs),
        out_shape=shapes,
        in_specs=[whole] * len(operands),
        out_specs=[whole] * len(shapes),
        scratch_shapes=scratch,
        compiler_params=pltpu.CompilerParams(
            collective_id=collective_id, has_side_effects=True, vmem_limit_bytes=VMEM_LIMIT
        ),
    )(*operands)
    outs = list(outs)
    if has_gather:
        outs[0] = outs[0].reshape(count * rows, width)
    return outs


def swap_body(count, x_ref, out_ref, send_sem, recv_sem, own_sem):
    place = lax.axis_index("seq")
    barrier = pltpu.get_barrier_semaphore()
    for k in range(1, count):
        peer = (place + k) % count
        pl.semaphore_signal(barrier, inc=1, device_id={"seq": peer}, device_id_type=MESH)
    pl.semaphore_wait(barrier, count - 1)
    copies = []
    for k in range(1, count):
        peer = (place + k) % count
        copy = pltpu.make_async_remote_copy(
            src_ref=x_ref.at[peer],
            dst_ref=out_ref.at[place],
            send_sem=send_sem.at[k],
            recv_sem=recv_sem.at[k],
            device_id={"seq": peer},
            device_id_type=MESH,
        )
        copy.start()
        copies.append(copy)
    own = pltpu.make_async_copy(x_ref.at[place], out_ref.at[place], own_sem)
    own.start()
    own.wait()
    for copy in copies:
        copy.wait()


def swap(x, collective_id):
    count = lax.axis_size("seq")
    return pl.pallas_call(
        partial(swap_body, count),
        out_shape=jax.ShapeDtypeStruct(x.shape, x.dtype),
        in_specs=[pl.BlockSpec(memory_space=pl.ANY)],
        out_specs=pl.BlockSpec(memory_space=pl.ANY),
        scratch_shapes=[
            pltpu.SemaphoreType.DMA((count,)),
            pltpu.SemaphoreType.DMA((count,)),
            pltpu.SemaphoreType.DMA,
        ],
        compiler_params=pltpu.CompilerParams(collective_id=collective_id, has_side_effects=True),
    )(x)


def less_exp(doubled):
    small = doubled * (
        1.0
        - doubled
        * (
            0.5
            - doubled
            * (1.0 / 6 - doubled * (1.0 / 24 - doubled * (1.0 / 120 - doubled * (1.0 / 720))))
        )
    )
    return jnp.where(doubled < 0.25, small, 1.0 - jnp.exp(-doubled))


def gelu_pair(v):
    c = np.float32(np.sqrt(2 / np.pi))
    t = jnp.tanh(c * (v + 0.044715 * v * v * v))
    slope = 0.5 * (1.0 + t) + 0.5 * v * (1.0 - t * t) * c * (1.0 + 3 * 0.044715 * v * v)
    return 0.5 * v * (1.0 + t), slope


def dot(a, b):
    return jnp.dot(a, b, preferred_element_type=f32)


def dot_t(a, b):
    return lax.dot_general(a, b, (((1,), (1,)), ((), ())), preferred_element_type=f32)


def dot_rows(a, b):
    return lax.dot_general(a, b, (((0,), (0,)), ((), ())), preferred_element_type=f32)


def soft(lru):
    spread = jnp.maximum(-lru, 0.0) + jnp.log1p(jnp.exp(-jnp.abs(lru)))
    return spread, -1.0 / (1.0 + jnp.exp(lru))


def middle_forward_body(
    rows,
    width,
    is_ref,
    marks_ref,
    blocks_ref,
    small_ref,
    rim_ref,
    first_ref,
    gated_ref,
    mixed_ref,
    rate_ref,
    inflow_ref,
    states_ref,
    before_ref,
    ext,
    decays,
    drives,
    carry,
):
    @pl.when(pl.program_id(0) == 0)
    def _():
        ext[0:8] = rim_ref[...]
        carry[...] = first_ref[...]

    block = width // 2
    inner = is_ref[:, :width].astype(bf16).astype(f32)
    ext[8 : 8 + rows] = inner
    reset = marks_ref[:, 0:1]
    mixed = (
        small_ref[6:7]
        + small_ref[2:3] * inner
        + small_ref[3:4] * (ext[7 : 7 + rows] * marks_ref[:, 1:2])
        + small_ref[4:5] * (ext[6 : 6 + rows] * marks_ref[:, 2:3])
        + small_ref[5:6] * (ext[5 : 5 + rows] * marks_ref[:, 3:4])
    )
    ext[0:8] = ext[rows : rows + 8]
    mixed_ref[...] = mixed
    low = mixed.astype(bf16)
    for b in range(2):
        lanes = slice(b * block, (b + 1) * block)
        rate_ref[:, lanes] = dot(low[:, lanes], blocks_ref[0, b]) + small_ref[0:1, lanes]
        inflow_ref[:, lanes] = dot(low[:, lanes], blocks_ref[1, b]) + small_ref[1:2, lanes]
    spread, _ = soft(small_ref[7:8])
    log_decay = (-rate_scale * spread) * jax.nn.sigmoid(rate_ref[...])
    kept = 1.0 - reset
    decays[...] = jnp.exp(log_decay) * kept
    factor = reset + kept * jnp.sqrt(less_exp(-2.0 * log_decay))
    drives[...] = factor * jax.nn.sigmoid(inflow_ref[...]) * mixed

    place = lax.broadcasted_iota(jnp.int32, (8, width), 0)

    def step(j, last):
        at = pl.ds(pl.multiple_of(j * 8, 8), 8)
        a, h = decays[at], drives[at]
        for k in (1, 2, 4):
            inside = place >= k
            h = jnp.where(inside, a * pltpu.roll(h, k, 0) + h, h)
            a = jnp.where(inside, a * pltpu.roll(a, k, 0), a)
        h = h + a * last
        states_ref[at] = h
        before_ref[at] = jnp.where(place >= 1, pltpu.roll(h, 1, 0), last)
        return jnp.broadcast_to(h[7:8], (8, width))

    carry[...] = lax.fori_loop(0, rows // 8, step, carry[...])
    gated_ref[...] = (states_ref[...] * gelu_pair(is_ref[:, width:])[0]).astype(bf16)


def middle_backward_body(
    rows,
    width,
    dg_ref,
    is_ref,
    mixed_ref,
    rate_ref,
    inflow_ref,
    states_ref,
    before_ref,
    marks_ref,
    blocks_ref,
    small_ref,
    rim_ref,
    own_ref,
    dib_ref,
    drate_ref,
    dinflow_ref,
    sums_ref,
    dm_ext,
    decays,
    dstates,
    carry,
):
    @pl.when(pl.program_id(0) == 0)
    def _():
        dm_ext[rows : rows + 8] = jnp.zeros((8, width), f32)
        carry[...] = jnp.zeros((8, width), f32)
        sums_ref[...] = jnp.zeros_like(sums_ref)

    block = width // 2
    own = own_ref[0:1]
    reset = marks_ref[:, 0:1]
    kept = 1.0 - reset
    side, slope = gelu_pair(is_ref[:, width:])
    d_gated = dg_ref[...]
    dib_ref[:, width:] = (d_gated * states_ref[...] * slope * own).astype(bf16)
    dstates[...] = d_gated * side
    spread, spread_slope = soft(small_ref[7:8])
    rate = jax.nn.sigmoid(rate_ref[...])
    log_decay = (-rate_scale * spread) * rate
    decays[...] = jnp.exp(log_decay) * kept

    place = lax.broadcasted_iota(jnp.int32, (8, width), 0)

    def step(j, after):
        at = pl.ds(pl.multiple_of(rows - 8 - j * 8, 8), 8)
        own_decay, h = decays[at], dstates[at]
        a = jnp.where(place < 7, pltpu.roll(own_decay, 7, 0), 1.0)
        for k in (1, 2, 4):
            inside = place < 8 - k
            h = jnp.where(inside, a * pltpu.roll(h, 8 - k, 0) + h, h)
            a = jnp.where(inside, a * pltpu.roll(a, 8 - k, 0), a)
        h = h + a * after
        dstates[at] = h
        return jnp.broadcast_to((own_decay * h)[0:1], (8, width))

    carry[...] = lax.fori_loop(0, rows // 8, step, carry[...])

    d_h = dstates[...]
    mixed = mixed_ref[...]
    inflow = jax.nn.sigmoid(inflow_ref[...])
    root = jnp.sqrt(less_exp(-2.0 * log_decay))
    factor = reset + kept * root
    decay = decays[...]
    twice = jnp.exp(2.0 * log_decay)
    d_log = d_h * before_ref[...] * decay - d_h * inflow * mixed * kept * (twice / root)
    d_lru = jnp.sum(d_log * rate, axis=0, keepdims=True) * (-rate_scale * spread_slope)
    d_rate = (d_log * (-rate_scale * spread) * rate * (1.0 - rate)).astype(bf16)
    through = d_h * factor
    d_inflow = (through * mixed * inflow * (1.0 - inflow)).astype(bf16)
    drate_ref[...] = d_rate
    dinflow_ref[...] = d_inflow
    for b in range(2):
        lanes = slice(b * block, (b + 1) * block)
        dm_ext[0:rows, lanes] = (
            ((through * inflow)[:, lanes] + dot_t(d_rate[:, lanes], blocks_ref[0, b]) + dot_t(d_inflow[:, lanes], blocks_ref[1, b]))
            .astype(bf16)
            .astype(f32)
        )
    d_mixed = dm_ext[0:rows]
    inner = is_ref[:, :width].astype(bf16).astype(f32)
    shifted = [d_mixed] + [dm_ext[k : k + rows] * marks_ref[:, 3 + k : 4 + k] for k in (1, 2, 3)]
    d_inner = small_ref[2:3] * shifted[0]
    for k in (1, 2, 3):
        d_inner = d_inner + small_ref[2 + k : 3 + k] * shifted[k]
    dib_ref[:, :width] = (d_inner * own).astype(bf16)

    def add(row, value):
        sums_ref[row : row + 1] += value

    add(0, jnp.sum(d_rate.astype(f32), axis=0, keepdims=True))
    add(1, jnp.sum(d_inflow.astype(f32), axis=0, keepdims=True))
    for k in range(4):
        add(2 + k, jnp.sum(shifted[k] * inner, axis=0, keepdims=True))
    add(6, jnp.sum(d_mixed, axis=0, keepdims=True))
    add(7, d_lru)

    @pl.when(pl.program_id(0) == pl.num_programs(0) - 1)
    def _():
        for k in (1, 2, 3):
            for t in range(k):
                add(2 + k, dm_ext[t : t + 1] * marks_ref[t : t + 1, k : k + 1] * rim_ref[8 + t - k : 9 + t - k])

    dm_ext[rows : rows + 8] = dm_ext[0:8]


def row_spec(rows, width, steps, reverse):
    if reverse:
        return pl.BlockSpec((rows, width), lambda i: (steps - 1 - i, 0))
    return pl.BlockSpec((rows, width), lambda i: (i, 0))


def whole_spec(shape):
    return pl.BlockSpec(shape, lambda i: (0,) * len(shape))


def middle_forward(wide, marks, blocks, small, rim, first):
    tokens, width = wide.shape[0], wide.shape[1] // 2
    rows = min(256, tokens)
    steps = tokens // rows
    here = partial(row_spec, rows, steps=steps, reverse=False)
    whole = [blocks, small, rim, first]
    kinds = [bf16, f32, f32, f32, f32, f32]
    return pl.pallas_call(
        partial(middle_forward_body, rows, width),
        grid=(steps,),
        out_shape=[jax.ShapeDtypeStruct((tokens, width), kind) for kind in kinds],
        in_specs=[here(2 * width), here(8)] + [whole_spec(a.shape) for a in whole],
        out_specs=[here(width)] * 6,
        scratch_shapes=[
            pltpu.VMEM((rows + 8, width), f32),
            pltpu.VMEM((rows, width), f32),
            pltpu.VMEM((rows, width), f32),
            pltpu.VMEM((8, width), f32),
        ],
        compiler_params=pltpu.CompilerParams(vmem_limit_bytes=VMEM_LIMIT),
    )(wide, marks, *whole)


def middle_backward(d_gated, wide, saved, marks, blocks, small, rim, own):
    tokens, width = d_gated.shape
    rows = min(256, tokens)
    steps = tokens // rows
    here = partial(row_spec, rows, steps=steps, reverse=True)
    whole = [blocks, small, rim, own]
    return pl.pallas_call(
        partial(middle_backward_body, rows, width),
        grid=(steps,),
        out_shape=[
            jax.ShapeDtypeStruct((tokens, 2 * width), bf16),
            jax.ShapeDtypeStruct((tokens, width), bf16),
            jax.ShapeDtypeStruct((tokens, width), bf16),
            jax.ShapeDtypeStruct((8, width), f32),
        ],
        in_specs=[here(width), here(2 * width)] + [here(width)] * 5 + [here(8)] + [whole_spec(a.shape) for a in whole],
        out_specs=[here(2 * width), here(width), here(width), whole_spec((8, width))],
        scratch_shapes=[
            pltpu.VMEM((rows + 8, width), f32),
            pltpu.VMEM((rows, width), f32),
            pltpu.VMEM((rows, width), f32),
            pltpu.VMEM((8, width), f32),
        ],
        compiler_params=pltpu.CompilerParams(vmem_limit_bytes=VMEM_LIMIT),
    )(d_gated, wide, *saved, marks, *whole)


def stream_marks(starts, tokens):
    places = jnp.arange(tokens + 3, dtype=jnp.int32)

    def resets(p):
        return jnp.any(p[:, None] == starts[None, :], axis=1).astype(f32)

    first = 1.0 - resets(places)
    second = first * (1.0 - resets(places - 1))
    third = second * (1.0 - resets(places - 2))
    inside = (places < tokens).astype(f32)
    columns = [resets(places)[:tokens], first[:tokens], second[:tokens], third[:tokens]]
    for k, keep in ((1, first), (2, second), (3, third)):
        columns.append((keep * inside)[k : k + tokens])
    columns.append(jnp.zeros((tokens,), f32))
    return jnp.stack(columns, axis=1)


def on_device(
    inputs,
    doc_starts,
    valid_mask,
    cotangent,
    prev_state,
    prev_inputs,
    rec_gain,
    in_weight,
    side_weight,
    out_weight,
    rate_blocks,
    inflow_blocks,
    rate_bias,
    inflow_bias,
    conv_taps,
    conv_bias,
    lru_param,
    mlp_gain,
    gate_weight,
    up_weight,
    down_weight,
):
    sections = lax.axis_size("section")
    section = lax.axis_index("section")
    count = lax.axis_size("seq")
    place = lax.axis_index("seq")
    layers, d_rows, lru_width = in_weight.shape
    model = inputs.shape[2]
    tokens = inputs.shape[1] * count
    hidden_part = down_weight.shape[1]
    own_width = out_weight.shape[1]
    block_count, block_rows, block_width = rate_blocks.shape[1:]
    window = 2 * block_width
    quarter = d_rows // sections
    block_quarter = block_rows // sections
    pad_rows = -(-block_quarter * 4 * block_width // (2 * window) // 16) * 16
    first_block = [min(q * own_width // block_width, block_count - 2) for q in range(count)]
    owner = [min(q for q in range(count) if first_block[q] <= b <= first_block[q] + 1) for b in range(block_count)]
    block_start = jnp.asarray(first_block, jnp.int32)[place]
    offset = place * own_width - block_start * block_width
    window_start = block_start * block_width
    next_id = iter(range(64))

    def quarter_of(a, axis):
        size = a.shape[axis] // sections
        return lax.dynamic_slice_in_dim(a, section * size, size, axis)

    def window_of(a, axis):
        return lax.dynamic_slice_in_dim(a, window_start, window, axis)

    packed = jnp.concatenate(
        [rate_bias[:, None], inflow_bias[:, None], conv_taps, conv_bias[:, None], lru_param[:, None]], axis=1
    )
    gains_own = jnp.stack([rec_gain, mlp_gain], axis=1)
    flat = jnp.concatenate([packed.reshape(-1), gains_own.reshape(-1)])
    flat = lax.all_gather(flat, "seq", axis=0)
    small_all = flat[:, : packed.size].reshape(count, layers, 8, own_width)
    small_all = jnp.transpose(small_all, (1, 2, 0, 3)).reshape(layers, 8, lru_width)
    gains = flat[:, packed.size :].reshape(count, layers, 2, d_rows)
    gains = jnp.transpose(gains, (1, 2, 0, 3)).reshape(layers, 2, model)
    small = window_of(small_all, 2).astype(f32)

    x0 = lax.dynamic_index_in_dim(inputs, section, 0, False)
    cot = lax.dynamic_index_in_dim(cotangent, section, 0, False)
    valid = lax.dynamic_index_in_dim(valid_mask, section, 0, False)
    masked = (cot.astype(f32) * valid[:, None].astype(f32)).astype(bf16)
    masked_all = lax.all_gather(masked, "seq", axis=0, tiled=True)
    marks = stream_marks(lax.dynamic_index_in_dim(doc_starts, section, 0, False), tokens)
    first_state = window_of(lax.dynamic_index_in_dim(prev_state, section, 0, False), 1).astype(f32)
    first_state = jnp.broadcast_to(first_state[:, None], (layers, 8, window))
    rim = window_of(lax.dynamic_index_in_dim(prev_inputs, section, 0, False), 2).astype(f32)
    rim = jnp.concatenate([jnp.zeros((layers, 5, window), f32), rim], axis=1)
    channel = jnp.arange(window, dtype=jnp.int32)
    own = jnp.logical_and(channel >= offset, channel < offset + own_width).astype(f32)
    own = jnp.broadcast_to(own[None], (8, window))

    def across(blocks):
        return lax.all_gather(swap(blocks, next(next_id)), "section", axis=1)

    def fetch_rec(l):
        in_q, side_q = quarter_of(in_weight[l], 0), quarter_of(side_weight[l], 0)
        rate_q, inflow_q = quarter_of(rate_blocks[l], 1), quarter_of(inflow_blocks[l], 1)
        pieces = []
        for q in range(count):
            b = first_block[q]
            lanes = slice(b * block_width, b * block_width + window)
            wide = jnp.concatenate([in_q[:, lanes], side_q[:, lanes]], axis=1)
            gates = jnp.stack([rate_q[b : b + 2], inflow_q[b : b + 2]]).reshape(-1, 2 * window)
            gates = jnp.pad(gates, ((0, pad_rows - gates.shape[0]), (0, 0)))
            pieces.append(jnp.concatenate([wide, gates], axis=0))
        got = across(jnp.stack(pieces))
        wide = got[:, :, :quarter].reshape(model, 2 * window)
        gate_rows = block_quarter * 4 * block_width // (2 * window)
        gates = got[:, :, quarter : quarter + gate_rows]
        gates = gates.reshape(count, sections, 2, 2, block_quarter, block_width)
        gates = jnp.transpose(gates, (2, 3, 0, 1, 4, 5)).reshape(2, 2, block_width, block_width)
        return wide, gates

    def fetch_mlp(l):
        both = jnp.stack([quarter_of(gate_weight[l], 0), quarter_of(up_weight[l], 0)], axis=1)
        both = both.reshape(quarter, 2, count, hidden_part)
        both = jnp.transpose(both, (2, 0, 1, 3)).reshape(count, quarter, 2 * hidden_part)
        return across(both).reshape(model, 2 * hidden_part)

    def fetch_out():
        part = lax.all_gather(quarter_of(out_weight, 2), "seq", axis=1, tiled=True)
        return lax.all_gather(window_of(part, 1), "section", axis=2, tiled=True)

    own_out = [
        lax.dynamic_update_slice(jnp.zeros((window, model), bf16), out_weight[l], (offset, 0)) for l in range(layers)
    ]

    x = x0
    kept = []
    normed = exchange("start", next(next_id), None, x0, None, gains[0, 0])[0]
    rec_weights, mlp_weights = [], []
    for l in range(layers):
        rec_weights.append(fetch_rec(l))
        mlp_weights.append(fetch_mlp(l))
    out_windows = fetch_out()
    for l in range(layers):
        wide_weight, gates = rec_weights[l]
        wide = dot(normed, wide_weight)
        gated, *saved = middle_forward(wide, marks, gates, small[l], rim[l], first_state[l])
        part = dot(gated, own_out[l]).astype(bf16)
        kept.append((x, normed, wide, gated, saved))
        normed, x = exchange("forward", next(next_id), part, x, None, gains[l, 1])
        both = dot(normed, mlp_weights[l])
        hidden = (jax.nn.gelu(both[:, :hidden_part]) * both[:, hidden_part:]).astype(bf16)
        part = dot(hidden, down_weight[l]).astype(bf16)
        kept.append((x, normed, both, hidden))
        if l + 1 < layers:
            normed, x = exchange("forward", next(next_id), part, x, None, gains[l + 1, 0])
        else:
            branch = lax.psum_scatter(part, "seq", scatter_dimension=0, tiled=True)
            outputs = (x.astype(f32) + branch.astype(f32)).astype(bf16)

    def sum_rows(grad):
        cols = grad.shape[1]
        grad = grad.astype(bf16).reshape(count, sections, quarter, cols)
        grad = jnp.transpose(grad, (1, 0, 2, 3)).reshape(sections * count * quarter, cols)
        grad = lax.psum_scatter(grad, "section", scatter_dimension=0, tiled=True)
        got = swap(grad.reshape(count, quarter, cols), next(next_id))
        return lax.all_gather(got, "section", axis=0)

    def spread_rows(got, lanes):
        part = got[..., lanes]
        return jnp.transpose(part, (0, 2, 1, 3)).reshape(d_rows, -1).astype(f32)

    d_rows_own, d_all = masked, masked_all
    dgains = [[None, None] for _ in range(layers)]
    grads = {}
    for l in reversed(range(layers)):
        x, normed, both, hidden = kept[2 * l + 1]
        d_hidden = dot_t(d_all, down_weight[l])
        gate, slope = gelu_pair(both[:, :hidden_part])
        d_gate = (d_hidden * both[:, hidden_part:] * slope).astype(bf16)
        d_up = (d_hidden * gate).astype(bf16)
        d_both = jnp.concatenate([d_gate, d_up], axis=1)
        part = dot_t(d_both, mlp_weights[l]).astype(bf16)
        grads["down", l] = lax.psum(dot_rows(hidden, d_all).astype(bf16), "section")
        grads["both", l] = sum_rows(dot_rows(normed, d_both))
        d_all, d_rows_own, dgains[l][1] = exchange("back", next(next_id), part, x, d_rows_own, gains[l, 1])

        x, normed, wide, gated, saved = kept[2 * l]
        wide_weight, gates = rec_weights[l]
        d_gated = dot_t(d_all, out_windows[l])
        dib, d_rate, d_inflow, sums = middle_backward(
            d_gated, wide, saved, marks, gates, small[l], rim[l], own
        )
        part = dot_t(dib, wide_weight).astype(bf16)
        grad_out = lax.dynamic_slice_in_dim(dot_rows(gated, d_all), offset, own_width, 0)
        grads["out", l] = lax.psum(grad_out.astype(bf16), "section")
        grad_wide = dot_rows(normed, dib)
        grads["wide", l] = sum_rows(
            jnp.concatenate(
                [
                    lax.dynamic_slice_in_dim(grad_wide, offset, own_width, 1),
                    lax.dynamic_slice_in_dim(grad_wide, offset + window, own_width, 1),
                ],
                axis=1,
            )
        )
        low = saved[0].astype(bf16).reshape(tokens, 2, block_width)
        d_gates = jnp.stack([d_rate, d_inflow]).reshape(2, tokens, 2, block_width)
        grads["gates", l] = jnp.einsum("tbi,gtbj->gbij", low, d_gates, preferred_element_type=f32)
        grads["sums", l] = lax.dynamic_slice_in_dim(sums, offset, own_width, 1)
        if l > 0:
            d_all, d_rows_own, dgains[l][0] = exchange("back", next(next_id), part, x, d_rows_own, gains[l, 0])
        else:
            input_grad, dgains[l][0] = exchange("last", next(next_id), part, x, d_rows_own, gains[l, 0])

    gate_grads = jnp.stack([grads["gates", l] for l in range(layers)]).astype(bf16)
    gate_grads = lax.psum(gate_grads, "section")
    gate_grads = gate_grads.reshape(layers * 4, count, block_rows, block_width)
    got = swap(
        jnp.transpose(gate_grads, (1, 0, 2, 3)).reshape(count, layers * 4 * block_rows, block_width), next(next_id)
    )
    got = got.reshape(count, layers, 2, 2, block_rows, block_width)
    gate_out = jnp.stack([got[owner[b], :, :, b - first_block[owner[b]]] for b in range(block_count)], axis=2)
    gate_out = gate_out.astype(f32)

    sums = lax.psum(jnp.stack([grads["sums", l] for l in range(layers)]), "section")
    dgain_all = jnp.stack([jnp.concatenate(dgains[l], axis=0) for l in range(layers)])
    dgain_all = lax.psum(dgain_all, ("section", "seq"))
    dgain_all = lax.dynamic_slice_in_dim(dgain_all, place * d_rows, d_rows, 2)

    def stacked(name, lanes):
        return jnp.stack([spread_rows(grads[name, l], lanes) for l in range(layers)])

    return (
        outputs[None],
        input_grad[None],
        dgain_all[:, 0],
        stacked("wide", slice(0, own_width)),
        stacked("wide", slice(own_width, None)),
        jnp.stack([grads["out", l] for l in range(layers)]).astype(f32),
        gate_out[:, 0],
        gate_out[:, 1],
        sums[:, 0],
        sums[:, 1],
        sums[:, 2:6],
        sums[:, 6],
        sums[:, 7],
        dgain_all[:, 1],
        stacked("both", slice(0, hidden_part)),
        stacked("both", slice(hidden_part, None)),
        jnp.stack([grads["down", l] for l in range(layers)]).astype(f32),
    )


def solution(mesh):
    return jax.shard_map(
        on_device,
        mesh=mesh,
        in_specs=(
            P(None, "seq", None),
            P(),
            P(None, "seq"),
            P(None, "seq", None),
            P(),
            P(),
            P(None, "seq"),
            P(None, "seq", None),
            P(None, "seq", None),
            P(None, "seq", None),
            P(None, None, "seq", None),
            P(None, None, "seq", None),
            P(None, "seq"),
            P(None, "seq"),
            P(None, None, "seq"),
            P(None, "seq"),
            P(None, "seq"),
            P(None, "seq"),
            P(None, "seq", None),
            P(None, "seq", None),
            P(None, "seq", None),
        ),
        out_specs=(
            P("section", "seq", None),
            P("section", "seq", None),
            P(None, "seq"),
            P(None, "seq", None),
            P(None, "seq", None),
            P(None, "seq", None),
            P(None, None, "seq", None),
            P(None, None, "seq", None),
            P(None, "seq"),
            P(None, "seq"),
            P(None, None, "seq"),
            P(None, "seq"),
            P(None, "seq"),
            P(None, "seq"),
            P(None, "seq", None),
            P(None, "seq", None),
            P(None, "seq", None),
        ),
        check_vma=False,
    )
```

```python
from functools import partial

import jax
import jax.numpy as jnp
import numpy as np
from jax import lax
from jax.experimental import pallas as pl
from jax.experimental.pallas import tpu as pltpu
from jax.sharding import PartitionSpec as P


epsilon = 1e-06
rate_scale = 8.0
MESH = pl.DeviceIdType.MESH
VMEM_LIMIT = 60 * 1024 * 1024
f32 = jnp.float32
bf16 = jnp.bfloat16


def plane_place():
    section = lax.axis_index("section")
    column, row = section % 2, section // 2
    return section, row * 2 + 1 - column, (1 - row) * 2 + column


def dma(*shape):
    return pltpu.SemaphoreType.DMA(shape)


def along(source, target, send, receive, peer):
    return pltpu.make_async_remote_copy(
        src_ref=source,
        dst_ref=target,
        send_sem=send,
        recv_sem=receive,
        device_id={"seq": peer},
        device_id_type=MESH,
    )


class Item:
    def __init__(self, first, at, sems, slot, even):
        self.first, self.at, self.sems, self.slot, self.even = first, at, sems, slot, even
        self.section, self.side, self.up = plane_place()

    def copy(self, way, source, holder, target):
        return pltpu.make_async_remote_copy(
            src_ref=source,
            dst_ref=self.at(holder),
            send_sem=self.sems.at[way, 0, self.slot],
            recv_sem=self.sems.at[way, 1, self.slot],
            device_id={"section": target},
            device_id_type=MESH,
        )

    def start(self):
        self.to_side = self.copy(0, self.first, self.section, self.side)
        self.to_up = self.copy(1, self.first, self.section, self.up)
        self.to_side.start()
        self.to_up.start()

    def forward(self):
        self.to_side.wait_recv()
        if self.even:
            self.onward = self.copy(2, self.at(self.side), self.side, self.up)
            self.onward.start()
        self.to_up.wait_recv()
        if not self.even:
            self.onward = self.copy(2, self.at(self.up), self.up, self.side)
            self.onward.start()

    def finish(self):
        self.onward.wait()
        self.to_side.wait_send()
        self.to_up.wait_send()


class Spread:
    on_line, in_plane = True, True

    def __init__(self, arrays, shape, pieces, cut, fill, slot):
        self.arrays, self.pieces, self.cut, self.fill, self.slot = list(arrays), pieces, cut, fill, slot
        self.shape = jax.ShapeDtypeStruct(shape, self.arrays[0].dtype)

    def scratch(self, count):
        return [dma(2, self.pieces, count), dma(3, 2, count)]

    def begin(self, refs, out, sems, place, count):
        line, plane = sems
        self.own, self.sends, self.items = [], [], []
        section = plane_place()[0]
        for i, (piece, there) in enumerate(zip(self.cut(refs, place), self.fill(self.slot(out, place, section)))):
            copy = pltpu.make_async_copy(piece, there, line.at[0, i, 0])
            copy.start()
            self.own.append(copy)
        for k in range(count):
            source = (place + count - k) % count
            self.items.append(
                Item(
                    self.slot(out, source, section),
                    lambda s, source=source: self.slot(out, source, s),
                    plane,
                    k,
                    k % 2 == 0,
                )
            )

        def push():
            for k in range(1, count):
                peer = (place + k) % count
                pieces = zip(self.cut(refs, peer), self.fill(self.slot(out, place, section)))
                group = [
                    along(piece, there, line.at[0, i, k], line.at[1, i, k], peer)
                    for i, (piece, there) in enumerate(pieces)
                ]
                for copy in group:
                    copy.start()
                self.sends.append(group)

        self.push = push

    def own_block(self):
        for copy in self.own:
            copy.wait()
        self.items[0].start()

    def arrive(self, k):
        for copy in self.sends[k - 1]:
            copy.wait_recv()
        self.items[k].start()
        self.items[k - 1].forward()

    def finish(self):
        self.items[-1].forward()
        for item in self.items:
            item.finish()
        for group in self.sends:
            for copy in group:
                copy.wait_send()


class Share:
    on_line, in_plane = False, True

    def __init__(self, array, start, size):
        self.arrays, self.start, self.size = [array], start, size
        self.shape = jax.ShapeDtypeStruct((4, size, array.shape[1]), array.dtype)

    def scratch(self, count):
        return [dma(3, 2, 2), dma(1)]

    def begin(self, refs, out, sems, place, count):
        plane, own = sems
        section = plane_place()[0]
        mine = refs[0].at[pl.ds(self.start, self.size)]
        self.own = pltpu.make_async_copy(mine, out.at[section], own.at[0])
        self.own.start()
        half = self.size // 2
        self.items = []
        for h in range(2):
            rows = pl.ds(h * half, half)
            first = refs[0].at[pl.ds(self.start + h * half, half)]
            item = Item(first, lambda s, rows=rows: out.at[s, rows], plane, h, h == 0)
            item.start()
            self.items.append(item)

    def push(self):
        pass

    def own_block(self):
        self.own.wait()

    def arrive(self, k):
        if k in (4, 6):
            self.items[k // 2 - 2].forward()

    def finish(self):
        for item in self.items:
            item.finish()


class Everyone:
    on_line, in_plane = True, False

    def __init__(self, array, count):
        self.arrays = [array]
        self.shape = jax.ShapeDtypeStruct((count,) + array.shape, array.dtype)

    def scratch(self, count):
        return [dma(2, count)]

    def begin(self, refs, out, sems, place, count):
        self.own = pltpu.make_async_copy(refs[0], out.at[place], sems[0].at[0, 0])
        self.own.start()
        self.sends = []
        for k in range(1, count):
            copy = along(refs[0], out.at[place], sems[0].at[0, k], sems[0].at[1, k], (place + k) % count)
            copy.start()
            self.sends.append(copy)

    def push(self):
        pass

    def own_block(self):
        self.own.wait()

    def arrive(self, k):
        self.sends[k - 1].wait_recv()

    def finish(self):
        for copy in self.sends:
            copy.wait_send()


class Beside:
    on_line, in_plane = True, False

    def __init__(self, array, layer, reach):
        self.arrays, self.layer, self.reach = [array], layer, reach
        self.rows = array.shape[1]
        self.shape = jax.ShapeDtypeStruct((self.rows + 2 * reach, array.shape[2]), array.dtype)
        self.sizes = [min(self.rows, reach - at) for at in range(0, reach, self.rows)]

    def scratch(self, count):
        return [dma(2, 2, len(self.sizes) + 1)]

    def begin(self, refs, out, sems, place, count):
        mine, sem = refs[0].at[self.layer], sems[0]
        self.own = pltpu.make_async_copy(mine, out.at[pl.ds(self.reach, self.rows)], sem.at[0, 0, 0])
        self.own.start()
        self.ends = []
        done = 0
        for k, size in enumerate(self.sizes, 1):
            ahead = along(
                mine.at[pl.ds(self.rows - size, size)],
                out.at[pl.ds(self.reach - done - size, size)],
                sem.at[0, 0, k],
                sem.at[0, 1, k],
                place + k,
            )
            back = along(
                mine.at[pl.ds(0, size)],
                out.at[pl.ds(self.reach + self.rows + done, size)],
                sem.at[1, 0, k],
                sem.at[1, 1, k],
                place - k,
            )
            pl.when(place + k < count)(ahead.start)
            pl.when(place >= k)(back.start)
            self.ends.append((k, ahead, back))
            done += size
        self.place, self.count = place, count

    def push(self):
        pass

    def own_block(self):
        self.own.wait()

    def arrive(self, k):
        pass

    def finish(self):
        for k, ahead, back in self.ends:
            pl.when(self.place >= k)(ahead.wait_recv)
            pl.when(self.place + k < self.count)(back.wait_recv)
            pl.when(self.place + k < self.count)(ahead.wait_send)
            pl.when(self.place >= k)(back.wait_send)


def comm_body(mode, count, jobs, refs):
    chips = count // 2
    has_sum = mode in ("forward", "back", "last", "rows")
    has_gather = mode in ("start", "forward", "back")
    backward = mode in ("back", "last")
    refs = list(refs)
    take = refs.pop
    part_ref = take(0) if has_sum else None
    x_ref = take(0) if mode != "none" else None
    dy_ref = take(0) if backward else None
    gain_ref = take(0) if mode in ("forward", "back", "last") else None
    job_refs = [[take(0) for _ in job.arrays] for job in jobs]
    out_ref = take(0) if has_gather else None
    rows_ref = take(0) if has_sum else None
    dgain_ref = take(0) if backward else None
    job_outs = [take(0) for _ in jobs]
    if has_sum:
        pair_ref, staged_ref, landed_ref, pair_sem, sum_sem = (take(0) for _ in range(5))
    if has_gather:
        hop_sem, mate_sem = (take(0) for _ in range(2))
    job_sems = [[take(0) for _ in job.scratch(count)] for job in jobs]

    place = lax.axis_index("seq")
    chip, core = place // 2, place % 2
    mate = chip * 2 + 1 - core
    section, side, up = plane_place()

    barrier = pltpu.get_barrier_semaphore()
    met = 0
    line = []
    if any(job.on_line for job in jobs):
        line = [(place + k) % count for k in range(1, count)]
    elif mode != "none":
        line = [mate] + [((chip + k) % chips) * 2 + core for k in range(1, chips)]
    for peer in line:
        pl.semaphore_signal(barrier, inc=1, device_id={"seq": peer}, device_id_type=MESH)
        met += 1
    if any(job.in_plane for job in jobs):
        for peer in (side, up):
            pl.semaphore_signal(barrier, inc=1, device_id={"section": peer}, device_id_type=MESH)
            met += 1
    pl.semaphore_wait(barrier, met)

    def origin(way, k):
        return chip - k if way == 0 else chip + k

    def comes(way, k):
        return chip >= k if way == 0 else chip + k < chips

    def goes_on(way):
        return chip + 1 < chips if way == 0 else chip >= 1

    def hop(way, k):
        slot = origin(way, k) * 2 + core
        onward = chip + 1 if way == 0 else chip - 1
        return along(
            out_ref.at[slot], out_ref.at[slot], hop_sem.at[way, 0, k], hop_sem.at[way, 1, k + 1], onward * 2 + core
        )

    def landing(way, k):
        slot = origin(way, k) * 2 + core
        return along(out_ref.at[slot], out_ref.at[slot], hop_sem.at[way, 0, k], hop_sem.at[way, 1, k], mate)

    def across(way, k):
        slot = origin(way, k) * 2 + core
        return along(out_ref.at[slot], out_ref.at[slot], mate_sem.at[way, 0, k], mate_sem.at[way, 1, k], mate)

    def begin_gather(rows):
        out_ref[place] = rows
        for way in range(2):
            pl.when(goes_on(way))(hop(way, 0).start)
        across(0, 0).start()

    def land(k):
        for way in range(2):

            @pl.when(comes(way, k))
            def _(way=way, k=k):
                landing(way, k).wait_recv()
                pl.when(goes_on(way))(hop(way, k).start)
                across(way, k).start()

    if mode == "start":
        begin_gather(x_ref[...])
    if has_sum:
        pair_copies = []
        for k in list(range(1, chips)) + [0]:
            to_chip = (chip + k) % chips
            copy = along(
                part_ref.at[to_chip * 2 + 1 - core], pair_ref.at[k], pair_sem.at[0, k], pair_sem.at[1, k], mate
            )
            copy.start()
            pair_copies.append((k, copy))
    for job, ref, out, sems in zip(jobs, job_refs, job_outs, job_sems):
        job.begin(ref, out, sems, place, count)
    if has_sum:
        sum_copies = []
        total = None
        for k, copy in pair_copies:
            to_chip = (chip + k) % chips
            copy.wait_recv()
            both = part_ref[to_chip * 2 + core].astype(f32) + pair_ref[k].astype(f32)
            if k == 0:
                total = both
            else:
                staged_ref[k] = both.astype(bf16)
                send = along(
                    staged_ref.at[k], landed_ref.at[k], sum_sem.at[0, k], sum_sem.at[1, k], to_chip * 2 + core
                )
                send.start()
                sum_copies.append((k, send))
    for job in jobs:
        job.push()
    for job in jobs:
        job.own_block()
    for k in range(1, count):
        for job in jobs:
            job.arrive(k)
        if mode == "start" and k % 2 == 0:
            land(k // 2)
    if has_sum:
        for k, send in sum_copies:
            send.wait_recv()
            total = total + landed_ref[k].astype(f32)

    if mode != "none":
        x_wide = x_ref[...].astype(f32)
    if mode == "rows":
        rows_ref[...] = (x_wide + total).astype(bf16)
    elif mode == "forward":
        x_low = (x_wide + total).astype(bf16)
        rows_ref[...] = x_low
        x_wide = x_low.astype(f32)
        scale = lax.rsqrt(jnp.mean(x_wide * x_wide, axis=-1, keepdims=True) + epsilon)
        sent = (x_wide * scale * gain_ref[...]).astype(bf16)
    elif backward:
        scale = lax.rsqrt(jnp.mean(x_wide * x_wide, axis=-1, keepdims=True) + epsilon)
        scaled = total * gain_ref[...]
        inner_mean = jnp.mean(scaled * x_wide, axis=-1, keepdims=True)
        back = scale * scaled - x_wide * (scale * scale * scale * inner_mean)
        dgain_ref[...] = jnp.sum(total * x_wide * scale, axis=0, keepdims=True)
        sent = (dy_ref[...].astype(f32) + back).astype(bf16)
        rows_ref[...] = sent

    if has_gather and mode != "start":
        begin_gather(sent)
        for k in range(1, chips):
            land(k)

    for job in jobs:
        job.finish()
    if has_gather:
        across(0, 0).wait()
        for way in range(2):
            pl.when(goes_on(way))(hop(way, 0).wait_send)
        for k in range(1, chips):
            for way in range(2):

                @pl.when(comes(way, k))
                def _(way=way, k=k):
                    across(way, k).wait()
                    pl.when(goes_on(way))(hop(way, k).wait_send)

    if has_sum:
        for _, copy in pair_copies:
            copy.wait_send()
        for _, send in sum_copies:
            send.wait_send()


def comm(mode, collective_id, part=None, x=None, dy=None, gain=None, jobs=(), us=50):
    count = lax.axis_size("seq")
    chips = count // 2
    has_sum = mode in ("forward", "back", "last", "rows")
    has_gather = mode in ("start", "forward", "back")
    backward = mode in ("back", "last")
    in_vmem = pl.BlockSpec(memory_space=pltpu.VMEM)
    in_hbm = pl.BlockSpec(memory_space=pl.ANY)
    operands, in_specs, shapes, out_specs, scratch = [], [], [], [], []

    def give(a, spec):
        operands.append(a)
        in_specs.append(spec)

    def want(shape, spec):
        shapes.append(shape)
        out_specs.append(spec)

    if mode != "none":
        rows, width = x.shape
    if has_sum:
        give(part.reshape(count, rows, width), in_vmem)
    if mode != "none":
        give(x, in_vmem)
    if backward:
        give(dy, in_vmem)
    if mode in ("forward", "back", "last"):
        give(gain.astype(f32).reshape(1, width), in_vmem)
    for job in jobs:
        for a in job.arrays:
            give(a, in_hbm)
    if has_gather:
        want(jax.ShapeDtypeStruct((count, rows, width), bf16), in_vmem)
    if has_sum:
        want(jax.ShapeDtypeStruct((rows, width), bf16), in_vmem)
    if backward:
        want(jax.ShapeDtypeStruct((1, width), f32), in_vmem)
    for job in jobs:
        want(job.shape, in_hbm)
    if has_sum:
        scratch += [pltpu.VMEM((chips, rows, width), bf16)] * 3 + [dma(2, chips)] * 2
    if has_gather:
        scratch += [dma(2, 2, chips + 1), dma(2, 2, chips)]
    for job in jobs:
        scratch += job.scratch(count)
    outs = pl.pallas_call(
        lambda *refs: comm_body(mode, count, jobs, refs),
        out_shape=shapes,
        in_specs=in_specs,
        out_specs=out_specs,
        scratch_shapes=scratch,
        cost_estimate=pl.CostEstimate(flops=us * 1_000_000_000, bytes_accessed=1_000_000, transcendentals=0),
        compiler_params=pltpu.CompilerParams(
            collective_id=collective_id, has_side_effects=True, vmem_limit_bytes=VMEM_LIMIT
        ),
    )(*operands)
    outs = list(outs)
    if has_gather:
        outs[0] = outs[0].reshape(count * rows, width)
    return outs


def less_exp(doubled):
    small = doubled * (
        1.0
        - doubled
        * (
            0.5
            - doubled
            * (1.0 / 6 - doubled * (1.0 / 24 - doubled * (1.0 / 120 - doubled * (1.0 / 720))))
        )
    )
    return jnp.where(doubled < 0.25, small, 1.0 - jnp.exp(-doubled))


def gelu_pair(v):
    c = np.float32(np.sqrt(2 / np.pi))
    t = jnp.tanh(c * (v + 0.044715 * v * v * v))
    slope = 0.5 * (1.0 + t) + 0.5 * v * (1.0 - t * t) * c * (1.0 + 3 * 0.044715 * v * v)
    return 0.5 * v * (1.0 + t), slope


def dot(a, b):
    return jnp.dot(a, b, preferred_element_type=f32)


def dot_t(a, b):
    return lax.dot_general(a, b, (((1,), (1,)), ((), ())), preferred_element_type=f32)


def dot_rows(a, b):
    return lax.dot_general(a, b, (((0,), (0,)), ((), ())), preferred_element_type=f32)


def soft(lru):
    spread = jnp.maximum(-lru, 0.0) + jnp.log1p(jnp.exp(-jnp.abs(lru)))
    return spread, -1.0 / (1.0 + jnp.exp(lru))


def middle_forward_body(
    rows,
    width,
    is_ref,
    marks_ref,
    blocks_ref,
    small_ref,
    rim_ref,
    first_ref,
    gated_ref,
    mixed_ref,
    rate_ref,
    inflow_ref,
    states_ref,
    before_ref,
    ext,
    decays,
    drives,
    carry,
):
    @pl.when(pl.program_id(0) == 0)
    def _():
        ext[0:8] = rim_ref[...]
        carry[...] = first_ref[...]

    block = width // 2
    inner = is_ref[:, :width].astype(bf16).astype(f32)
    ext[8 : 8 + rows] = inner
    reset = marks_ref[:, 0:1]
    mixed = (
        small_ref[6:7]
        + small_ref[2:3] * inner
        + small_ref[3:4] * (ext[7 : 7 + rows] * marks_ref[:, 1:2])
        + small_ref[4:5] * (ext[6 : 6 + rows] * marks_ref[:, 2:3])
        + small_ref[5:6] * (ext[5 : 5 + rows] * marks_ref[:, 3:4])
    )
    ext[0:8] = ext[rows : rows + 8]
    mixed_ref[...] = mixed
    low = mixed.astype(bf16)
    for b in range(2):
        lanes = slice(b * block, (b + 1) * block)
        rate_ref[:, lanes] = dot(low[:, lanes], blocks_ref[0, b]) + small_ref[0:1, lanes]
        inflow_ref[:, lanes] = dot(low[:, lanes], blocks_ref[1, b]) + small_ref[1:2, lanes]
    spread, _ = soft(small_ref[7:8])
    log_decay = (-rate_scale * spread) * jax.nn.sigmoid(rate_ref[...])
    kept = 1.0 - reset
    decays[...] = jnp.exp(log_decay) * kept
    factor = reset + kept * jnp.sqrt(less_exp(-2.0 * log_decay))
    drives[...] = factor * jax.nn.sigmoid(inflow_ref[...]) * mixed

    place = lax.broadcasted_iota(jnp.int32, (8, width), 0)

    def step(j, last):
        at = pl.ds(pl.multiple_of(j * 8, 8), 8)
        a, h = decays[at], drives[at]
        for k in (1, 2, 4):
            inside = place >= k
            h = jnp.where(inside, a * pltpu.roll(h, k, 0) + h, h)
            a = jnp.where(inside, a * pltpu.roll(a, k, 0), a)
        h = h + a * last
        states_ref[at] = h
        before_ref[at] = jnp.where(place >= 1, pltpu.roll(h, 1, 0), last)
        return jnp.broadcast_to(h[7:8], (8, width))

    carry[...] = lax.fori_loop(0, rows // 8, step, carry[...])
    gated_ref[...] = (states_ref[...] * gelu_pair(is_ref[:, width:])[0]).astype(bf16)


def middle_backward_body(
    rows,
    width,
    dg_ref,
    is_ref,
    mixed_ref,
    rate_ref,
    inflow_ref,
    states_ref,
    before_ref,
    marks_ref,
    blocks_ref,
    small_ref,
    rim_ref,
    own_ref,
    dib_ref,
    drate_ref,
    dinflow_ref,
    sums_ref,
    dm_ext,
    decays,
    dstates,
    carry,
):
    @pl.when(pl.program_id(0) == 0)
    def _():
        dm_ext[rows : rows + 8] = jnp.zeros((8, width), f32)
        carry[...] = jnp.zeros((8, width), f32)
        sums_ref[...] = jnp.zeros_like(sums_ref)

    block = width // 2
    own = own_ref[0:1]
    reset = marks_ref[:, 0:1]
    kept = 1.0 - reset
    side, slope = gelu_pair(is_ref[:, width:])
    d_gated = dg_ref[...]
    dib_ref[:, width:] = (d_gated * states_ref[...] * slope * own).astype(bf16)
    dstates[...] = d_gated * side
    spread, spread_slope = soft(small_ref[7:8])
    rate = jax.nn.sigmoid(rate_ref[...])
    log_decay = (-rate_scale * spread) * rate
    decays[...] = jnp.exp(log_decay) * kept

    place = lax.broadcasted_iota(jnp.int32, (8, width), 0)

    def step(j, after):
        at = pl.ds(pl.multiple_of(rows - 8 - j * 8, 8), 8)
        own_decay, h = decays[at], dstates[at]
        a = jnp.where(place < 7, pltpu.roll(own_decay, 7, 0), 1.0)
        for k in (1, 2, 4):
            inside = place < 8 - k
            h = jnp.where(inside, a * pltpu.roll(h, 8 - k, 0) + h, h)
            a = jnp.where(inside, a * pltpu.roll(a, 8 - k, 0), a)
        h = h + a * after
        dstates[at] = h
        return jnp.broadcast_to((own_decay * h)[0:1], (8, width))

    carry[...] = lax.fori_loop(0, rows // 8, step, carry[...])

    d_h = dstates[...]
    mixed = mixed_ref[...]
    inflow = jax.nn.sigmoid(inflow_ref[...])
    root = jnp.sqrt(less_exp(-2.0 * log_decay))
    factor = reset + kept * root
    decay = decays[...]
    twice = jnp.exp(2.0 * log_decay)
    d_log = d_h * before_ref[...] * decay - d_h * inflow * mixed * kept * (twice / root)
    d_lru = jnp.sum(d_log * rate, axis=0, keepdims=True) * (-rate_scale * spread_slope)
    d_rate = (d_log * (-rate_scale * spread) * rate * (1.0 - rate)).astype(bf16)
    through = d_h * factor
    d_inflow = (through * mixed * inflow * (1.0 - inflow)).astype(bf16)
    drate_ref[...] = d_rate
    dinflow_ref[...] = d_inflow
    for b in range(2):
        lanes = slice(b * block, (b + 1) * block)
        dm_ext[0:rows, lanes] = (
            ((through * inflow)[:, lanes] + dot_t(d_rate[:, lanes], blocks_ref[0, b]) + dot_t(d_inflow[:, lanes], blocks_ref[1, b]))
            .astype(bf16)
            .astype(f32)
        )
    d_mixed = dm_ext[0:rows]
    inner = is_ref[:, :width].astype(bf16).astype(f32)
    shifted = [d_mixed] + [dm_ext[k : k + rows] * marks_ref[:, 3 + k : 4 + k] for k in (1, 2, 3)]
    d_inner = small_ref[2:3] * shifted[0]
    for k in (1, 2, 3):
        d_inner = d_inner + small_ref[2 + k : 3 + k] * shifted[k]
    dib_ref[:, :width] = (d_inner * own).astype(bf16)

    def add(row, value):
        sums_ref[row : row + 1] += value

    add(0, jnp.sum(d_rate.astype(f32), axis=0, keepdims=True))
    add(1, jnp.sum(d_inflow.astype(f32), axis=0, keepdims=True))
    for k in range(4):
        add(2 + k, jnp.sum(shifted[k] * inner, axis=0, keepdims=True))
    add(6, jnp.sum(d_mixed, axis=0, keepdims=True))
    add(7, d_lru)

    @pl.when(pl.program_id(0) == pl.num_programs(0) - 1)
    def _():
        for k in (1, 2, 3):
            for t in range(k):
                add(2 + k, dm_ext[t : t + 1] * marks_ref[t : t + 1, k : k + 1] * rim_ref[8 + t - k : 9 + t - k])

    dm_ext[rows : rows + 8] = dm_ext[0:8]


def row_spec(rows, width, steps, reverse):
    if reverse:
        return pl.BlockSpec((rows, width), lambda i: (steps - 1 - i, 0))
    return pl.BlockSpec((rows, width), lambda i: (i, 0))


def whole_spec(shape):
    return pl.BlockSpec(shape, lambda i: (0,) * len(shape))


def middle_forward(wide, marks, blocks, small, rim, first):
    tokens, width = wide.shape[0], wide.shape[1] // 2
    rows = min(256, tokens)
    steps = tokens // rows
    here = partial(row_spec, rows, steps=steps, reverse=False)
    whole = [blocks, small, rim, first]
    kinds = [bf16, f32, f32, f32, f32, f32]
    return pl.pallas_call(
        partial(middle_forward_body, rows, width),
        grid=(steps,),
        out_shape=[jax.ShapeDtypeStruct((tokens, width), kind) for kind in kinds],
        in_specs=[here(2 * width), here(8)] + [whole_spec(a.shape) for a in whole],
        out_specs=[here(width)] * 6,
        scratch_shapes=[
            pltpu.VMEM((rows + 8, width), f32),
            pltpu.VMEM((rows, width), f32),
            pltpu.VMEM((rows, width), f32),
            pltpu.VMEM((8, width), f32),
        ],
        compiler_params=pltpu.CompilerParams(vmem_limit_bytes=VMEM_LIMIT),
    )(wide, marks, *whole)


def middle_backward(d_gated, wide, saved, marks, blocks, small, rim, own):
    tokens, width = d_gated.shape
    rows = min(256, tokens)
    steps = tokens // rows
    here = partial(row_spec, rows, steps=steps, reverse=True)
    whole = [blocks, small, rim, own]
    return pl.pallas_call(
        partial(middle_backward_body, rows, width),
        grid=(steps,),
        out_shape=[
            jax.ShapeDtypeStruct((tokens, 2 * width), bf16),
            jax.ShapeDtypeStruct((tokens, width), bf16),
            jax.ShapeDtypeStruct((tokens, width), bf16),
            jax.ShapeDtypeStruct((8, width), f32),
        ],
        in_specs=[here(width), here(2 * width)] + [here(width)] * 5 + [here(8)] + [whole_spec(a.shape) for a in whole],
        out_specs=[here(2 * width), here(width), here(width), whole_spec((8, width))],
        scratch_shapes=[
            pltpu.VMEM((rows + 8, width), f32),
            pltpu.VMEM((rows, width), f32),
            pltpu.VMEM((rows, width), f32),
            pltpu.VMEM((8, width), f32),
        ],
        compiler_params=pltpu.CompilerParams(vmem_limit_bytes=VMEM_LIMIT),
    )(d_gated, wide, *saved, marks, *whole)


def grads_mlp(normed, d_both, hidden, d_all, sections, count, lanes):
    tokens, model = normed.shape
    d_rows = model // count
    quarter = d_rows // sections
    chunks = d_both.shape[1] // lanes
    rows = chunks * quarter
    down_rows = hidden.shape[1] // sections
    per_block = rows // down_rows
    down_blocks = model // lanes // per_block

    def body(normed_ref, both_ref, hidden_ref, all_ref, out_ref):
        j = pl.program_id(0)

        @pl.when(j < count)
        def _():
            grad = dot_rows(normed_ref[...], both_ref[...])
            for s in range(sections):
                for ch in range(chunks):
                    out_ref[s, 0, ch * quarter : (ch + 1) * quarter] = grad[
                        s * quarter : (s + 1) * quarter, ch * lanes : (ch + 1) * lanes
                    ].astype(bf16)

        @pl.when(j >= count)
        def _():
            grad = dot_rows(hidden_ref[...], all_ref[...])
            for s in range(sections):
                for ch in range(per_block):
                    out_ref[s, 0, ch * down_rows : (ch + 1) * down_rows] = grad[
                        s * down_rows : (s + 1) * down_rows, ch * lanes : (ch + 1) * lanes
                    ].astype(bf16)

    return pl.pallas_call(
        body,
        grid=(count + down_blocks,),
        out_shape=jax.ShapeDtypeStruct((sections, count + down_blocks, rows, lanes), bf16),
        in_specs=[
            pl.BlockSpec((tokens, d_rows), lambda j: (0, jnp.minimum(j, count - 1))),
            pl.BlockSpec(d_both.shape, lambda j: (0, 0)),
            pl.BlockSpec(hidden.shape, lambda j: (0, 0)),
            pl.BlockSpec((tokens, per_block * lanes), lambda j: (0, jnp.maximum(j - count, 0))),
        ],
        out_specs=pl.BlockSpec((sections, 1, rows, lanes), lambda j: (0, j, 0, 0)),
        compiler_params=pltpu.CompilerParams(vmem_limit_bytes=VMEM_LIMIT),
    )(normed, d_both, hidden, d_all)


def grads_rec(normed, dib, gated, d_all, mixed, d_rate, d_inflow, offset, own_width, sections, count, lanes):
    tokens, model = normed.shape
    window = gated.shape[1]
    block = window // 2
    d_rows = model // count
    quarter = d_rows // sections
    chunks = 2 * own_width // lanes
    gate_rows = block // count // sections
    gate_chunks = block // lanes
    rows = chunks * quarter + 4 * gate_chunks * gate_rows
    out_rows = own_width // sections
    padded = out_rows + 16
    per_block = rows // padded
    out_blocks = model // lanes // per_block

    def body(offset_ref, normed_ref, dib_ref, gated_ref, all_ref, mixed_ref, rate_ref, inflow_ref, out_ref, own, gates, out_grad):
        j = pl.program_id(0)
        first = offset_ref[0]

        @pl.when(j == 0)
        def _():
            row = lax.broadcasted_iota(jnp.int32, (window, own_width), 0)
            column = lax.broadcasted_iota(jnp.int32, (window, own_width), 1)
            pick = (row == column + first).astype(f32).astype(bf16)
            own[...] = jnp.concatenate(
                [dot(dib_ref[:, :window], pick), dot(dib_ref[:, window:], pick)], axis=1
            ).astype(bf16)
            low = mixed_ref[...].astype(bf16)
            for i, ref in enumerate((rate_ref, inflow_ref)):
                for b in range(2):
                    at = slice(b * block, (b + 1) * block)
                    gates[2 * i + b] = dot_rows(low[:, at], ref[:, at])

        @pl.when(j < count)
        def _():
            grad = dot_rows(normed_ref[...], own[...])
            for s in range(sections):
                for ch in range(chunks):
                    out_ref[s, 0, ch * quarter : (ch + 1) * quarter] = grad[
                        s * quarter : (s + 1) * quarter, ch * lanes : (ch + 1) * lanes
                    ].astype(bf16)
                here = pl.ds(pl.multiple_of((j * sections + s) * gate_rows, gate_rows), gate_rows)
                pieces = [
                    gates[g, here, ch * lanes : (ch + 1) * lanes] for g in range(4) for ch in range(gate_chunks)
                ]
                out_ref[s, 0, chunks * quarter :] = jnp.concatenate(pieces, axis=0).astype(bf16)

        @pl.when(j >= count)
        def _():
            out_grad[...] = dot_rows(gated_ref[...], all_ref[...])
            for s in range(sections):
                here = pl.ds(pl.multiple_of(first + s * out_rows, 8), out_rows)
                for ch in range(per_block):
                    out_ref[s, 0, ch * padded : ch * padded + out_rows] = out_grad[
                        here, ch * lanes : (ch + 1) * lanes
                    ].astype(bf16)
                    out_ref[s, 0, ch * padded + out_rows : (ch + 1) * padded] = jnp.zeros((16, lanes), bf16)

    whole = lambda a: pl.BlockSpec(a.shape, lambda j, o, n=a.ndim: (0,) * n)
    return pl.pallas_call(
        body,
        grid_spec=pltpu.PrefetchScalarGridSpec(
            num_scalar_prefetch=1,
            grid=(count + out_blocks,),
            in_specs=[
                pl.BlockSpec((tokens, d_rows), lambda j, o: (0, jnp.minimum(j, count - 1))),
                whole(dib),
                whole(gated),
                pl.BlockSpec((tokens, per_block * lanes), lambda j, o: (0, jnp.maximum(j - count, 0))),
                whole(mixed),
                whole(d_rate),
                whole(d_inflow),
            ],
            out_specs=pl.BlockSpec((sections, 1, rows, lanes), lambda j, o: (0, j, 0, 0)),
            scratch_shapes=[
                pltpu.VMEM((tokens, 2 * own_width), bf16),
                pltpu.VMEM((4, block, block), f32),
                pltpu.VMEM((window, per_block * lanes), f32),
            ],
        ),
        out_shape=jax.ShapeDtypeStruct((sections, count + out_blocks, rows, lanes), bf16),
        compiler_params=pltpu.CompilerParams(vmem_limit_bytes=VMEM_LIMIT),
    )(offset.reshape(1), normed, dib, gated, d_all, mixed, d_rate, d_inflow)


def place_mlp(swapped, shared, quarter, hidden_part):
    layers = len(swapped)
    count, sections, rows, lanes = swapped[0].shape
    chunks = rows // quarter
    half = chunks // 2
    model = shared[0].shape[1] // (hidden_part // sections) * lanes
    down_rows = hidden_part // sections

    def columns_body(*refs):
        gate_ref, up_ref = refs[layers:]
        for l in range(layers):
            for s in range(sections):
                for ch in range(chunks):
                    target = gate_ref if ch < half else up_ref
                    at = ch % half
                    target[l, s * quarter : (s + 1) * quarter, at * lanes : (at + 1) * lanes] = refs[l][
                        0, s, ch * quarter : (ch + 1) * quarter
                    ].astype(f32)

    wide = jax.ShapeDtypeStruct((layers, sections * quarter, count * hidden_part), f32)
    gate, up = pl.pallas_call(
        columns_body,
        grid=(count,),
        out_shape=[wide, wide],
        in_specs=[pl.BlockSpec((1, sections, rows, lanes), lambda q: (q, 0, 0, 0))] * layers,
        out_specs=[pl.BlockSpec((layers, sections * quarter, hidden_part), lambda q: (0, 0, q))] * 2,
        compiler_params=pltpu.CompilerParams(vmem_limit_bytes=VMEM_LIMIT),
    )(*swapped)

    def rows_body(*refs):
        for l in range(layers):
            for ch in range(model // lanes):
                refs[layers][l, :, ch * lanes : (ch + 1) * lanes] = refs[l][
                    0, ch * down_rows : (ch + 1) * down_rows
                ].astype(f32)

    down = pl.pallas_call(
        rows_body,
        grid=(sections,),
        out_shape=jax.ShapeDtypeStruct((layers, hidden_part, model), f32),
        in_specs=[pl.BlockSpec((1,) + shared[0].shape[1:], lambda s: (s, 0, 0))] * layers,
        out_specs=pl.BlockSpec((layers, down_rows, model), lambda s: (0, s, 0)),
        compiler_params=pltpu.CompilerParams(vmem_limit_bytes=VMEM_LIMIT),
    )(*shared)
    return gate, up, down


def place_rec(swapped, shared, quarter, own_width):
    layers = len(swapped)
    count, sections, _, lanes = swapped[0].shape
    chunks = 2 * own_width // lanes
    out_rows = own_width // sections
    padded = out_rows + 16
    model = shared[0].shape[1] // padded * lanes

    def body(*refs):
        in_ref, side_ref, out_ref = refs[2 * layers :]
        for l in range(layers):

            @pl.when(pl.program_id(0) == l)
            def _(l=l):
                for q in range(count):
                    for s in range(sections):
                        rows = slice(s * quarter, (s + 1) * quarter)
                        for ch in range(chunks):
                            value = refs[l][q, s, ch * quarter : (ch + 1) * quarter].astype(f32)
                            first, last = ch * lanes, (ch + 1) * lanes
                            base = q * own_width
                            if first < own_width:
                                end = min(last, own_width)
                                in_ref[0, rows, base + first : base + end] = value[:, : end - first]
                            if last > own_width:
                                begin = max(first, own_width)
                                side_ref[0, rows, base + begin - own_width : base + last - own_width] = value[
                                    :, begin - first :
                                ]
                for s in range(sections):
                    for ch in range(model // lanes):
                        out_ref[0, s * out_rows : (s + 1) * out_rows, ch * lanes : (ch + 1) * lanes] = refs[
                            layers + l
                        ][s, ch * padded : ch * padded + out_rows].astype(f32)

    wide = jax.ShapeDtypeStruct((layers, sections * quarter, count * own_width), f32)
    arrays = list(swapped) + list(shared)
    return pl.pallas_call(
        body,
        grid=(layers,),
        out_shape=[wide, wide, jax.ShapeDtypeStruct((layers, own_width, model), f32)],
        in_specs=[pl.BlockSpec(a.shape, lambda l, n=a.ndim: (0,) * n) for a in arrays],
        out_specs=[
            pl.BlockSpec((1, sections * quarter, count * own_width), lambda l: (l, 0, 0)),
            pl.BlockSpec((1, sections * quarter, count * own_width), lambda l: (l, 0, 0)),
            pl.BlockSpec((1, own_width, model), lambda l: (l, 0, 0)),
        ],
        compiler_params=pltpu.CompilerParams(vmem_limit_bytes=VMEM_LIMIT),
    )(*arrays)


def stream_marks(starts, tokens):
    places = jnp.arange(tokens + 3, dtype=jnp.int32)

    def resets(p):
        return jnp.any(p[:, None] == starts[None, :], axis=1).astype(f32)

    first = 1.0 - resets(places)
    second = first * (1.0 - resets(places - 1))
    third = second * (1.0 - resets(places - 2))
    inside = (places < tokens).astype(f32)
    columns = [resets(places)[:tokens], first[:tokens], second[:tokens], third[:tokens]]
    for k, keep in ((1, first), (2, second), (3, third)):
        columns.append((keep * inside)[k : k + tokens])
    columns.append(jnp.zeros((tokens,), f32))
    return jnp.stack(columns, axis=1)


def on_device(
    inputs,
    doc_starts,
    valid_mask,
    cotangent,
    prev_state,
    prev_inputs,
    rec_gain,
    in_weight,
    side_weight,
    out_weight,
    rate_blocks,
    inflow_blocks,
    rate_bias,
    inflow_bias,
    conv_taps,
    conv_bias,
    lru_param,
    mlp_gain,
    gate_weight,
    up_weight,
    down_weight,
):
    sections = lax.axis_size("section")
    section = lax.axis_index("section")
    count = lax.axis_size("seq")
    place = lax.axis_index("seq")
    layers, d_rows, lru_width = in_weight.shape
    model = inputs.shape[2]
    tokens = inputs.shape[1] * count
    hidden_part = down_weight.shape[1]
    own_width = out_weight.shape[1]
    block_count, block_rows, block_width = rate_blocks.shape[1:]
    window = 2 * block_width
    quarter = d_rows // sections
    block_quarter = block_rows // sections
    first_block = [min(q * own_width // block_width, block_count - 2) for q in range(count)]
    owner = [min(q for q in range(count) if first_block[q] <= b <= first_block[q] + 1) for b in range(block_count)]
    block_start = jnp.asarray(first_block, jnp.int32)[place]
    offset = place * own_width - block_start * block_width
    window_start = block_start * block_width
    next_id = iter(range(64))

    def window_of(a, axis):
        return lax.dynamic_slice_in_dim(a, window_start, window, axis)

    x0 = lax.dynamic_index_in_dim(inputs, section, 0, False)
    cot = lax.dynamic_index_in_dim(cotangent, section, 0, False)
    valid = lax.dynamic_index_in_dim(valid_mask, section, 0, False)

    gate_blocks = jnp.stack([rate_blocks, inflow_blocks])

    def block_of(target):
        block = target * own_width // block_width
        return block - block // (block_count - 1)

    def rows_here():
        return pl.ds(pl.multiple_of(lax.axis_index("section") * quarter, quarter), quarter)

    def send_rec(l):
        def cut(refs, target):
            lanes = pl.ds(pl.multiple_of(block_of(target) * block_width, block_width), window)
            return [ref.at[l, rows_here(), lanes] for ref in refs]

        def fill(view):
            return [view.at[:, pl.ds(i * window, window)] for i in range(2)]

        wide = Spread(
            [in_weight, side_weight],
            (count, sections, quarter, 2 * window),
            2,
            cut,
            fill,
            lambda out, source, s: out.at[source, s],
        )

        def cut_gates(refs, target):
            s = lax.axis_index("section")
            return [refs[0].at[s // 2, l, block_of(target) + s % 2]]

        gates = Spread(
            [gate_blocks],
            (sections, count, block_rows, block_width),
            1,
            cut_gates,
            lambda view: [view],
            lambda out, source, s: out.at[s, source],
        )
        return [wide, gates]

    def send_mlp(l):
        shape = (count, sections, quarter, 2 * hidden_part)
        if hidden_part % 128:
            pair = [
                lax.dynamic_slice_in_dim(a[l], section * quarter, quarter, 0).reshape(quarter, count, hidden_part)
                for a in (gate_weight, up_weight)
            ]
            packed = jnp.transpose(jnp.concatenate(pair, axis=2), (1, 0, 2))
            return [
                Spread(
                    [packed],
                    shape,
                    1,
                    lambda refs, target: [refs[0].at[target]],
                    lambda view: [view],
                    lambda out, source, s: out.at[source, s],
                )
            ]

        def cut(refs, target):
            lanes = pl.ds(pl.multiple_of(target * hidden_part, hidden_part), hidden_part)
            return [ref.at[l, rows_here(), lanes] for ref in refs]

        def fill(view):
            return [view.at[:, pl.ds(i * hidden_part, hidden_part)] for i in range(2)]

        return [
            Spread(
                [gate_weight, up_weight],
                shape,
                2,
                cut,
                fill,
                lambda out, source, s: out.at[source, s],
            )
        ]

    def unpack_rec(wide, gates):
        return wide.reshape(model, 2 * window), gates.reshape(2, 2, block_width, block_width)

    reach = window - own_width

    def out_window(strip):
        return lax.dynamic_slice_in_dim(strip, reach - offset, window, 0)

    packed = jnp.concatenate(
        [rate_bias[:, None], inflow_bias[:, None], conv_taps, conv_bias[:, None], lru_param[:, None]], axis=1
    )
    gains_own = jnp.stack([rec_gain, mlp_gain], axis=1)
    flat = jnp.concatenate([packed.reshape(-1), gains_own.reshape(-1)]).reshape(16, -1)
    x_all, flat, *got = comm("start", next(next_id), x=x0, jobs=[Everyone(flat, count)] + send_rec(0))
    flat = flat.reshape(count, -1)
    small_all = flat[:, : packed.size].reshape(count, layers, 8, own_width)
    small_all = jnp.transpose(small_all, (1, 2, 0, 3)).reshape(layers, 8, lru_width)
    gains = flat[:, packed.size :].reshape(count, layers, 2, d_rows)
    gains = jnp.transpose(gains, (1, 2, 0, 3)).reshape(layers, 2, model)
    small = window_of(small_all, 2).astype(f32)
    x_wide = x_all.astype(f32)
    scale = lax.rsqrt(jnp.mean(x_wide * x_wide, axis=-1, keepdims=True) + epsilon)
    normed = (x_wide * scale * gains[0, 0].astype(f32)).astype(bf16)

    masked = (cot.astype(f32) * valid[:, None].astype(f32)).astype(bf16)
    marks = stream_marks(lax.dynamic_index_in_dim(doc_starts, section, 0, False), tokens)
    first_state = window_of(lax.dynamic_index_in_dim(prev_state, section, 0, False), 1).astype(f32)
    first_state = jnp.broadcast_to(first_state[:, None], (layers, 8, window))
    rim = window_of(lax.dynamic_index_in_dim(prev_inputs, section, 0, False), 2).astype(f32)
    rim = jnp.concatenate([jnp.zeros((layers, 5, window), f32), rim], axis=1)
    channel = jnp.arange(window, dtype=jnp.int32)
    own = jnp.logical_and(channel >= offset, channel < offset + own_width).astype(f32)
    own = jnp.broadcast_to(own[None], (8, window))
    own_out = [
        lax.dynamic_update_slice(jnp.zeros((window, model), bf16), out_weight[l], (offset, 0)) for l in range(layers)
    ]

    x = x0
    kept = []
    rec_weights, mlp_weights = [], []
    for l in range(layers):
        wide_weight, gates = unpack_rec(*got)
        rec_weights.append((wide_weight, gates))
        wide = dot(normed, wide_weight)
        gated, *saved = middle_forward(wide, marks, gates, small[l], rim[l], first_state[l])
        part = dot(gated, own_out[l]).astype(bf16)
        kept.append((x, normed, wide, gated, saved))
        normed, x, *got = comm("forward", next(next_id), part, x, gain=gains[l, 1], jobs=send_mlp(l))
        mlp_weights.append(got[0].reshape(model, 2 * hidden_part))
        if l == 0:
            masked_all = lax.all_gather(lax.optimization_barrier((masked, x))[0], "seq", axis=0, tiled=True)
        both = dot(normed, mlp_weights[l])
        hidden = (jax.nn.gelu(both[:, :hidden_part]) * both[:, hidden_part:]).astype(bf16)
        part = dot(hidden, down_weight[l]).astype(bf16)
        kept.append((x, normed, both, hidden))
        if l + 1 < layers:
            normed, x, *got = comm("forward", next(next_id), part, x, gain=gains[l + 1, 0], jobs=send_rec(l + 1))
        else:
            last_part, last_x = part, x

    mlp_lanes = np.gcd(256, hidden_part).item()
    rec_lanes = np.gcd(128, 2 * own_width).item()

    def by_target(grad, lanes):
        chunks = grad.shape[1] // lanes
        grad = grad.astype(bf16).reshape(count, sections, quarter, chunks, lanes)
        return jnp.transpose(grad, (1, 0, 3, 2, 4)).reshape(sections, count, chunks * quarter, lanes)

    def by_section(grad, lanes):
        rows, chunks = grad.shape[0] // sections, grad.shape[1] // lanes
        grad = grad.astype(bf16).reshape(sections, rows, chunks, lanes)
        return jnp.transpose(grad, (0, 2, 1, 3)).reshape(sections, chunks * rows, lanes)

    def gates_by_target(grad, lanes):
        chunks = block_width // lanes
        grad = grad.astype(bf16).reshape(2, 2, count, sections, block_quarter, chunks, lanes)
        return jnp.transpose(grad, (3, 2, 0, 1, 5, 4, 6)).reshape(sections, count, -1, lanes)

    direct = hidden_part % 256 == 0 and rec_lanes == 128 and own_width % 64 == 0

    def bundle(swapped, shared):
        lanes = swapped.shape[3]
        return jnp.concatenate([swapped.reshape(sections, -1, lanes), shared], axis=1)

    def scatter(whole, rows):
        whole = whole.reshape(-1, whole.shape[-1])
        mine = lax.psum_scatter(whole, "section", scatter_dimension=0, tiled=True)
        return grad_jobs(mine, rows)

    def grad_jobs(mine, rows):
        def cut(refs, target):
            return [refs[0].at[pl.ds(pl.multiple_of(target * rows, 8), rows)]]

        return [
            Spread(
                [mine],
                (count, sections, rows, mine.shape[1]),
                1,
                cut,
                lambda view: [view],
                lambda out, source, s: out.at[source, s],
            ),
            Share(mine, count * rows, mine.shape[0] - count * rows),
        ]

    d_rows_own, d_all = masked, masked_all
    dgains = [[None, None] for _ in range(layers)]
    waiting, spread, sums_own = {}, {}, [None] * layers
    for l in reversed(range(layers)):
        x, normed, both, hidden = kept[2 * l + 1]
        d_hidden = dot_t(d_all, down_weight[l])
        gate, slope = gelu_pair(both[:, :hidden_part])
        d_gate = (d_hidden * both[:, hidden_part:] * slope).astype(bf16)
        d_up = (d_hidden * gate).astype(bf16)
        d_both = jnp.concatenate([d_gate, d_up], axis=1)
        part = dot_t(d_both, mlp_weights[l]).astype(bf16)
        if direct:
            whole = grads_mlp(normed, d_both, hidden, d_all, sections, count, mlp_lanes)
        else:
            down = by_section(dot_rows(hidden, d_all), mlp_lanes)
            whole = bundle(by_target(dot_rows(normed, d_both), mlp_lanes), down)
        part, whole = lax.optimization_barrier((part, whole))
        waiting["mlp", l] = scatter(whole, 2 * hidden_part // mlp_lanes * quarter)
        jobs = waiting["mlp", l + 1] if l + 1 < layers else []
        d_all, d_rows_own, dgains[l][1], strip, *got = comm(
            "back", next(next_id), part, x, d_rows_own, gains[l, 1], [Beside(out_weight, l, reach)] + jobs
        )
        if jobs:
            spread["mlp", l + 1] = got

        x, normed, wide, gated, saved = kept[2 * l]
        wide_weight, gates = rec_weights[l]
        d_gated = dot_t(d_all, out_window(strip))
        dib, d_rate, d_inflow, sums = middle_backward(
            d_gated, wide, saved, marks, gates, small[l], rim[l], own
        )
        part = dot_t(dib, wide_weight).astype(bf16)
        if direct:
            whole = grads_rec(
                normed, dib, gated, d_all, saved[0], d_rate, d_inflow, offset, own_width, sections, count, rec_lanes
            )
        else:
            grad_out = lax.dynamic_slice_in_dim(dot_rows(gated, d_all), offset, own_width, 0)
            grad_wide = dot_rows(normed, dib)
            swapped = by_target(
                jnp.concatenate(
                    [
                        lax.dynamic_slice_in_dim(grad_wide, offset, own_width, 1),
                        lax.dynamic_slice_in_dim(grad_wide, offset + window, own_width, 1),
                    ],
                    axis=1,
                ),
                rec_lanes,
            )
            low = saved[0].astype(bf16).reshape(tokens, 2, block_width)
            d_gates = jnp.stack([d_rate, d_inflow]).reshape(2, tokens, 2, block_width)
            grad_gates = jnp.einsum("tbi,gtbj->gbij", low, d_gates, preferred_element_type=f32)
            swapped = jnp.concatenate([swapped, gates_by_target(grad_gates, rec_lanes)], axis=2)
            whole = bundle(swapped, by_section(grad_out, rec_lanes))
        sums_own[l] = lax.dynamic_slice_in_dim(sums, offset, own_width, 1)
        part, whole = lax.optimization_barrier((part, whole))
        waiting["rec", l] = scatter(whole, (2 * own_width * quarter + 4 * block_width * block_quarter) // rec_lanes)
        jobs = waiting["rec", l + 1] if l + 1 < layers else []
        if l > 0:
            d_all, d_rows_own, dgains[l][0], *got = comm(
                "back", next(next_id), part, x, d_rows_own, gains[l, 0], jobs
            )
        else:
            input_grad, dgains[l][0], *got = comm("last", next(next_id), part, x, d_rows_own, gains[l, 0], jobs)
        if jobs:
            spread["rec", l + 1] = got

    last_part, last_x, _ = lax.optimization_barrier((last_part, last_x, input_grad))
    outputs, *got = comm("rows", next(next_id), last_part, last_x, jobs=waiting["mlp", 0])
    spread["mlp", 0] = got

    sums_lanes = -(-own_width // 256) * 256
    sums = jnp.pad(jnp.concatenate(sums_own, axis=0), ((0, 0), (0, sums_lanes - own_width)))
    sums = sums.reshape(-1, 256)
    dgain_all = jnp.concatenate([a for pair in dgains for a in pair], axis=0).reshape(2 * layers, count, d_rows)
    dgain_all = jnp.pad(jnp.transpose(dgain_all, (1, 0, 2)), ((0, 0), (0, 8 - 2 * layers), (0, 256 - d_rows)))
    tiny = jnp.concatenate([dgain_all.reshape(-1, 256), sums], axis=0)
    tiny, _ = lax.optimization_barrier((tiny, outputs))
    *got, dgain_all, sums = comm("none", next(next_id), jobs=waiting["rec", 0] + grad_jobs(tiny, 8))
    spread["rec", 0] = got
    sums = jnp.sum(sums, axis=0).reshape(layers, 8, sums_lanes)[:, :, :own_width]
    dgain_all = jnp.sum(dgain_all, axis=(0, 1))[: 2 * layers, :d_rows].reshape(layers, 2, d_rows)

    def both_layers(name):
        return [spread[name, l][0] for l in range(layers)], [spread[name, l][1] for l in range(layers)]

    def columns(parts, first, last, lanes):
        out = []
        for p in parts:
            chunks = p.shape[2] // quarter
            p = p[:, :, : chunks * quarter].reshape(count, sections, chunks, quarter, lanes)
            p = jnp.transpose(p, (1, 3, 0, 2, 4)).reshape(d_rows, count, chunks * lanes)
            out.append(p[:, :, first:last].reshape(d_rows, -1).astype(f32))
        return jnp.stack(out)

    def rows(parts, size, lanes):
        out = []
        for p in parts:
            p = jnp.transpose(p.reshape(sections, -1, size, lanes), (0, 2, 1, 3))
            out.append(p.reshape(sections * size, -1).astype(f32))
        return jnp.stack(out)

    mlp_swapped, mlp_shared = both_layers("mlp")
    rec_swapped, rec_shared = both_layers("rec")
    if direct:
        gate_grad, up_grad, down_grad = place_mlp(mlp_swapped, mlp_shared, quarter, hidden_part)
        in_grad, side_grad, out_grad = place_rec(rec_swapped, rec_shared, quarter, own_width)
    else:
        gate_grad = columns(mlp_swapped, 0, hidden_part, mlp_lanes)
        up_grad = columns(mlp_swapped, hidden_part, 2 * hidden_part, mlp_lanes)
        down_grad = rows(mlp_shared, hidden_part // sections, mlp_lanes)
        in_grad = columns(rec_swapped, 0, own_width, rec_lanes)
        side_grad = columns(rec_swapped, own_width, 2 * own_width, rec_lanes)
        out_grad = rows(rec_shared, own_width // sections, rec_lanes)

    gate_out = []
    for l in range(layers):
        got = rec_swapped[l][:, :, 2 * own_width // rec_lanes * quarter :]
        got = got.reshape(count, sections, 2, 2, block_width // rec_lanes, block_quarter, rec_lanes)
        blocks = jnp.stack([got[owner[b], :, :, b - first_block[owner[b]]] for b in range(block_count)])
        blocks = jnp.transpose(blocks, (2, 0, 1, 4, 3, 5))
        gate_out.append(blocks.reshape(2, block_count, block_rows, block_width))
    gate_out = jnp.stack(gate_out).astype(f32)

    return (
        outputs[None],
        input_grad[None],
        dgain_all[:, 0],
        in_grad,
        side_grad,
        out_grad,
        gate_out[:, 0],
        gate_out[:, 1],
        sums[:, 0],
        sums[:, 1],
        sums[:, 2:6],
        sums[:, 6],
        sums[:, 7],
        dgain_all[:, 1],
        gate_grad,
        up_grad,
        down_grad,
    )


def solution(mesh):
    return jax.shard_map(
        on_device,
        mesh=mesh,
        in_specs=(
            P(None, "seq", None),
            P(),
            P(None, "seq"),
            P(None, "seq", None),
            P(),
            P(),
            P(None, "seq"),
            P(None, "seq", None),
            P(None, "seq", None),
            P(None, "seq", None),
            P(None, None, "seq", None),
            P(None, None, "seq", None),
            P(None, "seq"),
            P(None, "seq"),
            P(None, None, "seq"),
            P(None, "seq"),
            P(None, "seq"),
            P(None, "seq"),
            P(None, "seq", None),
            P(None, "seq", None),
            P(None, "seq", None),
        ),
        out_specs=(
            P("section", "seq", None),
            P("section", "seq", None),
            P(None, "seq"),
            P(None, "seq", None),
            P(None, "seq", None),
            P(None, "seq", None),
            P(None, None, "seq", None),
            P(None, None, "seq", None),
            P(None, "seq"),
            P(None, "seq"),
            P(None, None, "seq"),
            P(None, "seq"),
            P(None, "seq"),
            P(None, "seq"),
            P(None, "seq", None),
            P(None, "seq", None),
            P(None, "seq", None),
        ),
        check_vma=False,
    )
```

```python
from functools import partial

import jax
import jax.numpy as jnp
import numpy as np
from jax import lax
from jax.experimental import pallas as pl
from jax.experimental.pallas import tpu as pltpu
from jax.sharding import PartitionSpec as P


epsilon = 1e-06
rate_scale = 8.0
MESH = pl.DeviceIdType.MESH
VMEM_LIMIT = 60 * 1024 * 1024
f32 = jnp.float32
bf16 = jnp.bfloat16


def plane_place():
    section = lax.axis_index("section")
    column, row = section % 2, section // 2
    return section, row * 2 + 1 - column, (1 - row) * 2 + column


def dma(*shape):
    return pltpu.SemaphoreType.DMA(shape)


def along(source, target, send, receive, peer):
    return pltpu.make_async_remote_copy(
        src_ref=source,
        dst_ref=target,
        send_sem=send,
        recv_sem=receive,
        device_id={"seq": peer},
        device_id_type=MESH,
    )


class Item:
    def __init__(self, first, at, sems, slot, even):
        self.first, self.at, self.sems, self.slot, self.even = first, at, sems, slot, even
        self.section, self.side, self.up = plane_place()

    def copy(self, way, source, holder, target):
        return pltpu.make_async_remote_copy(
            src_ref=source,
            dst_ref=self.at(holder),
            send_sem=self.sems.at[way, 0, self.slot],
            recv_sem=self.sems.at[way, 1, self.slot],
            device_id={"section": target},
            device_id_type=MESH,
        )

    def start(self):
        self.to_side = self.copy(0, self.first, self.section, self.side)
        self.to_up = self.copy(1, self.first, self.section, self.up)
        self.to_side.start()
        self.to_up.start()

    def forward(self):
        self.to_side.wait_recv()
        if self.even:
            self.onward = self.copy(2, self.at(self.side), self.side, self.up)
            self.onward.start()
        self.to_up.wait_recv()
        if not self.even:
            self.onward = self.copy(2, self.at(self.up), self.up, self.side)
            self.onward.start()

    def finish(self):
        self.onward.wait()
        self.to_side.wait_send()
        self.to_up.wait_send()


class Keep:
    def __init__(self, pieces, places, stage, target, sems, out_sem):
        self.come = [pltpu.make_async_copy(a, b, sems.at[i]) for i, (a, b) in enumerate(zip(pieces, places))]
        self.go = pltpu.make_async_copy(stage, target, out_sem)
        for copy in self.come:
            copy.start()

    def land(self):
        for copy in self.come:
            copy.wait()
        self.go.start()

    def finish(self):
        self.go.wait()


class Spread:
    on_line, in_plane = True, True

    def __init__(self, arrays, shape, pieces, cut, fill, slot):
        self.arrays, self.pieces, self.cut, self.fill, self.slot = list(arrays), pieces, cut, fill, slot
        self.shape = jax.ShapeDtypeStruct(shape, self.arrays[0].dtype)

    def scratch(self, count):
        return [dma(2, self.pieces, count), dma(3, 2, count), pltpu.VMEM(self.shape.shape[2:], self.shape.dtype)]

    def begin(self, refs, out, sems, place, count):
        line, plane, stage = sems
        self.sends, self.items = [], []
        section = plane_place()[0]
        self.own = Keep(
            self.cut(refs, place), self.fill(stage), stage, self.slot(out, place, section), line.at[0, :, 0], line.at[1, 0, 0]
        )
        for k in range(count):
            source = (place + count - k) % count
            self.items.append(
                Item(
                    self.slot(out, source, section) if k > 0 else stage,
                    lambda s, source=source: self.slot(out, source, s),
                    plane,
                    k,
                    k % 2 == 0,
                )
            )

        def push():
            for k in range(1, count):
                peer = (place + k) % count
                pieces = zip(self.cut(refs, peer), self.fill(self.slot(out, place, section)))
                group = [
                    along(piece, there, line.at[0, i, k], line.at[1, i, k], peer)
                    for i, (piece, there) in enumerate(pieces)
                ]
                for copy in group:
                    copy.start()
                self.sends.append(group)

        self.push = push

    def own_block(self):
        self.own.land()
        self.items[0].start()

    def arrive(self, k):
        for copy in self.sends[k - 1]:
            copy.wait_recv()
        self.items[k].start()
        self.items[k - 1].forward()

    def finish(self):
        self.items[-1].forward()
        self.own.finish()
        for item in self.items:
            item.finish()
        for group in self.sends:
            for copy in group:
                copy.wait_send()


class Line:
    on_line, in_plane = True, False

    def __init__(self, arrays, shape, pieces, cut, fill):
        self.arrays, self.pieces, self.cut, self.fill = list(arrays), pieces, cut, fill
        self.shape = jax.ShapeDtypeStruct(shape, self.arrays[0].dtype)

    def scratch(self, count):
        return [dma(2, self.pieces, count), pltpu.VMEM(self.shape.shape[1:], self.shape.dtype)]

    def begin(self, refs, out, sems, place, count):
        line, stage = sems
        self.sends = []
        self.own = Keep(
            self.cut(refs, place), self.fill(stage), stage, out.at[place], line.at[0, :, 0], line.at[1, 0, 0]
        )

        def push():
            for k in range(1, count):
                peer = (place + k) % count
                pieces = zip(self.cut(refs, peer), self.fill(out.at[place]))
                group = [
                    along(piece, there, line.at[0, i, k], line.at[1, i, k], peer)
                    for i, (piece, there) in enumerate(pieces)
                ]
                for copy in group:
                    copy.start()
                self.sends.append(group)

        self.push = push

    def own_block(self):
        self.own.land()

    def arrive(self, k):
        pass

    def finish(self):
        self.own.finish()
        for group in self.sends:
            for copy in group:
                copy.wait()


class Plane:
    on_line, in_plane = False, True

    def __init__(self, array, shape, slot, column):
        self.arrays, self.slot, self.column = [array], slot, column
        self.shape = jax.ShapeDtypeStruct(shape, array.dtype)

    def scratch(self, count):
        return [dma(3, 2, count), dma(2), pltpu.VMEM(self.arrays[0].shape, self.shape.dtype)]

    def begin(self, refs, out, sems, place, count):
        plane, own, stage = sems
        section = plane_place()[0]
        self.items = []
        self.own = Keep([refs[0]], [stage], stage, self.column(out, section), own, own.at[1])
        for k in range(count):
            item = Item(refs[0].at[k], lambda s, k=k: self.slot(out, k, s), plane, k, k % 2 == 0)
            item.start()
            self.items.append(item)

    def push(self):
        pass

    def own_block(self):
        self.own.land()

    def arrive(self, k):
        if k > 1:
            self.items[k - 2].forward()

    def finish(self):
        for item in self.items[-2:]:
            item.forward()
        for item in self.items:
            item.finish()
        self.own.finish()


class Share:
    on_line, in_plane = False, True

    def __init__(self, array, start, size):
        self.arrays, self.start, self.size = [array], start, size
        self.shape = jax.ShapeDtypeStruct((4, size, array.shape[1]), array.dtype)

    def scratch(self, count):
        return [dma(3, 2, 2), dma(2), pltpu.VMEM(self.shape.shape[1:], self.shape.dtype)]

    def begin(self, refs, out, sems, place, count):
        plane, own, stage = sems
        section = plane_place()[0]
        mine = refs[0].at[pl.ds(self.start, self.size)]
        self.own = Keep([mine], [stage], stage, out.at[section], own, own.at[1])
        half = self.size // 2
        self.items = []
        for h in range(2):
            rows = pl.ds(h * half, half)
            first = refs[0].at[pl.ds(self.start + h * half, half)]
            item = Item(first, lambda s, rows=rows: out.at[s, rows], plane, h, h == 0)
            item.start()
            self.items.append(item)

    def push(self):
        pass

    def own_block(self):
        self.own.land()

    def arrive(self, k):
        if k in (4, 6):
            self.items[k // 2 - 2].forward()

    def finish(self):
        self.own.finish()
        for item in self.items:
            item.finish()


class Everyone:
    on_line, in_plane = True, False

    def __init__(self, array, count):
        self.arrays = [array]
        self.shape = jax.ShapeDtypeStruct((count,) + array.shape, array.dtype)

    def scratch(self, count):
        return [dma(2, count)]

    def begin(self, refs, out, sems, place, count):
        self.own = pltpu.make_async_copy(refs[0], out.at[place], sems[0].at[0, 0])
        self.own.start()
        self.sends = []
        for k in range(1, count):
            copy = along(refs[0], out.at[place], sems[0].at[0, k], sems[0].at[1, k], (place + k) % count)
            copy.start()
            self.sends.append(copy)

    def push(self):
        pass

    def own_block(self):
        self.own.wait()

    def arrive(self, k):
        self.sends[k - 1].wait_recv()

    def finish(self):
        for copy in self.sends:
            copy.wait_send()


class Beside:
    on_line, in_plane = True, False

    def __init__(self, array, layer, reach):
        self.arrays, self.layer, self.reach = [array], layer, reach
        self.rows = array.shape[1]
        self.shape = jax.ShapeDtypeStruct((2, reach, array.shape[2]), array.dtype)
        self.sizes = [min(self.rows, reach - at) for at in range(0, reach, self.rows)]

    def scratch(self, count):
        return [dma(2, 2, len(self.sizes) + 1)]

    def begin(self, refs, out, sems, place, count):
        mine, sem = refs[0].at[self.layer], sems[0]
        self.ends = []
        done = 0
        for k, size in enumerate(self.sizes, 1):
            ahead = along(
                mine.at[pl.ds(self.rows - size, size)],
                out.at[0, pl.ds(self.reach - done - size, size)],
                sem.at[0, 0, k],
                sem.at[0, 1, k],
                place + k,
            )
            back = along(
                mine.at[pl.ds(0, size)],
                out.at[1, pl.ds(done, size)],
                sem.at[1, 0, k],
                sem.at[1, 1, k],
                place - k,
            )
            pl.when(place + k < count)(ahead.start)
            pl.when(place >= k)(back.start)
            self.ends.append((k, ahead, back))
            done += size
        self.place, self.count = place, count

    def push(self):
        pass

    def own_block(self):
        pass

    def arrive(self, k):
        pass

    def finish(self):
        for k, ahead, back in self.ends:
            pl.when(self.place >= k)(ahead.wait_recv)
            pl.when(self.place + k < self.count)(back.wait_recv)
            pl.when(self.place + k < self.count)(ahead.wait_send)
            pl.when(self.place >= k)(back.wait_send)


def comm_body(mode, count, jobs, refs):
    chips = count // 2
    has_sum = mode in ("forward", "back", "last", "rows")
    has_gather = mode in ("start", "forward", "back")
    backward = mode in ("back", "last")
    refs = list(refs)
    take = refs.pop
    part_ref = take(0) if has_sum else None
    x_ref = take(0) if mode != "none" else None
    dy_ref = take(0) if backward else None
    gain_ref = take(0) if mode in ("forward", "back", "last") else None
    job_refs = [[take(0) for _ in job.arrays] for job in jobs]
    out_ref = take(0) if has_gather else None
    rows_ref = take(0) if has_sum else None
    dgain_ref = take(0) if backward else None
    job_outs = [take(0) for _ in jobs]
    if has_sum:
        pair_ref, staged_ref, landed_ref, pair_sem, sum_sem = (take(0) for _ in range(5))
    if has_gather:
        hop_sem, mate_sem = (take(0) for _ in range(2))
    job_sems = [[take(0) for _ in job.scratch(count)] for job in jobs]

    place = lax.axis_index("seq")
    chip, core = place // 2, place % 2
    mate = chip * 2 + 1 - core
    section, side, up = plane_place()

    barrier = pltpu.get_barrier_semaphore()
    met = 0
    line = []
    if any(job.on_line for job in jobs):
        line = [(place + k) % count for k in range(1, count)]
    elif mode != "none":
        line = [mate] + [((chip + k) % chips) * 2 + core for k in range(1, chips)]
    for peer in line:
        pl.semaphore_signal(barrier, inc=1, device_id={"seq": peer}, device_id_type=MESH)
        met += 1
    if any(job.in_plane for job in jobs):
        for peer in (side, up):
            pl.semaphore_signal(barrier, inc=1, device_id={"section": peer}, device_id_type=MESH)
            met += 1
    pl.semaphore_wait(barrier, met)

    def origin(way, k):
        return chip - k if way == 0 else chip + k

    def comes(way, k):
        return chip >= k if way == 0 else chip + k < chips

    def goes_on(way):
        return chip + 1 < chips if way == 0 else chip >= 1

    def hop(way, k):
        slot = origin(way, k) * 2 + core
        onward = chip + 1 if way == 0 else chip - 1
        return along(
            out_ref.at[slot], out_ref.at[slot], hop_sem.at[way, 0, k], hop_sem.at[way, 1, k + 1], onward * 2 + core
        )

    def landing(way, k):
        slot = origin(way, k) * 2 + core
        return along(out_ref.at[slot], out_ref.at[slot], hop_sem.at[way, 0, k], hop_sem.at[way, 1, k], mate)

    def across(way, k):
        slot = origin(way, k) * 2 + core
        return along(out_ref.at[slot], out_ref.at[slot], mate_sem.at[way, 0, k], mate_sem.at[way, 1, k], mate)

    def begin_gather(rows):
        out_ref[place] = rows
        for way in range(2):
            pl.when(goes_on(way))(hop(way, 0).start)
        across(0, 0).start()

    def land(k):
        for way in range(2):

            @pl.when(comes(way, k))
            def _(way=way, k=k):
                landing(way, k).wait_recv()
                pl.when(goes_on(way))(hop(way, k).start)
                across(way, k).start()

    if mode == "start":
        begin_gather(x_ref[...])
    if has_sum:
        pair_copies = []
        for k in list(range(1, chips)) + [0]:
            to_chip = (chip + k) % chips
            copy = along(
                part_ref.at[to_chip * 2 + 1 - core], pair_ref.at[k], pair_sem.at[0, k], pair_sem.at[1, k], mate
            )
            copy.start()
            pair_copies.append((k, copy))
    for job, ref, out, sems in zip(jobs, job_refs, job_outs, job_sems):
        job.begin(ref, out, sems, place, count)
    for job in jobs:
        job.push()
    if has_sum:
        sum_copies = []
        total = None
        for k, copy in pair_copies:
            to_chip = (chip + k) % chips
            copy.wait_recv()
            both = part_ref[to_chip * 2 + core].astype(f32) + pair_ref[k].astype(f32)
            if k == 0:
                total = both
            else:
                staged_ref[k] = both.astype(bf16)
                send = along(
                    staged_ref.at[k], landed_ref.at[k], sum_sem.at[0, k], sum_sem.at[1, k], to_chip * 2 + core
                )
                send.start()
                sum_copies.append((k, send))
    for job in jobs:
        job.own_block()
    for k in range(1, count):
        for job in jobs:
            job.arrive(k)
        if mode == "start" and k % 2 == 0:
            land(k // 2)
    if has_sum:
        for k, send in sum_copies:
            send.wait_recv()
            total = total + landed_ref[k].astype(f32)

    if mode != "none":
        x_wide = x_ref[...].astype(f32)
    if mode == "rows":
        rows_ref[...] = (x_wide + total).astype(bf16)
    elif mode == "forward":
        x_low = (x_wide + total).astype(bf16)
        rows_ref[...] = x_low
        x_wide = x_low.astype(f32)
        scale = lax.rsqrt(jnp.mean(x_wide * x_wide, axis=-1, keepdims=True) + epsilon)
        sent = (x_wide * scale * gain_ref[...]).astype(bf16)
    elif backward:
        scale = lax.rsqrt(jnp.mean(x_wide * x_wide, axis=-1, keepdims=True) + epsilon)
        scaled = total * gain_ref[...]
        inner_mean = jnp.mean(scaled * x_wide, axis=-1, keepdims=True)
        back = scale * scaled - x_wide * (scale * scale * scale * inner_mean)
        dgain_ref[...] = jnp.sum(total * x_wide * scale, axis=0, keepdims=True)
        sent = (dy_ref[...].astype(f32) + back).astype(bf16)
        rows_ref[...] = sent

    if has_gather and mode != "start":
        begin_gather(sent)
        for k in range(1, chips):
            land(k)

    for job in jobs:
        job.finish()
    if has_gather:
        across(0, 0).wait()
        for way in range(2):
            pl.when(goes_on(way))(hop(way, 0).wait_send)
        for k in range(1, chips):
            for way in range(2):

                @pl.when(comes(way, k))
                def _(way=way, k=k):
                    across(way, k).wait()
                    pl.when(goes_on(way))(hop(way, k).wait_send)

    if has_sum:
        for _, copy in pair_copies:
            copy.wait_send()
        for _, send in sum_copies:
            send.wait_send()


def comm(mode, collective_id, part=None, x=None, dy=None, gain=None, jobs=(), us=50):
    count = lax.axis_size("seq")
    chips = count // 2
    has_sum = mode in ("forward", "back", "last", "rows")
    has_gather = mode in ("start", "forward", "back")
    backward = mode in ("back", "last")
    in_vmem = pl.BlockSpec(memory_space=pltpu.VMEM)
    in_hbm = pl.BlockSpec(memory_space=pl.ANY)
    operands, in_specs, shapes, out_specs, scratch = [], [], [], [], []

    def give(a, spec):
        operands.append(a)
        in_specs.append(spec)

    def want(shape, spec):
        shapes.append(shape)
        out_specs.append(spec)

    if mode != "none":
        rows, width = x.shape
    if has_sum:
        give(part.reshape(count, rows, width), in_vmem)
    if mode != "none":
        give(x, in_vmem)
    if backward:
        give(dy, in_vmem)
    if mode in ("forward", "back", "last"):
        give(gain.astype(f32).reshape(1, width), in_vmem)
    for job in jobs:
        for a in job.arrays:
            give(a, in_hbm)
    if has_gather:
        want(jax.ShapeDtypeStruct((count, rows, width), bf16), in_vmem)
    if has_sum:
        want(jax.ShapeDtypeStruct((rows, width), bf16), in_vmem)
    if backward:
        want(jax.ShapeDtypeStruct((1, width), f32), in_vmem)
    for job in jobs:
        want(job.shape, in_hbm)
    if has_sum:
        scratch += [pltpu.VMEM((chips, rows, width), bf16)] * 3 + [dma(2, chips)] * 2
    if has_gather:
        scratch += [dma(2, 2, chips + 1), dma(2, 2, chips)]
    for job in jobs:
        scratch += job.scratch(count)
    outs = pl.pallas_call(
        lambda *refs: comm_body(mode, count, jobs, refs),
        out_shape=shapes,
        in_specs=in_specs,
        out_specs=out_specs,
        scratch_shapes=scratch,
        cost_estimate=pl.CostEstimate(flops=us * 1_000_000_000, bytes_accessed=1_000_000, transcendentals=0),
        compiler_params=pltpu.CompilerParams(
            collective_id=collective_id, has_side_effects=True, vmem_limit_bytes=VMEM_LIMIT
        ),
    )(*operands)
    outs = list(outs)
    if has_gather:
        outs[0] = outs[0].reshape(count * rows, width)
    return outs


def less_exp(doubled):
    small = doubled * (
        1.0
        - doubled
        * (
            0.5
            - doubled
            * (1.0 / 6 - doubled * (1.0 / 24 - doubled * (1.0 / 120 - doubled * (1.0 / 720))))
        )
    )
    return jnp.where(doubled < 0.25, small, 1.0 - jnp.exp(-doubled))


def gelu_pair(v):
    c = np.float32(np.sqrt(2 / np.pi))
    t = jnp.tanh(c * (v + 0.044715 * v * v * v))
    slope = 0.5 * (1.0 + t) + 0.5 * v * (1.0 - t * t) * c * (1.0 + 3 * 0.044715 * v * v)
    return 0.5 * v * (1.0 + t), slope


def dot(a, b):
    return jnp.dot(a, b, preferred_element_type=f32)


def dot_t(a, b):
    return lax.dot_general(a, b, (((1,), (1,)), ((), ())), preferred_element_type=f32)


def dot_rows(a, b):
    return lax.dot_general(a, b, (((0,), (0,)), ((), ())), preferred_element_type=f32)


def soft(lru):
    spread = jnp.maximum(-lru, 0.0) + jnp.log1p(jnp.exp(-jnp.abs(lru)))
    return spread, -1.0 / (1.0 + jnp.exp(lru))


def middle_forward_body(
    rows,
    width,
    is_ref,
    marks_ref,
    blocks_ref,
    small_ref,
    rim_ref,
    first_ref,
    gated_ref,
    mixed_ref,
    rate_ref,
    inflow_ref,
    states_ref,
    before_ref,
    ext,
    decays,
    drives,
    carry,
):
    @pl.when(pl.program_id(0) == 0)
    def _():
        ext[0:8] = rim_ref[...]
        carry[...] = first_ref[...]

    block = width // 2
    inner = is_ref[:, :width].astype(bf16).astype(f32)
    ext[8 : 8 + rows] = inner
    reset = marks_ref[:, 0:1]
    mixed = (
        small_ref[6:7]
        + small_ref[2:3] * inner
        + small_ref[3:4] * (ext[7 : 7 + rows] * marks_ref[:, 1:2])
        + small_ref[4:5] * (ext[6 : 6 + rows] * marks_ref[:, 2:3])
        + small_ref[5:6] * (ext[5 : 5 + rows] * marks_ref[:, 3:4])
    )
    ext[0:8] = ext[rows : rows + 8]
    mixed_ref[...] = mixed
    low = mixed.astype(bf16)
    for b in range(2):
        lanes = slice(b * block, (b + 1) * block)
        rate_ref[:, lanes] = dot(low[:, lanes], blocks_ref[0, b]) + small_ref[0:1, lanes]
        inflow_ref[:, lanes] = dot(low[:, lanes], blocks_ref[1, b]) + small_ref[1:2, lanes]
    spread, _ = soft(small_ref[7:8])
    log_decay = (-rate_scale * spread) * jax.nn.sigmoid(rate_ref[...])
    kept = 1.0 - reset
    decays[...] = jnp.exp(log_decay) * kept
    factor = reset + kept * jnp.sqrt(less_exp(-2.0 * log_decay))
    drives[...] = factor * jax.nn.sigmoid(inflow_ref[...]) * mixed

    place = lax.broadcasted_iota(jnp.int32, (8, width), 0)

    def step(j, last):
        at = pl.ds(pl.multiple_of(j * 8, 8), 8)
        a, h = decays[at], drives[at]
        for k in (1, 2, 4):
            inside = place >= k
            h = jnp.where(inside, a * pltpu.roll(h, k, 0) + h, h)
            a = jnp.where(inside, a * pltpu.roll(a, k, 0), a)
        h = h + a * last
        states_ref[at] = h
        before_ref[at] = jnp.where(place >= 1, pltpu.roll(h, 1, 0), last)
        return jnp.broadcast_to(h[7:8], (8, width))

    carry[...] = lax.fori_loop(0, rows // 8, step, carry[...])
    gated_ref[...] = (states_ref[...] * gelu_pair(is_ref[:, width:])[0]).astype(bf16)


def middle_backward_body(
    rows,
    width,
    dg_ref,
    is_ref,
    mixed_ref,
    rate_ref,
    inflow_ref,
    states_ref,
    before_ref,
    marks_ref,
    blocks_ref,
    small_ref,
    rim_ref,
    own_ref,
    dib_ref,
    drate_ref,
    dinflow_ref,
    sums_ref,
    dm_ext,
    decays,
    dstates,
    carry,
):
    @pl.when(pl.program_id(0) == 0)
    def _():
        dm_ext[rows : rows + 8] = jnp.zeros((8, width), f32)
        carry[...] = jnp.zeros((8, width), f32)
        sums_ref[...] = jnp.zeros_like(sums_ref)

    block = width // 2
    own = own_ref[0:1]
    reset = marks_ref[:, 0:1]
    kept = 1.0 - reset
    side, slope = gelu_pair(is_ref[:, width:])
    d_gated = dg_ref[...]
    dib_ref[:, width:] = (d_gated * states_ref[...] * slope * own).astype(bf16)
    dstates[...] = d_gated * side
    spread, spread_slope = soft(small_ref[7:8])
    rate = jax.nn.sigmoid(rate_ref[...])
    log_decay = (-rate_scale * spread) * rate
    decays[...] = jnp.exp(log_decay) * kept

    place = lax.broadcasted_iota(jnp.int32, (8, width), 0)

    def step(j, after):
        at = pl.ds(pl.multiple_of(rows - 8 - j * 8, 8), 8)
        own_decay, h = decays[at], dstates[at]
        a = jnp.where(place < 7, pltpu.roll(own_decay, 7, 0), 1.0)
        for k in (1, 2, 4):
            inside = place < 8 - k
            h = jnp.where(inside, a * pltpu.roll(h, 8 - k, 0) + h, h)
            a = jnp.where(inside, a * pltpu.roll(a, 8 - k, 0), a)
        h = h + a * after
        dstates[at] = h
        return jnp.broadcast_to((own_decay * h)[0:1], (8, width))

    carry[...] = lax.fori_loop(0, rows // 8, step, carry[...])

    d_h = dstates[...]
    mixed = mixed_ref[...]
    inflow = jax.nn.sigmoid(inflow_ref[...])
    root = jnp.sqrt(less_exp(-2.0 * log_decay))
    factor = reset + kept * root
    decay = decays[...]
    twice = jnp.exp(2.0 * log_decay)
    d_log = d_h * before_ref[...] * decay - d_h * inflow * mixed * kept * (twice / root)
    d_lru = jnp.sum(d_log * rate, axis=0, keepdims=True) * (-rate_scale * spread_slope)
    d_rate = (d_log * (-rate_scale * spread) * rate * (1.0 - rate)).astype(bf16)
    through = d_h * factor
    d_inflow = (through * mixed * inflow * (1.0 - inflow)).astype(bf16)
    drate_ref[...] = d_rate
    dinflow_ref[...] = d_inflow
    for b in range(2):
        lanes = slice(b * block, (b + 1) * block)
        dm_ext[0:rows, lanes] = (
            ((through * inflow)[:, lanes] + dot_t(d_rate[:, lanes], blocks_ref[0, b]) + dot_t(d_inflow[:, lanes], blocks_ref[1, b]))
            .astype(bf16)
            .astype(f32)
        )
    d_mixed = dm_ext[0:rows]
    inner = is_ref[:, :width].astype(bf16).astype(f32)
    shifted = [d_mixed] + [dm_ext[k : k + rows] * marks_ref[:, 3 + k : 4 + k] for k in (1, 2, 3)]
    d_inner = small_ref[2:3] * shifted[0]
    for k in (1, 2, 3):
        d_inner = d_inner + small_ref[2 + k : 3 + k] * shifted[k]
    dib_ref[:, :width] = (d_inner * own).astype(bf16)

    def add(row, value):
        sums_ref[row : row + 1] += value

    add(0, jnp.sum(d_rate.astype(f32), axis=0, keepdims=True))
    add(1, jnp.sum(d_inflow.astype(f32), axis=0, keepdims=True))
    for k in range(4):
        add(2 + k, jnp.sum(shifted[k] * inner, axis=0, keepdims=True))
    add(6, jnp.sum(d_mixed, axis=0, keepdims=True))
    add(7, d_lru)

    @pl.when(pl.program_id(0) == pl.num_programs(0) - 1)
    def _():
        for k in (1, 2, 3):
            for t in range(k):
                add(2 + k, dm_ext[t : t + 1] * marks_ref[t : t + 1, k : k + 1] * rim_ref[8 + t - k : 9 + t - k])

    dm_ext[rows : rows + 8] = dm_ext[0:8]


def row_spec(rows, width, steps, reverse):
    if reverse:
        return pl.BlockSpec((rows, width), lambda i: (steps - 1 - i, 0))
    return pl.BlockSpec((rows, width), lambda i: (i, 0))


def whole_spec(shape):
    return pl.BlockSpec(shape, lambda i: (0,) * len(shape))


def middle_forward(wide, marks, blocks, small, rim, first):
    tokens, width = wide.shape[0], wide.shape[1] // 2
    rows = min(256, tokens)
    steps = tokens // rows
    here = partial(row_spec, rows, steps=steps, reverse=False)
    whole = [blocks, small, rim, first]
    kinds = [bf16, f32, f32, f32, f32, f32]
    return pl.pallas_call(
        partial(middle_forward_body, rows, width),
        grid=(steps,),
        out_shape=[jax.ShapeDtypeStruct((tokens, width), kind) for kind in kinds],
        in_specs=[here(2 * width), here(8)] + [whole_spec(a.shape) for a in whole],
        out_specs=[here(width)] * 6,
        scratch_shapes=[
            pltpu.VMEM((rows + 8, width), f32),
            pltpu.VMEM((rows, width), f32),
            pltpu.VMEM((rows, width), f32),
            pltpu.VMEM((8, width), f32),
        ],
        compiler_params=pltpu.CompilerParams(vmem_limit_bytes=VMEM_LIMIT),
    )(wide, marks, *whole)


def middle_backward(d_gated, wide, saved, marks, blocks, small, rim, own):
    tokens, width = d_gated.shape
    rows = min(256, tokens)
    steps = tokens // rows
    here = partial(row_spec, rows, steps=steps, reverse=True)
    whole = [blocks, small, rim, own]
    return pl.pallas_call(
        partial(middle_backward_body, rows, width),
        grid=(steps,),
        out_shape=[
            jax.ShapeDtypeStruct((tokens, 2 * width), bf16),
            jax.ShapeDtypeStruct((tokens, width), bf16),
            jax.ShapeDtypeStruct((tokens, width), bf16),
            jax.ShapeDtypeStruct((8, width), f32),
        ],
        in_specs=[here(width), here(2 * width)] + [here(width)] * 5 + [here(8)] + [whole_spec(a.shape) for a in whole],
        out_specs=[here(2 * width), here(width), here(width), whole_spec((8, width))],
        scratch_shapes=[
            pltpu.VMEM((rows + 8, width), f32),
            pltpu.VMEM((rows, width), f32),
            pltpu.VMEM((rows, width), f32),
            pltpu.VMEM((8, width), f32),
        ],
        compiler_params=pltpu.CompilerParams(vmem_limit_bytes=VMEM_LIMIT),
    )(d_gated, wide, *saved, marks, *whole)


def grads_mlp(normed, d_both, hidden, d_all, sections, count, lanes):
    tokens, model = normed.shape
    d_rows = model // count
    quarter = d_rows // sections
    chunks = d_both.shape[1] // lanes
    rows = chunks * quarter
    down_rows = hidden.shape[1] // sections
    per_block = rows // down_rows
    down_blocks = model // lanes // per_block

    def body(normed_ref, both_ref, hidden_ref, all_ref, out_ref):
        j = pl.program_id(0)

        @pl.when(j < count)
        def _():
            grad = dot_rows(normed_ref[...], both_ref[...])
            for s in range(sections):
                for ch in range(chunks):
                    out_ref[s, 0, ch * quarter : (ch + 1) * quarter] = grad[
                        s * quarter : (s + 1) * quarter, ch * lanes : (ch + 1) * lanes
                    ].astype(bf16)

        @pl.when(j >= count)
        def _():
            grad = dot_rows(hidden_ref[...], all_ref[...])
            for s in range(sections):
                for ch in range(per_block):
                    out_ref[s, 0, ch * down_rows : (ch + 1) * down_rows] = grad[
                        s * down_rows : (s + 1) * down_rows, ch * lanes : (ch + 1) * lanes
                    ].astype(bf16)

    return pl.pallas_call(
        body,
        grid=(count + down_blocks,),
        out_shape=jax.ShapeDtypeStruct((sections, count + down_blocks, rows, lanes), bf16),
        in_specs=[
            pl.BlockSpec((tokens, d_rows), lambda j: (0, jnp.minimum(j, count - 1))),
            pl.BlockSpec(d_both.shape, lambda j: (0, 0)),
            pl.BlockSpec(hidden.shape, lambda j: (0, 0)),
            pl.BlockSpec((tokens, per_block * lanes), lambda j: (0, jnp.maximum(j - count, 0))),
        ],
        out_specs=pl.BlockSpec((sections, 1, rows, lanes), lambda j: (0, j, 0, 0)),
        compiler_params=pltpu.CompilerParams(vmem_limit_bytes=VMEM_LIMIT),
    )(normed, d_both, hidden, d_all)


def grads_rec(normed, dib, gated, d_all, mixed, d_rate, d_inflow, offset, own_width, sections, count, lanes):
    tokens, model = normed.shape
    window = gated.shape[1]
    block = window // 2
    d_rows = model // count
    quarter = d_rows // sections
    chunks = 2 * own_width // lanes
    gate_rows = block // count // sections
    gate_chunks = block // lanes
    rows = chunks * quarter + 4 * gate_chunks * gate_rows
    out_rows = own_width // sections
    padded = out_rows + 16
    per_block = rows // padded
    out_blocks = model // lanes // per_block

    def body(offset_ref, normed_ref, dib_ref, gated_ref, all_ref, mixed_ref, rate_ref, inflow_ref, out_ref, own, gates, out_grad):
        j = pl.program_id(0)
        first = offset_ref[0]

        @pl.when(j == 0)
        def _():
            row = lax.broadcasted_iota(jnp.int32, (window, own_width), 0)
            column = lax.broadcasted_iota(jnp.int32, (window, own_width), 1)
            pick = (row == column + first).astype(f32).astype(bf16)
            own[...] = jnp.concatenate(
                [dot(dib_ref[:, :window], pick), dot(dib_ref[:, window:], pick)], axis=1
            ).astype(bf16)
            low = mixed_ref[...].astype(bf16)
            for i, ref in enumerate((rate_ref, inflow_ref)):
                for b in range(2):
                    at = slice(b * block, (b + 1) * block)
                    gates[2 * i + b] = dot_rows(low[:, at], ref[:, at])

        @pl.when(j < count)
        def _():
            grad = dot_rows(normed_ref[...], own[...])
            for s in range(sections):
                for ch in range(chunks):
                    out_ref[s, 0, ch * quarter : (ch + 1) * quarter] = grad[
                        s * quarter : (s + 1) * quarter, ch * lanes : (ch + 1) * lanes
                    ].astype(bf16)
                here = pl.ds(pl.multiple_of((j * sections + s) * gate_rows, gate_rows), gate_rows)
                pieces = [
                    gates[g, here, ch * lanes : (ch + 1) * lanes] for g in range(4) for ch in range(gate_chunks)
                ]
                out_ref[s, 0, chunks * quarter :] = jnp.concatenate(pieces, axis=0).astype(bf16)

        @pl.when(j >= count)
        def _():
            out_grad[...] = dot_rows(gated_ref[...], all_ref[...])
            for s in range(sections):
                here = pl.ds(pl.multiple_of(first + s * out_rows, 8), out_rows)
                for ch in range(per_block):
                    out_ref[s, 0, ch * padded : ch * padded + out_rows] = out_grad[
                        here, ch * lanes : (ch + 1) * lanes
                    ].astype(bf16)
                    out_ref[s, 0, ch * padded + out_rows : (ch + 1) * padded] = jnp.zeros((16, lanes), bf16)

    whole = lambda a: pl.BlockSpec(a.shape, lambda j, o, n=a.ndim: (0,) * n)
    return pl.pallas_call(
        body,
        grid_spec=pltpu.PrefetchScalarGridSpec(
            num_scalar_prefetch=1,
            grid=(count + out_blocks,),
            in_specs=[
                pl.BlockSpec((tokens, d_rows), lambda j, o: (0, jnp.minimum(j, count - 1))),
                whole(dib),
                whole(gated),
                pl.BlockSpec((tokens, per_block * lanes), lambda j, o: (0, jnp.maximum(j - count, 0))),
                whole(mixed),
                whole(d_rate),
                whole(d_inflow),
            ],
            out_specs=pl.BlockSpec((sections, 1, rows, lanes), lambda j, o: (0, j, 0, 0)),
            scratch_shapes=[
                pltpu.VMEM((tokens, 2 * own_width), bf16),
                pltpu.VMEM((4, block, block), f32),
                pltpu.VMEM((window, per_block * lanes), f32),
            ],
        ),
        out_shape=jax.ShapeDtypeStruct((sections, count + out_blocks, rows, lanes), bf16),
        compiler_params=pltpu.CompilerParams(vmem_limit_bytes=VMEM_LIMIT),
    )(offset.reshape(1), normed, dib, gated, d_all, mixed, d_rate, d_inflow)


def place_mlp(swapped, shared, quarter, hidden_part):
    layers = len(swapped)
    count, sections, rows, lanes = swapped[0].shape
    chunks = rows // quarter
    half = chunks // 2
    model = shared[0].shape[1] // (hidden_part // sections) * lanes
    down_rows = hidden_part // sections

    def columns_body(*refs):
        gate_ref, up_ref = refs[layers:]
        for l in range(layers):
            for s in range(sections):
                for ch in range(chunks):
                    target = gate_ref if ch < half else up_ref
                    at = ch % half
                    target[l, s * quarter : (s + 1) * quarter, at * lanes : (at + 1) * lanes] = refs[l][
                        0, s, ch * quarter : (ch + 1) * quarter
                    ].astype(f32)

    wide = jax.ShapeDtypeStruct((layers, sections * quarter, count * hidden_part), f32)
    gate, up = pl.pallas_call(
        columns_body,
        grid=(count,),
        out_shape=[wide, wide],
        in_specs=[pl.BlockSpec((1, sections, rows, lanes), lambda q: (q, 0, 0, 0))] * layers,
        out_specs=[pl.BlockSpec((layers, sections * quarter, hidden_part), lambda q: (0, 0, q))] * 2,
        compiler_params=pltpu.CompilerParams(vmem_limit_bytes=VMEM_LIMIT),
    )(*swapped)

    def rows_body(*refs):
        for l in range(layers):
            for ch in range(model // lanes):
                refs[layers][l, :, ch * lanes : (ch + 1) * lanes] = refs[l][
                    0, ch * down_rows : (ch + 1) * down_rows
                ].astype(f32)

    down = pl.pallas_call(
        rows_body,
        grid=(sections,),
        out_shape=jax.ShapeDtypeStruct((layers, hidden_part, model), f32),
        in_specs=[pl.BlockSpec((1,) + shared[0].shape[1:], lambda s: (s, 0, 0))] * layers,
        out_specs=pl.BlockSpec((layers, down_rows, model), lambda s: (0, s, 0)),
        compiler_params=pltpu.CompilerParams(vmem_limit_bytes=VMEM_LIMIT),
    )(*shared)
    return gate, up, down


def place_rec(swapped, shared, quarter, own_width):
    layers = len(swapped)
    count, sections, _, lanes = swapped[0].shape
    chunks = 2 * own_width // lanes
    out_rows = own_width // sections
    padded = out_rows + 16
    model = shared[0].shape[1] // padded * lanes

    def body(*refs):
        in_ref, side_ref, out_ref = refs[2 * layers :]
        for l in range(layers):

            @pl.when(pl.program_id(0) == l)
            def _(l=l):
                for q in range(count):
                    for s in range(sections):
                        rows = slice(s * quarter, (s + 1) * quarter)
                        for ch in range(chunks):
                            value = refs[l][q, s, ch * quarter : (ch + 1) * quarter].astype(f32)
                            first, last = ch * lanes, (ch + 1) * lanes
                            base = q * own_width
                            if first < own_width:
                                end = min(last, own_width)
                                in_ref[0, rows, base + first : base + end] = value[:, : end - first]
                            if last > own_width:
                                begin = max(first, own_width)
                                side_ref[0, rows, base + begin - own_width : base + last - own_width] = value[
                                    :, begin - first :
                                ]
                for s in range(sections):
                    for ch in range(model // lanes):
                        out_ref[0, s * out_rows : (s + 1) * out_rows, ch * lanes : (ch + 1) * lanes] = refs[
                            layers + l
                        ][s, ch * padded : ch * padded + out_rows].astype(f32)

    wide = jax.ShapeDtypeStruct((layers, sections * quarter, count * own_width), f32)
    arrays = list(swapped) + list(shared)
    return pl.pallas_call(
        body,
        grid=(layers,),
        out_shape=[wide, wide, jax.ShapeDtypeStruct((layers, own_width, model), f32)],
        in_specs=[pl.BlockSpec(a.shape, lambda l, n=a.ndim: (0,) * n) for a in arrays],
        out_specs=[
            pl.BlockSpec((1, sections * quarter, count * own_width), lambda l: (l, 0, 0)),
            pl.BlockSpec((1, sections * quarter, count * own_width), lambda l: (l, 0, 0)),
            pl.BlockSpec((1, own_width, model), lambda l: (l, 0, 0)),
        ],
        compiler_params=pltpu.CompilerParams(vmem_limit_bytes=VMEM_LIMIT),
    )(*arrays)


def stream_marks(starts, tokens):
    places = jnp.arange(tokens + 3, dtype=jnp.int32)

    def resets(p):
        return jnp.any(p[:, None] == starts[None, :], axis=1).astype(f32)

    first = 1.0 - resets(places)
    second = first * (1.0 - resets(places - 1))
    third = second * (1.0 - resets(places - 2))
    inside = (places < tokens).astype(f32)
    columns = [resets(places)[:tokens], first[:tokens], second[:tokens], third[:tokens]]
    for k, keep in ((1, first), (2, second), (3, third)):
        columns.append((keep * inside)[k : k + tokens])
    columns.append(jnp.zeros((tokens,), f32))
    return jnp.stack(columns, axis=1)


def on_device(
    inputs,
    doc_starts,
    valid_mask,
    cotangent,
    prev_state,
    prev_inputs,
    rec_gain,
    in_weight,
    side_weight,
    out_weight,
    rate_blocks,
    inflow_blocks,
    rate_bias,
    inflow_bias,
    conv_taps,
    conv_bias,
    lru_param,
    mlp_gain,
    gate_weight,
    up_weight,
    down_weight,
):
    sections = lax.axis_size("section")
    section = lax.axis_index("section")
    count = lax.axis_size("seq")
    place = lax.axis_index("seq")
    layers, d_rows, lru_width = in_weight.shape
    model = inputs.shape[2]
    tokens = inputs.shape[1] * count
    hidden_part = down_weight.shape[1]
    own_width = out_weight.shape[1]
    block_count, block_rows, block_width = rate_blocks.shape[1:]
    window = 2 * block_width
    quarter = d_rows // sections
    block_quarter = block_rows // sections
    first_block = [min(q * own_width // block_width, block_count - 2) for q in range(count)]
    owner = [min(q for q in range(count) if first_block[q] <= b <= first_block[q] + 1) for b in range(block_count)]
    block_start = jnp.asarray(first_block, jnp.int32)[place]
    offset = place * own_width - block_start * block_width
    window_start = block_start * block_width
    next_id = iter(range(64))

    def window_of(a, axis):
        return lax.dynamic_slice_in_dim(a, window_start, window, axis)

    x0 = lax.dynamic_index_in_dim(inputs, section, 0, False)
    cot = lax.dynamic_index_in_dim(cotangent, section, 0, False)
    valid = lax.dynamic_index_in_dim(valid_mask, section, 0, False)

    gate_blocks = jnp.stack([rate_blocks, inflow_blocks])

    def block_of(target):
        block = target * own_width // block_width
        return block - block // (block_count - 1)

    def rows_here():
        return pl.ds(pl.multiple_of(lax.axis_index("section") * quarter, quarter), quarter)

    def natural(out, source, s):
        return out.at[source, s]

    def by_piece(out, source, s):
        return out.at[s, source]

    wide_shape = (quarter, 2 * window)
    gates_shape = (block_rows, block_width)
    both_shape = (quarter, 2 * hidden_part)

    def wide_pieces(l):
        def cut(refs, target):
            lanes = pl.ds(pl.multiple_of(block_of(target) * block_width, block_width), window)
            return [ref.at[l, rows_here(), lanes] for ref in refs]

        def fill(view):
            return [view.at[:, pl.ds(i * window, window)] for i in range(2)]

        return cut, fill

    def gate_pieces(l):
        def cut(refs, target):
            s = lax.axis_index("section")
            return [refs[0].at[s // 2, l, block_of(target) + s % 2]]

        return cut, lambda view: [view]

    def line_rec(l):
        return [
            Line([in_weight, side_weight], (count,) + wide_shape, 2, *wide_pieces(l)),
            Line([gate_blocks], (count,) + gates_shape, 1, *gate_pieces(l)),
        ]

    def plane_rec(wide, gates):
        return [
            Plane(wide, (count, sections) + wide_shape, natural, lambda out, s: out.at[:, s]),
            Plane(gates, (sections, count) + gates_shape, by_piece, lambda out, s: out.at[s]),
        ]

    def spread_rec(l):
        return [
            Spread([in_weight, side_weight], (count, sections) + wide_shape, 2, *wide_pieces(l), natural),
            Spread([gate_blocks], (sections, count) + gates_shape, 1, *gate_pieces(l), by_piece),
        ]

    def line_mlp(l):
        if hidden_part % 128:
            pair = [
                lax.dynamic_slice_in_dim(a[l], section * quarter, quarter, 0).reshape(quarter, count, hidden_part)
                for a in (gate_weight, up_weight)
            ]
            packed = jnp.transpose(jnp.concatenate(pair, axis=2), (1, 0, 2))
            return [
                Line(
                    [packed],
                    (count,) + both_shape,
                    1,
                    lambda refs, target: [refs[0].at[target]],
                    lambda view: [view],
                )
            ]

        def cut(refs, target):
            lanes = pl.ds(pl.multiple_of(target * hidden_part, hidden_part), hidden_part)
            return [ref.at[l, rows_here(), lanes] for ref in refs]

        def fill(view):
            return [view.at[:, pl.ds(i * hidden_part, hidden_part)] for i in range(2)]

        return [Line([gate_weight, up_weight], (count,) + both_shape, 2, cut, fill)]

    def plane_mlp(both):
        return [Plane(both, (count, sections) + both_shape, natural, lambda out, s: out.at[:, s])]

    def unpack_rec(wide, gates):
        return wide.reshape(model, 2 * window), gates.reshape(2, 2, block_width, block_width)

    reach = window - own_width

    def out_window(strip, l):
        strip = jnp.concatenate([strip[0], out_weight[l], strip[1]], axis=0)
        return lax.dynamic_slice_in_dim(strip, reach - offset, window, 0)

    packed = jnp.concatenate(
        [rate_bias[:, None], inflow_bias[:, None], conv_taps, conv_bias[:, None], lru_param[:, None]], axis=1
    )
    gains_own = jnp.stack([rec_gain, mlp_gain], axis=1)
    flat = jnp.concatenate([packed.reshape(-1), gains_own.reshape(-1)]).reshape(16, -1)
    jobs = [Everyone(flat, count)] + spread_rec(0) + line_mlp(0)
    x_all, flat, *rec_got, mlp_line = comm("start", next(next_id), x=x0, jobs=jobs)
    flat = flat.reshape(count, -1)
    small_all = flat[:, : packed.size].reshape(count, layers, 8, own_width)
    small_all = jnp.transpose(small_all, (1, 2, 0, 3)).reshape(layers, 8, lru_width)
    gains = flat[:, packed.size :].reshape(count, layers, 2, d_rows)
    gains = jnp.transpose(gains, (1, 2, 0, 3)).reshape(layers, 2, model)
    small = window_of(small_all, 2).astype(f32)
    x_wide = x_all.astype(f32)
    scale = lax.rsqrt(jnp.mean(x_wide * x_wide, axis=-1, keepdims=True) + epsilon)
    normed = (x_wide * scale * gains[0, 0].astype(f32)).astype(bf16)

    masked = (cot.astype(f32) * valid[:, None].astype(f32)).astype(bf16)
    marks = stream_marks(lax.dynamic_index_in_dim(doc_starts, section, 0, False), tokens)
    first_state = window_of(lax.dynamic_index_in_dim(prev_state, section, 0, False), 1).astype(f32)
    first_state = jnp.broadcast_to(first_state[:, None], (layers, 8, window))
    rim = window_of(lax.dynamic_index_in_dim(prev_inputs, section, 0, False), 2).astype(f32)
    rim = jnp.concatenate([jnp.zeros((layers, 5, window), f32), rim], axis=1)
    channel = jnp.arange(window, dtype=jnp.int32)
    own = jnp.logical_and(channel >= offset, channel < offset + own_width).astype(f32)
    own = jnp.broadcast_to(own[None], (8, window))
    own_out = [
        lax.dynamic_update_slice(jnp.zeros((window, model), bf16), out_weight[l], (offset, 0)) for l in range(layers)
    ]

    x = x0
    kept = []
    rec_weights, mlp_weights = [], []
    for l in range(layers):
        wide_weight, gates = unpack_rec(*rec_got)
        rec_weights.append((wide_weight, gates))
        wide = dot(normed, wide_weight)
        gated, *saved = middle_forward(wide, marks, gates, small[l], rim[l], first_state[l])
        part = dot(gated, own_out[l]).astype(bf16)
        kept.append((x, normed, wide, gated, saved))
        jobs = plane_mlp(mlp_line)
        if l + 1 < layers:
            jobs += line_rec(l + 1)
        else:
            jobs += [Beside(out_weight, m, reach) for m in range(layers)]
        normed, x, both, *rec_line = comm("forward", next(next_id), part, x, gain=gains[l, 1], jobs=jobs)
        mlp_weights.append(both.reshape(model, 2 * hidden_part))
        if l == 0:
            masked_all = lax.all_gather(lax.optimization_barrier((masked, x))[0], "seq", axis=0, tiled=True)
        both = dot(normed, mlp_weights[l])
        hidden = (jax.nn.gelu(both[:, :hidden_part]) * both[:, hidden_part:]).astype(bf16)
        part = dot(hidden, down_weight[l]).astype(bf16)
        kept.append((x, normed, both, hidden))
        if l + 1 < layers:
            jobs = plane_rec(*rec_line) + line_mlp(l + 1)
            normed, x, *rec_got, mlp_line = comm("forward", next(next_id), part, x, gain=gains[l + 1, 0], jobs=jobs)
        else:
            last_part, last_x = part, x

    strips = rec_line

    mlp_lanes = np.gcd(256, hidden_part).item()
    rec_lanes = np.gcd(128, 2 * own_width).item()

    def by_target(grad, lanes):
        chunks = grad.shape[1] // lanes
        grad = grad.astype(bf16).reshape(count, sections, quarter, chunks, lanes)
        return jnp.transpose(grad, (1, 0, 3, 2, 4)).reshape(sections, count, chunks * quarter, lanes)

    def by_section(grad, lanes):
        rows, chunks = grad.shape[0] // sections, grad.shape[1] // lanes
        grad = grad.astype(bf16).reshape(sections, rows, chunks, lanes)
        return jnp.transpose(grad, (0, 2, 1, 3)).reshape(sections, chunks * rows, lanes)

    def gates_by_target(grad, lanes):
        chunks = block_width // lanes
        grad = grad.astype(bf16).reshape(2, 2, count, sections, block_quarter, chunks, lanes)
        return jnp.transpose(grad, (3, 2, 0, 1, 5, 4, 6)).reshape(sections, count, -1, lanes)

    direct = hidden_part % 256 == 0 and rec_lanes == 128 and own_width % 64 == 0

    def bundle(swapped, shared):
        lanes = swapped.shape[3]
        return jnp.concatenate([swapped.reshape(sections, -1, lanes), shared], axis=1)

    def scatter(whole):
        return lax.psum_scatter(
            whole.reshape(-1, whole.shape[-1]), "section", scatter_dimension=0, tiled=True
        )

    rows_of = {
        "mlp": 2 * hidden_part // mlp_lanes * quarter,
        "rec": (2 * own_width * quarter + 4 * block_width * block_quarter) // rec_lanes,
    }

    def grad_jobs(mine, rows):
        def cut(refs, target):
            return [refs[0].at[pl.ds(pl.multiple_of(target * rows, 8), rows)]]

        return [
            Spread(
                [mine],
                (count, sections, rows, mine.shape[1]),
                1,
                cut,
                lambda view: [view],
                lambda out, source, s: out.at[source, s],
            ),
            Share(mine, count * rows, mine.shape[0] - count * rows),
        ]

    d_rows_own, d_all = masked, masked_all
    dgains = [[None, None] for _ in range(layers)]
    waiting, spread, sums_own = {}, {}, [None] * layers
    for l in reversed(range(layers)):
        x, normed, both, hidden = kept[2 * l + 1]
        d_hidden = dot_t(d_all, down_weight[l])
        gate, slope = gelu_pair(both[:, :hidden_part])
        d_gate = (d_hidden * both[:, hidden_part:] * slope).astype(bf16)
        d_up = (d_hidden * gate).astype(bf16)
        d_both = jnp.concatenate([d_gate, d_up], axis=1)
        part = dot_t(d_both, mlp_weights[l]).astype(bf16)
        if direct:
            whole = grads_mlp(normed, d_both, hidden, d_all, sections, count, mlp_lanes)
        else:
            down = by_section(dot_rows(hidden, d_all), mlp_lanes)
            whole = bundle(by_target(dot_rows(normed, d_both), mlp_lanes), down)
        part, whole = lax.optimization_barrier((part, whole))
        waiting["mlp", l] = scatter(whole)
        if l + 1 < layers:
            part, waiting["rec", l + 1] = lax.optimization_barrier((part, waiting["rec", l + 1]))
        d_all, d_rows_own, dgains[l][1] = comm("back", next(next_id), part, x, d_rows_own, gains[l, 1])

        x, normed, wide, gated, saved = kept[2 * l]
        wide_weight, gates = rec_weights[l]
        d_gated = dot_t(d_all, out_window(strips[l], l))
        dib, d_rate, d_inflow, sums = middle_backward(
            d_gated, wide, saved, marks, gates, small[l], rim[l], own
        )
        part = dot_t(dib, wide_weight).astype(bf16)
        if direct:
            whole = grads_rec(
                normed, dib, gated, d_all, saved[0], d_rate, d_inflow, offset, own_width, sections, count, rec_lanes
            )
        else:
            grad_out = lax.dynamic_slice_in_dim(dot_rows(gated, d_all), offset, own_width, 0)
            grad_wide = dot_rows(normed, dib)
            swapped = by_target(
                jnp.concatenate(
                    [
                        lax.dynamic_slice_in_dim(grad_wide, offset, own_width, 1),
                        lax.dynamic_slice_in_dim(grad_wide, offset + window, own_width, 1),
                    ],
                    axis=1,
                ),
                rec_lanes,
            )
            low = saved[0].astype(bf16).reshape(tokens, 2, block_width)
            d_gates = jnp.stack([d_rate, d_inflow]).reshape(2, tokens, 2, block_width)
            grad_gates = jnp.einsum("tbi,gtbj->gbij", low, d_gates, preferred_element_type=f32)
            swapped = jnp.concatenate([swapped, gates_by_target(grad_gates, rec_lanes)], axis=2)
            whole = bundle(swapped, by_section(grad_out, rec_lanes))
        sums_own[l] = lax.dynamic_slice_in_dim(sums, offset, own_width, 1)
        part, whole = lax.optimization_barrier((part, whole))
        waiting["rec", l] = scatter(whole)
        part, waiting["mlp", l] = lax.optimization_barrier((part, waiting["mlp", l]))
        if l > 0:
            d_all, d_rows_own, dgains[l][0] = comm("back", next(next_id), part, x, d_rows_own, gains[l, 0])
            continue
        names = [(kind, m) for m in range(1, layers) for kind in ("mlp", "rec")]
        jobs = [job for name in names for job in grad_jobs(waiting[name], rows_of[name[0]])]
        input_grad, dgains[l][0], *got = comm("last", next(next_id), part, x, d_rows_own, gains[l, 0], jobs)
        for i, name in enumerate(names):
            spread[name] = got[2 * i : 2 * i + 2]

    sums_lanes = -(-own_width // 256) * 256
    sums = jnp.pad(jnp.concatenate(sums_own, axis=0), ((0, 0), (0, sums_lanes - own_width)))
    sums = sums.reshape(-1, 256)
    dgain_all = jnp.concatenate([a for pair in dgains for a in pair], axis=0).reshape(2 * layers, count, d_rows)
    dgain_all = jnp.pad(jnp.transpose(dgain_all, (1, 0, 2)), ((0, 0), (0, 8 - 2 * layers), (0, 256 - d_rows)))
    tiny = jnp.concatenate([dgain_all.reshape(-1, 256), sums], axis=0)
    last_part, last_x, _ = lax.optimization_barrier((last_part, last_x, input_grad))
    jobs = [job for kind in ("mlp", "rec") for job in grad_jobs(waiting[kind, 0], rows_of[kind])]
    outputs, *got, dgain_all, sums = comm(
        "rows", next(next_id), last_part, last_x, jobs=jobs + grad_jobs(tiny, 8)
    )
    spread["mlp", 0], spread["rec", 0] = got[:2], got[2:]
    sums = jnp.sum(sums, axis=0).reshape(layers, 8, sums_lanes)[:, :, :own_width]
    dgain_all = jnp.sum(dgain_all, axis=(0, 1))[: 2 * layers, :d_rows].reshape(layers, 2, d_rows)

    def both_layers(name):
        return [spread[name, l][0] for l in range(layers)], [spread[name, l][1] for l in range(layers)]

    def columns(parts, first, last, lanes):
        out = []
        for p in parts:
            chunks = p.shape[2] // quarter
            p = p[:, :, : chunks * quarter].reshape(count, sections, chunks, quarter, lanes)
            p = jnp.transpose(p, (1, 3, 0, 2, 4)).reshape(d_rows, count, chunks * lanes)
            out.append(p[:, :, first:last].reshape(d_rows, -1).astype(f32))
        return jnp.stack(out)

    def rows(parts, size, lanes):
        out = []
        for p in parts:
            p = jnp.transpose(p.reshape(sections, -1, size, lanes), (0, 2, 1, 3))
            out.append(p.reshape(sections * size, -1).astype(f32))
        return jnp.stack(out)

    mlp_swapped, mlp_shared = both_layers("mlp")
    rec_swapped, rec_shared = both_layers("rec")
    if direct:
        gate_grad, up_grad, down_grad = place_mlp(mlp_swapped, mlp_shared, quarter, hidden_part)
        in_grad, side_grad, out_grad = place_rec(rec_swapped, rec_shared, quarter, own_width)
    else:
        gate_grad = columns(mlp_swapped, 0, hidden_part, mlp_lanes)
        up_grad = columns(mlp_swapped, hidden_part, 2 * hidden_part, mlp_lanes)
        down_grad = rows(mlp_shared, hidden_part // sections, mlp_lanes)
        in_grad = columns(rec_swapped, 0, own_width, rec_lanes)
        side_grad = columns(rec_swapped, own_width, 2 * own_width, rec_lanes)
        out_grad = rows(rec_shared, own_width // sections, rec_lanes)

    gate_out = []
    for l in range(layers):
        got = rec_swapped[l][:, :, 2 * own_width // rec_lanes * quarter :]
        got = got.reshape(count, sections, 2, 2, block_width // rec_lanes, block_quarter, rec_lanes)
        blocks = jnp.stack([got[owner[b], :, :, b - first_block[owner[b]]] for b in range(block_count)])
        blocks = jnp.transpose(blocks, (2, 0, 1, 4, 3, 5))
        gate_out.append(blocks.reshape(2, block_count, block_rows, block_width))
    gate_out = jnp.stack(gate_out).astype(f32)

    return (
        outputs[None],
        input_grad[None],
        dgain_all[:, 0],
        in_grad,
        side_grad,
        out_grad,
        gate_out[:, 0],
        gate_out[:, 1],
        sums[:, 0],
        sums[:, 1],
        sums[:, 2:6],
        sums[:, 6],
        sums[:, 7],
        dgain_all[:, 1],
        gate_grad,
        up_grad,
        down_grad,
    )


def solution(mesh):
    return jax.shard_map(
        on_device,
        mesh=mesh,
        in_specs=(
            P(None, "seq", None),
            P(),
            P(None, "seq"),
            P(None, "seq", None),
            P(),
            P(),
            P(None, "seq"),
            P(None, "seq", None),
            P(None, "seq", None),
            P(None, "seq", None),
            P(None, None, "seq", None),
            P(None, None, "seq", None),
            P(None, "seq"),
            P(None, "seq"),
            P(None, None, "seq"),
            P(None, "seq"),
            P(None, "seq"),
            P(None, "seq"),
            P(None, "seq", None),
            P(None, "seq", None),
            P(None, "seq", None),
        ),
        out_specs=(
            P("section", "seq", None),
            P("section", "seq", None),
            P(None, "seq"),
            P(None, "seq", None),
            P(None, "seq", None),
            P(None, "seq", None),
            P(None, None, "seq", None),
            P(None, None, "seq", None),
            P(None, "seq"),
            P(None, "seq"),
            P(None, None, "seq"),
            P(None, "seq"),
            P(None, "seq"),
            P(None, "seq"),
            P(None, "seq", None),
            P(None, "seq", None),
            P(None, "seq", None),
        ),
        check_vma=False,
    )
```

```python
from functools import partial

import jax
import jax.numpy as jnp
import numpy as np
from jax import lax
from jax.experimental import pallas as pl
from jax.experimental.pallas import tpu as pltpu
from jax.sharding import PartitionSpec as P


epsilon = 1e-06
rate_scale = 8.0
MESH = pl.DeviceIdType.MESH
VMEM_LIMIT = 60 * 1024 * 1024
f32 = jnp.float32
bf16 = jnp.bfloat16


def plane_place():
    section = lax.axis_index("section")
    column, row = section % 2, section // 2
    return section, row * 2 + 1 - column, (1 - row) * 2 + column


def dma(*shape):
    return pltpu.SemaphoreType.DMA(shape)


def along(source, target, send, receive, peer):
    return pltpu.make_async_remote_copy(
        src_ref=source,
        dst_ref=target,
        send_sem=send,
        recv_sem=receive,
        device_id={"seq": peer},
        device_id_type=MESH,
    )


class Item:
    def __init__(self, first, at, sems, slot, even):
        self.first, self.at, self.sems, self.slot, self.even = first, at, sems, slot, even
        self.section, self.side, self.up = plane_place()

    def copy(self, way, source, holder, target):
        return pltpu.make_async_remote_copy(
            src_ref=source,
            dst_ref=self.at(holder),
            send_sem=self.sems.at[way, 0, self.slot],
            recv_sem=self.sems.at[way, 1, self.slot],
            device_id={"section": target},
            device_id_type=MESH,
        )

    def start(self):
        self.to_side = self.copy(0, self.first, self.section, self.side)
        self.to_up = self.copy(1, self.first, self.section, self.up)
        self.to_side.start()
        self.to_up.start()

    def forward(self):
        self.to_side.wait_recv()
        if self.even:
            self.onward = self.copy(2, self.at(self.side), self.side, self.up)
            self.onward.start()
        self.to_up.wait_recv()
        if not self.even:
            self.onward = self.copy(2, self.at(self.up), self.up, self.side)
            self.onward.start()

    def finish(self):
        self.onward.wait()
        self.to_side.wait_send()
        self.to_up.wait_send()


class Keep:
    def __init__(self, pieces, places, stage, target, sems, out_sem):
        self.come = [pltpu.make_async_copy(a, b, sems.at[i]) for i, (a, b) in enumerate(zip(pieces, places))]
        self.go = pltpu.make_async_copy(stage, target, out_sem)
        for copy in self.come:
            copy.start()

    def land(self):
        for copy in self.come:
            copy.wait()
        self.go.start()

    def finish(self):
        self.go.wait()


class Spread:
    queued = True
    on_line, in_plane = True, True

    def __init__(self, arrays, shape, pieces, cut, fill, slot):
        self.arrays, self.pieces, self.cut, self.fill, self.slot = list(arrays), pieces, cut, fill, slot
        self.shape = jax.ShapeDtypeStruct(shape, self.arrays[0].dtype)

    def scratch(self, count):
        return [dma(2, self.pieces, count), dma(3, 2, count), pltpu.VMEM(self.shape.shape[2:], self.shape.dtype)]

    def begin(self, refs, out, sems, place, count):
        line, plane, stage = sems
        self.sends, self.items = [], []
        section = plane_place()[0]
        self.own = Keep(
            self.cut(refs, place), self.fill(stage), stage, self.slot(out, place, section), line.at[0, :, 0], line.at[1, 0, 0]
        )
        for k in range(count):
            source = (place + count - k) % count
            self.items.append(
                Item(
                    self.slot(out, source, section) if k > 0 else stage,
                    lambda s, source=source: self.slot(out, source, s),
                    plane,
                    k,
                    k % 2 == 0,
                )
            )

        for k in range(1, count):
            peer = (place + k) % count
            pieces = zip(self.cut(refs, peer), self.fill(self.slot(out, place, section)))
            self.sends.append(
                [
                    along(piece, there, line.at[0, i, k], line.at[1, i, k], peer)
                    for i, (piece, there) in enumerate(pieces)
                ]
            )

    def own_block(self):
        self.own.land()
        self.items[0].start()
        return self.items[:1]

    def arrive(self, k):
        for copy in self.sends[k - 1]:
            copy.wait_recv()
        self.items[k].start()
        return self.items[k : k + 1]

    def finish(self):
        self.own.finish()
        for item in self.items:
            item.finish()
        for group in self.sends:
            for copy in group:
                copy.wait_send()


class Line:
    queued = True
    on_line, in_plane = True, False

    def __init__(self, arrays, shape, pieces, cut, fill):
        self.arrays, self.pieces, self.cut, self.fill = list(arrays), pieces, cut, fill
        self.shape = jax.ShapeDtypeStruct(shape, self.arrays[0].dtype)

    def scratch(self, count):
        return [dma(2, self.pieces, count), pltpu.VMEM(self.shape.shape[1:], self.shape.dtype)]

    def begin(self, refs, out, sems, place, count):
        line, stage = sems
        self.sends = []
        self.own = Keep(
            self.cut(refs, place), self.fill(stage), stage, out.at[place], line.at[0, :, 0], line.at[1, 0, 0]
        )

        for k in range(1, count):
            peer = (place + k) % count
            pieces = zip(self.cut(refs, peer), self.fill(out.at[place]))
            self.sends.append(
                [
                    along(piece, there, line.at[0, i, k], line.at[1, i, k], peer)
                    for i, (piece, there) in enumerate(pieces)
                ]
            )

    def own_block(self):
        self.own.land()
        return []

    def arrive(self, k):
        for copy in self.sends[k - 1]:
            copy.wait_recv()
        return []

    def finish(self):
        self.own.finish()
        for group in self.sends:
            for copy in group:
                copy.wait_send()


class Plane:
    queued = False
    on_line, in_plane = False, True

    def __init__(self, array, shape, slot, column):
        self.arrays, self.slot, self.column = [array], slot, column
        self.shape = jax.ShapeDtypeStruct(shape, array.dtype)

    def scratch(self, count):
        return [dma(3, 2, count), dma(2), pltpu.VMEM(self.arrays[0].shape, self.shape.dtype)]

    def begin(self, refs, out, sems, place, count):
        plane, own, stage = sems
        section = plane_place()[0]
        self.items = []
        self.own = Keep([refs[0]], [stage], stage, self.column(out, section), own, own.at[1])
        for k in range(count):
            item = Item(refs[0].at[k], lambda s, k=k: self.slot(out, k, s), plane, k, k % 2 == 0)
            item.start()
            self.items.append(item)

    def own_block(self):
        self.own.land()
        return []

    def arrive(self, k):
        self.items[k - 1].forward()

    def finish(self):
        self.items[-1].forward()
        for item in self.items:
            item.finish()
        self.own.finish()


class Share:
    queued = False
    on_line, in_plane = False, True

    def __init__(self, array, start, size):
        self.arrays, self.start, self.size = [array], start, size
        self.shape = jax.ShapeDtypeStruct((4, size, array.shape[1]), array.dtype)

    def scratch(self, count):
        return [dma(3, 2, 2), dma(2), pltpu.VMEM(self.shape.shape[1:], self.shape.dtype)]

    def begin(self, refs, out, sems, place, count):
        plane, own, stage = sems
        section = plane_place()[0]
        mine = refs[0].at[pl.ds(self.start, self.size)]
        self.own = Keep([mine], [stage], stage, out.at[section], own, own.at[1])
        half = self.size // 2
        self.items = []
        for h in range(2):
            rows = pl.ds(h * half, half)
            first = refs[0].at[pl.ds(self.start + h * half, half)]
            item = Item(first, lambda s, rows=rows: out.at[s, rows], plane, h, h == 0)
            item.start()
            self.items.append(item)

    def own_block(self):
        self.own.land()
        return self.items

    def arrive(self, k):
        return []

    def finish(self):
        self.own.finish()
        for item in self.items:
            item.finish()


class Everyone:
    queued = False
    on_line, in_plane = True, False

    def __init__(self, array, count):
        self.arrays = [array]
        self.shape = jax.ShapeDtypeStruct((count,) + array.shape, array.dtype)

    def scratch(self, count):
        return [dma(2, count)]

    def begin(self, refs, out, sems, place, count):
        self.own = pltpu.make_async_copy(refs[0], out.at[place], sems[0].at[0, 0])
        self.own.start()
        self.sends = []
        for k in range(1, count):
            copy = along(refs[0], out.at[place], sems[0].at[0, k], sems[0].at[1, k], (place + k) % count)
            copy.start()
            self.sends.append(copy)

    def own_block(self):
        self.own.wait()
        return []

    def arrive(self, k):
        pass

    def finish(self):
        for copy in self.sends:
            copy.wait()


class Beside:
    queued = False
    on_line, in_plane = True, False

    def __init__(self, array, layer, reach):
        self.arrays, self.layer, self.reach = [array], layer, reach
        self.rows = array.shape[1]
        self.shape = jax.ShapeDtypeStruct((2, reach, array.shape[2]), array.dtype)
        self.sizes = [min(self.rows, reach - at) for at in range(0, reach, self.rows)]

    def scratch(self, count):
        return [dma(2, 2, len(self.sizes) + 1)]

    def begin(self, refs, out, sems, place, count):
        mine, sem = refs[0].at[self.layer], sems[0]
        self.ends = []
        done = 0
        for k, size in enumerate(self.sizes, 1):
            ahead = along(
                mine.at[pl.ds(self.rows - size, size)],
                out.at[0, pl.ds(self.reach - done - size, size)],
                sem.at[0, 0, k],
                sem.at[0, 1, k],
                place + k,
            )
            back = along(
                mine.at[pl.ds(0, size)],
                out.at[1, pl.ds(done, size)],
                sem.at[1, 0, k],
                sem.at[1, 1, k],
                place - k,
            )
            pl.when(place + k < count)(ahead.start)
            pl.when(place >= k)(back.start)
            self.ends.append((k, ahead, back))
            done += size
        self.place, self.count = place, count

    def own_block(self):
        return []

    def arrive(self, k):
        pass

    def finish(self):
        for k, ahead, back in self.ends:
            pl.when(self.place >= k)(ahead.wait_recv)
            pl.when(self.place + k < self.count)(back.wait_recv)
            pl.when(self.place + k < self.count)(ahead.wait_send)
            pl.when(self.place >= k)(back.wait_send)


def comm_body(mode, count, jobs, groups, window, refs):
    chips = count // 2
    has_sum = mode in ("forward", "back", "last", "rows")
    has_gather = mode in ("start", "forward", "back")
    backward = mode in ("back", "last")
    refs = list(refs)
    take = refs.pop
    part_ref = take(0) if has_sum else None
    x_ref = take(0) if mode != "none" else None
    dy_ref = take(0) if backward else None
    gain_ref = take(0) if mode in ("forward", "back", "last") else None
    job_refs = [[take(0) for _ in job.arrays] for job in jobs]
    out_ref = take(0) if has_gather else None
    rows_ref = take(0) if has_sum else None
    dgain_ref = take(0) if backward else None
    job_outs = [take(0) for _ in jobs]
    if has_sum:
        pair_ref, staged_ref, landed_ref, pair_sem, sum_sem = (take(0) for _ in range(5))
    if has_gather:
        hop_sem, mate_sem = (take(0) for _ in range(2))
    job_sems = [[take(0) for _ in job.scratch(count)] for job in jobs]

    place = lax.axis_index("seq")
    chip, core = place // 2, place % 2
    mate = chip * 2 + 1 - core
    section, side, up = plane_place()

    barrier = pltpu.get_barrier_semaphore()
    met = 0
    line = []
    if any(job.on_line for job in jobs):
        line = [(place + k) % count for k in range(1, count)]
    elif mode != "none":
        line = [mate] + [((chip + k) % chips) * 2 + core for k in range(1, chips)]
    for peer in line:
        pl.semaphore_signal(barrier, inc=1, device_id={"seq": peer}, device_id_type=MESH)
        met += 1
    if any(job.in_plane for job in jobs):
        for peer in (side, up):
            pl.semaphore_signal(barrier, inc=1, device_id={"section": peer}, device_id_type=MESH)
            met += 1
    pl.semaphore_wait(barrier, met)

    def origin(way, k):
        return chip - k if way == 0 else chip + k

    def comes(way, k):
        return chip >= k if way == 0 else chip + k < chips

    def goes_on(way):
        return chip + 1 < chips if way == 0 else chip >= 1

    def hop(way, k):
        slot = origin(way, k) * 2 + core
        onward = chip + 1 if way == 0 else chip - 1
        return along(
            out_ref.at[slot], out_ref.at[slot], hop_sem.at[way, 0, k], hop_sem.at[way, 1, k + 1], onward * 2 + core
        )

    def landing(way, k):
        slot = origin(way, k) * 2 + core
        return along(out_ref.at[slot], out_ref.at[slot], hop_sem.at[way, 0, k], hop_sem.at[way, 1, k], mate)

    def across(way, k):
        slot = origin(way, k) * 2 + core
        return along(out_ref.at[slot], out_ref.at[slot], mate_sem.at[way, 0, k], mate_sem.at[way, 1, k], mate)

    def begin_gather(rows):
        out_ref[place] = rows
        for way in range(2):
            pl.when(goes_on(way))(hop(way, 0).start)
        across(0, 0).start()

    def land(k):
        for way in range(2):

            @pl.when(comes(way, k))
            def _(way=way, k=k):
                landing(way, k).wait_recv()
                pl.when(goes_on(way))(hop(way, k).start)
                across(way, k).start()

    early = mode in ("start", "forward", "back")
    for job, ref, out, sems in zip(jobs, job_refs, job_outs, job_sems):
        job.begin(ref, out, sems, place, count)
    queue = []
    for group in groups:
        members = [job for job in jobs[group[0] : group[1]] if job.queued]
        queue += [(job, k) for k in range(1, count) for job in members]
    issued, arrived, flowing, lag = [0], [0], [], 5

    def issue(number):
        for job, k in queue[issued[0] : issued[0] + number]:
            for copy in job.sends[k - 1]:
                copy.start()
        issued[0] += number

    def tick(k):
        until = -(-len(queue) * k // (count - 1))
        for job, index in queue[arrived[0] : until]:
            flowing.extend(job.arrive(index))
            issue(1)
            if len(flowing) > lag:
                flowing.pop(0).forward()
        arrived[0] = max(arrived[0], until)
        for job in jobs:
            if not job.queued:
                job.arrive(k)

    def own_blocks():
        for job in jobs:
            flowing.extend(job.own_block())

    def send_sums():
        total = None
        copies = []
        for k, copy in pair_copies:
            to_chip = (chip + k) % chips
            copy.wait_recv()
            both = part_ref[to_chip * 2 + core].astype(f32) + pair_ref[k].astype(f32)
            if k == 0:
                total = both
            else:
                staged_ref[k] = both.astype(bf16)
                send = along(
                    staged_ref.at[k], landed_ref.at[k], sum_sem.at[0, k], sum_sem.at[1, k], to_chip * 2 + core
                )
                send.start()
                copies.append((k, send))
        return total, copies

    if has_sum:
        pair_copies = []
        for k in list(range(1, chips)) + [0]:
            to_chip = (chip + k) % chips
            copy = along(
                part_ref.at[to_chip * 2 + 1 - core], pair_ref.at[k], pair_sem.at[0, k], pair_sem.at[1, k], mate
            )
            copy.start()
            pair_copies.append((k, copy))
    if mode == "start":
        begin_gather(x_ref[...])
    if not early or mode == "start":
        issue(window)
    if has_sum:
        total, sum_copies = send_sums()
    if early and mode != "start":
        issue(window)
    own_blocks()
    if not early:
        for k in range(1, count):
            tick(k)
    if has_sum:
        for k, send in sum_copies:
            send.wait_recv()
            total = total + landed_ref[k].astype(f32)

    if mode != "none":
        x_wide = x_ref[...].astype(f32)
    if mode == "rows":
        rows_ref[...] = (x_wide + total).astype(bf16)
    elif mode == "forward":
        x_low = (x_wide + total).astype(bf16)
        rows_ref[...] = x_low
        x_wide = x_low.astype(f32)
        scale = lax.rsqrt(jnp.mean(x_wide * x_wide, axis=-1, keepdims=True) + epsilon)
        sent = (x_wide * scale * gain_ref[...]).astype(bf16)
    elif backward:
        scale = lax.rsqrt(jnp.mean(x_wide * x_wide, axis=-1, keepdims=True) + epsilon)
        scaled = total * gain_ref[...]
        inner_mean = jnp.mean(scaled * x_wide, axis=-1, keepdims=True)
        back = scale * scaled - x_wide * (scale * scale * scale * inner_mean)
        dgain_ref[...] = jnp.sum(total * x_wide * scale, axis=0, keepdims=True)
        sent = (dy_ref[...].astype(f32) + back).astype(bf16)
        rows_ref[...] = sent

    if early:
        if mode != "start":
            begin_gather(sent)
        for k in range(1, count):
            tick(k)
            if k % 2 == 0:
                land(k // 2)
    for item in flowing:
        item.forward()
    for job in jobs:
        job.finish()
    if has_gather:
        across(0, 0).wait()
        for way in range(2):
            pl.when(goes_on(way))(hop(way, 0).wait_send)
        for k in range(1, chips):
            for way in range(2):

                @pl.when(comes(way, k))
                def _(way=way, k=k):
                    across(way, k).wait()
                    pl.when(goes_on(way))(hop(way, k).wait_send)

    if has_sum:
        for _, copy in pair_copies:
            copy.wait_send()
        for _, send in sum_copies:
            send.wait_send()


def comm(mode, collective_id, part=None, x=None, dy=None, gain=None, jobs=(), groups=None, window=4, us=50):
    count = lax.axis_size("seq")
    chips = count // 2
    has_sum = mode in ("forward", "back", "last", "rows")
    has_gather = mode in ("start", "forward", "back")
    backward = mode in ("back", "last")
    in_vmem = pl.BlockSpec(memory_space=pltpu.VMEM)
    in_hbm = pl.BlockSpec(memory_space=pl.ANY)
    operands, in_specs, shapes, out_specs, scratch = [], [], [], [], []

    def give(a, spec):
        operands.append(a)
        in_specs.append(spec)

    def want(shape, spec):
        shapes.append(shape)
        out_specs.append(spec)

    if mode != "none":
        rows, width = x.shape
    if has_sum:
        give(part.reshape(count, rows, width), in_vmem)
    if mode != "none":
        give(x, in_vmem)
    if backward:
        give(dy, in_vmem)
    if mode in ("forward", "back", "last"):
        give(gain.astype(f32).reshape(1, width), in_vmem)
    for job in jobs:
        for a in job.arrays:
            give(a, in_hbm)
    if has_gather:
        want(jax.ShapeDtypeStruct((count, rows, width), bf16), in_vmem)
    if has_sum:
        want(jax.ShapeDtypeStruct((rows, width), bf16), in_vmem)
    if backward:
        want(jax.ShapeDtypeStruct((1, width), f32), in_vmem)
    for job in jobs:
        want(job.shape, in_hbm)
    if has_sum:
        scratch += [pltpu.VMEM((chips, rows, width), bf16)] * 3 + [dma(2, chips)] * 2
    if has_gather:
        scratch += [dma(2, 2, chips + 1), dma(2, 2, chips)]
    for job in jobs:
        scratch += job.scratch(count)
    outs = pl.pallas_call(
        lambda *refs: comm_body(mode, count, jobs, groups or [(0, len(jobs))], window, refs),
        out_shape=shapes,
        in_specs=in_specs,
        out_specs=out_specs,
        scratch_shapes=scratch,
        cost_estimate=pl.CostEstimate(flops=us * 1_000_000_000, bytes_accessed=1_000_000, transcendentals=0),
        compiler_params=pltpu.CompilerParams(
            collective_id=collective_id, has_side_effects=True, vmem_limit_bytes=VMEM_LIMIT
        ),
    )(*operands)
    outs = list(outs)
    if has_gather:
        outs[0] = outs[0].reshape(count * rows, width)
    return outs


def less_exp(doubled):
    small = doubled * (
        1.0
        - doubled
        * (
            0.5
            - doubled
            * (1.0 / 6 - doubled * (1.0 / 24 - doubled * (1.0 / 120 - doubled * (1.0 / 720))))
        )
    )
    return jnp.where(doubled < 0.25, small, 1.0 - jnp.exp(-doubled))


def gelu_pair(v):
    c = np.float32(np.sqrt(2 / np.pi))
    t = jnp.tanh(c * (v + 0.044715 * v * v * v))
    slope = 0.5 * (1.0 + t) + 0.5 * v * (1.0 - t * t) * c * (1.0 + 3 * 0.044715 * v * v)
    return 0.5 * v * (1.0 + t), slope


def dot(a, b):
    return jnp.dot(a, b, preferred_element_type=f32)


def dot_t(a, b):
    return lax.dot_general(a, b, (((1,), (1,)), ((), ())), preferred_element_type=f32)


def dot_rows(a, b):
    return lax.dot_general(a, b, (((0,), (0,)), ((), ())), preferred_element_type=f32)


def soft(lru):
    spread = jnp.maximum(-lru, 0.0) + jnp.log1p(jnp.exp(-jnp.abs(lru)))
    return spread, -1.0 / (1.0 + jnp.exp(lru))


def middle_forward_body(
    rows,
    width,
    is_ref,
    marks_ref,
    blocks_ref,
    small_ref,
    rim_ref,
    first_ref,
    pick_ref,
    gated_ref,
    mixed_ref,
    rate_ref,
    inflow_ref,
    states_ref,
    before_ref,
    ext,
    decays,
    drives,
    carry,
):
    @pl.when(pl.program_id(0) == 0)
    def _():
        ext[0:8] = rim_ref[...]
        carry[...] = first_ref[...]

    block = width // 2
    inner = is_ref[:, :width].astype(bf16).astype(f32)
    ext[8 : 8 + rows] = inner
    reset = marks_ref[:, 0:1]
    mixed = (
        small_ref[6:7]
        + small_ref[2:3] * inner
        + small_ref[3:4] * (ext[7 : 7 + rows] * marks_ref[:, 1:2])
        + small_ref[4:5] * (ext[6 : 6 + rows] * marks_ref[:, 2:3])
        + small_ref[5:6] * (ext[5 : 5 + rows] * marks_ref[:, 3:4])
    )
    ext[0:8] = ext[rows : rows + 8]
    mixed_ref[...] = mixed
    low = mixed.astype(bf16)
    for b in range(2):
        lanes = slice(b * block, (b + 1) * block)
        rate_ref[:, lanes] = dot(low[:, lanes], blocks_ref[0, b]) + small_ref[0:1, lanes]
        inflow_ref[:, lanes] = dot(low[:, lanes], blocks_ref[1, b]) + small_ref[1:2, lanes]
    spread, _ = soft(small_ref[7:8])
    log_decay = (-rate_scale * spread) * jax.nn.sigmoid(rate_ref[...])
    kept = 1.0 - reset
    decays[...] = jnp.exp(log_decay) * kept
    factor = reset + kept * jnp.sqrt(less_exp(-2.0 * log_decay))
    drives[...] = factor * jax.nn.sigmoid(inflow_ref[...]) * mixed

    place = lax.broadcasted_iota(jnp.int32, (8, width), 0)

    def step(j, last):
        at = pl.ds(pl.multiple_of(j * 8, 8), 8)
        a, h = decays[at], drives[at]
        for k in (1, 2, 4):
            inside = place >= k
            h = jnp.where(inside, a * pltpu.roll(h, k, 0) + h, h)
            a = jnp.where(inside, a * pltpu.roll(a, k, 0), a)
        h = h + a * last
        states_ref[at] = h
        before_ref[at] = jnp.where(place >= 1, pltpu.roll(h, 1, 0), last)
        return jnp.broadcast_to(h[7:8], (8, width))

    carry[...] = lax.fori_loop(0, rows // 8, step, carry[...])
    gated = (states_ref[...] * gelu_pair(is_ref[:, width:])[0]).astype(bf16)
    gated_ref[...] = dot(gated, pick_ref[...]).astype(bf16)


def middle_backward_body(
    rows,
    width,
    dg_ref,
    is_ref,
    mixed_ref,
    rate_ref,
    inflow_ref,
    states_ref,
    before_ref,
    marks_ref,
    blocks_ref,
    small_ref,
    rim_ref,
    own_ref,
    dib_ref,
    drate_ref,
    dinflow_ref,
    sums_ref,
    dm_ext,
    decays,
    dstates,
    carry,
):
    @pl.when(pl.program_id(0) == 0)
    def _():
        dm_ext[rows : rows + 8] = jnp.zeros((8, width), f32)
        carry[...] = jnp.zeros((8, width), f32)
        sums_ref[...] = jnp.zeros_like(sums_ref)

    block = width // 2
    own = own_ref[0:1]
    reset = marks_ref[:, 0:1]
    kept = 1.0 - reset
    side, slope = gelu_pair(is_ref[:, width:])
    d_gated = dg_ref[...]
    dib_ref[:, width:] = (d_gated * states_ref[...] * slope * own).astype(bf16)
    dstates[...] = d_gated * side
    spread, spread_slope = soft(small_ref[7:8])
    rate = jax.nn.sigmoid(rate_ref[...])
    log_decay = (-rate_scale * spread) * rate
    decays[...] = jnp.exp(log_decay) * kept

    place = lax.broadcasted_iota(jnp.int32, (8, width), 0)

    def step(j, after):
        at = pl.ds(pl.multiple_of(rows - 8 - j * 8, 8), 8)
        own_decay, h = decays[at], dstates[at]
        a = jnp.where(place < 7, pltpu.roll(own_decay, 7, 0), 1.0)
        for k in (1, 2, 4):
            inside = place < 8 - k
            h = jnp.where(inside, a * pltpu.roll(h, 8 - k, 0) + h, h)
            a = jnp.where(inside, a * pltpu.roll(a, 8 - k, 0), a)
        h = h + a * after
        dstates[at] = h
        return jnp.broadcast_to((own_decay * h)[0:1], (8, width))

    carry[...] = lax.fori_loop(0, rows // 8, step, carry[...])

    d_h = dstates[...]
    mixed = mixed_ref[...]
    inflow = jax.nn.sigmoid(inflow_ref[...])
    root = jnp.sqrt(less_exp(-2.0 * log_decay))
    factor = reset + kept * root
    decay = decays[...]
    twice = jnp.exp(2.0 * log_decay)
    d_log = d_h * before_ref[...] * decay - d_h * inflow * mixed * kept * (twice / root)
    d_lru = jnp.sum(d_log * rate, axis=0, keepdims=True) * (-rate_scale * spread_slope)
    d_rate = (d_log * (-rate_scale * spread) * rate * (1.0 - rate)).astype(bf16)
    through = d_h * factor
    d_inflow = (through * mixed * inflow * (1.0 - inflow)).astype(bf16)
    drate_ref[...] = d_rate
    dinflow_ref[...] = d_inflow
    for b in range(2):
        lanes = slice(b * block, (b + 1) * block)
        dm_ext[0:rows, lanes] = (
            ((through * inflow)[:, lanes] + dot_t(d_rate[:, lanes], blocks_ref[0, b]) + dot_t(d_inflow[:, lanes], blocks_ref[1, b]))
            .astype(bf16)
            .astype(f32)
        )
    d_mixed = dm_ext[0:rows]
    inner = is_ref[:, :width].astype(bf16).astype(f32)
    shifted = [d_mixed] + [dm_ext[k : k + rows] * marks_ref[:, 3 + k : 4 + k] for k in (1, 2, 3)]
    d_inner = small_ref[2:3] * shifted[0]
    for k in (1, 2, 3):
        d_inner = d_inner + small_ref[2 + k : 3 + k] * shifted[k]
    dib_ref[:, :width] = (d_inner * own).astype(bf16)

    def add(row, value):
        sums_ref[row : row + 1] += value

    add(0, jnp.sum(d_rate.astype(f32), axis=0, keepdims=True))
    add(1, jnp.sum(d_inflow.astype(f32), axis=0, keepdims=True))
    for k in range(4):
        add(2 + k, jnp.sum(shifted[k] * inner, axis=0, keepdims=True))
    add(6, jnp.sum(d_mixed, axis=0, keepdims=True))
    add(7, d_lru)

    @pl.when(pl.program_id(0) == pl.num_programs(0) - 1)
    def _():
        for k in (1, 2, 3):
            for t in range(k):
                add(2 + k, dm_ext[t : t + 1] * marks_ref[t : t + 1, k : k + 1] * rim_ref[8 + t - k : 9 + t - k])

    dm_ext[rows : rows + 8] = dm_ext[0:8]


def row_spec(rows, width, steps, reverse):
    if reverse:
        return pl.BlockSpec((rows, width), lambda i: (steps - 1 - i, 0))
    return pl.BlockSpec((rows, width), lambda i: (i, 0))


def whole_spec(shape):
    return pl.BlockSpec(shape, lambda i: (0,) * len(shape))


def middle_forward(wide, marks, blocks, small, rim, first, pick):
    tokens, width = wide.shape[0], wide.shape[1] // 2
    rows = min(256, tokens)
    steps = tokens // rows
    here = partial(row_spec, rows, steps=steps, reverse=False)
    whole = [blocks, small, rim, first, pick]
    own_width = pick.shape[1]
    return pl.pallas_call(
        partial(middle_forward_body, rows, width),
        grid=(steps,),
        out_shape=[jax.ShapeDtypeStruct((tokens, own_width), bf16)] + [jax.ShapeDtypeStruct((tokens, width), f32)] * 5,
        in_specs=[here(2 * width), here(8)] + [whole_spec(a.shape) for a in whole],
        out_specs=[here(own_width)] + [here(width)] * 5,
        scratch_shapes=[
            pltpu.VMEM((rows + 8, width), f32),
            pltpu.VMEM((rows, width), f32),
            pltpu.VMEM((rows, width), f32),
            pltpu.VMEM((8, width), f32),
        ],
        compiler_params=pltpu.CompilerParams(vmem_limit_bytes=VMEM_LIMIT),
    )(wide, marks, *whole)


def middle_backward(d_gated, wide, saved, marks, blocks, small, rim, own):
    tokens, width = d_gated.shape
    rows = min(256, tokens)
    steps = tokens // rows
    here = partial(row_spec, rows, steps=steps, reverse=True)
    whole = [blocks, small, rim, own]
    return pl.pallas_call(
        partial(middle_backward_body, rows, width),
        grid=(steps,),
        out_shape=[
            jax.ShapeDtypeStruct((tokens, 2 * width), bf16),
            jax.ShapeDtypeStruct((tokens, width), bf16),
            jax.ShapeDtypeStruct((tokens, width), bf16),
            jax.ShapeDtypeStruct((8, width), f32),
        ],
        in_specs=[here(width), here(2 * width)] + [here(width)] * 5 + [here(8)] + [whole_spec(a.shape) for a in whole],
        out_specs=[here(2 * width), here(width), here(width), whole_spec((8, width))],
        scratch_shapes=[
            pltpu.VMEM((rows + 8, width), f32),
            pltpu.VMEM((rows, width), f32),
            pltpu.VMEM((rows, width), f32),
            pltpu.VMEM((8, width), f32),
        ],
        compiler_params=pltpu.CompilerParams(vmem_limit_bytes=VMEM_LIMIT),
    )(d_gated, wide, *saved, marks, *whole)


def grads_mlp(normed, d_both, hidden, d_all, sections, count, lanes):
    tokens, model = normed.shape
    d_rows = model // count
    quarter = d_rows // sections
    chunks = d_both.shape[1] // lanes
    rows = chunks * quarter
    down_rows = hidden.shape[1] // sections
    per_block = rows // down_rows
    down_blocks = model // lanes // per_block

    def body(normed_ref, both_ref, hidden_ref, all_ref, out_ref):
        j = pl.program_id(0)

        @pl.when(j < count)
        def _():
            grad = dot_rows(normed_ref[...], both_ref[...])
            for s in range(sections):
                for ch in range(chunks):
                    out_ref[s, 0, ch * quarter : (ch + 1) * quarter] = grad[
                        s * quarter : (s + 1) * quarter, ch * lanes : (ch + 1) * lanes
                    ].astype(bf16)

        @pl.when(j >= count)
        def _():
            grad = dot_rows(hidden_ref[...], all_ref[...])
            for s in range(sections):
                for ch in range(per_block):
                    out_ref[s, 0, ch * down_rows : (ch + 1) * down_rows] = grad[
                        s * down_rows : (s + 1) * down_rows, ch * lanes : (ch + 1) * lanes
                    ].astype(bf16)

    return pl.pallas_call(
        body,
        grid=(count + down_blocks,),
        out_shape=jax.ShapeDtypeStruct((sections, count + down_blocks, rows, lanes), bf16),
        in_specs=[
            pl.BlockSpec((tokens, d_rows), lambda j: (0, jnp.minimum(j, count - 1))),
            pl.BlockSpec(d_both.shape, lambda j: (0, 0)),
            pl.BlockSpec(hidden.shape, lambda j: (0, 0)),
            pl.BlockSpec((tokens, per_block * lanes), lambda j: (0, jnp.maximum(j - count, 0))),
        ],
        out_specs=pl.BlockSpec((sections, 1, rows, lanes), lambda j: (0, j, 0, 0)),
        compiler_params=pltpu.CompilerParams(vmem_limit_bytes=VMEM_LIMIT),
    )(normed, d_both, hidden, d_all)


def grads_rec(normed, dib, gated, d_all, mixed, d_rate, d_inflow, pick, own_width, sections, count, lanes):
    tokens, model = normed.shape
    window = mixed.shape[1]
    block = window // 2
    d_rows = model // count
    quarter = d_rows // sections
    chunks = 2 * own_width // lanes
    gate_rows = block // count // sections
    gate_chunks = block // lanes
    rows = chunks * quarter + 4 * gate_chunks * gate_rows
    out_rows = own_width // sections
    padded = out_rows + 16
    per_block = rows // padded
    out_blocks = model // lanes // per_block

    def body(normed_ref, dib_ref, gated_ref, all_ref, mixed_ref, rate_ref, inflow_ref, pick_ref, out_ref, own, gates):
        j = pl.program_id(0)

        @pl.when(j == 0)
        def _():
            pick = pick_ref[...]
            own[...] = jnp.concatenate(
                [dot(dib_ref[:, :window], pick), dot(dib_ref[:, window:], pick)], axis=1
            ).astype(bf16)
            low = mixed_ref[...].astype(bf16)
            for i, ref in enumerate((rate_ref, inflow_ref)):
                for b in range(2):
                    at = slice(b * block, (b + 1) * block)
                    gates[2 * i + b] = dot_rows(low[:, at], ref[:, at])

        @pl.when(j < count)
        def _():
            grad = dot_rows(normed_ref[...], own[...])
            for s in range(sections):
                for ch in range(chunks):
                    out_ref[s, 0, ch * quarter : (ch + 1) * quarter] = grad[
                        s * quarter : (s + 1) * quarter, ch * lanes : (ch + 1) * lanes
                    ].astype(bf16)
                here = pl.ds(pl.multiple_of((j * sections + s) * gate_rows, gate_rows), gate_rows)
                pieces = [
                    gates[g, here, ch * lanes : (ch + 1) * lanes] for g in range(4) for ch in range(gate_chunks)
                ]
                out_ref[s, 0, chunks * quarter :] = jnp.concatenate(pieces, axis=0).astype(bf16)

        @pl.when(j >= count)
        def _():
            grad = dot_rows(gated_ref[...], all_ref[...])
            for s in range(sections):
                for ch in range(per_block):
                    out_ref[s, 0, ch * padded : ch * padded + out_rows] = grad[
                        s * out_rows : (s + 1) * out_rows, ch * lanes : (ch + 1) * lanes
                    ].astype(bf16)
                    out_ref[s, 0, ch * padded + out_rows : (ch + 1) * padded] = jnp.zeros((16, lanes), bf16)

    def whole(a):
        return pl.BlockSpec(a.shape, lambda j: (0,) * a.ndim)

    return pl.pallas_call(
        body,
        grid=(count + out_blocks,),
        in_specs=[
            pl.BlockSpec((tokens, d_rows), lambda j: (0, jnp.minimum(j, count - 1))),
            whole(dib),
            whole(gated),
            pl.BlockSpec((tokens, per_block * lanes), lambda j: (0, jnp.maximum(j - count, 0))),
            whole(mixed),
            whole(d_rate),
            whole(d_inflow),
            whole(pick),
        ],
        out_specs=pl.BlockSpec((sections, 1, rows, lanes), lambda j: (0, j, 0, 0)),
        scratch_shapes=[pltpu.VMEM((tokens, 2 * own_width), bf16), pltpu.VMEM((4, block, block), f32)],
        out_shape=jax.ShapeDtypeStruct((sections, count + out_blocks, rows, lanes), bf16),
        compiler_params=pltpu.CompilerParams(vmem_limit_bytes=VMEM_LIMIT),
    )(normed, dib, gated, d_all, mixed, d_rate, d_inflow, pick)


def place_mlp(swapped, shared, quarter, hidden_part):
    layers = len(swapped)
    count, sections, rows, lanes = swapped[0].shape
    chunks = rows // quarter
    half = chunks // 2
    model = shared[0].shape[1] // (hidden_part // sections) * lanes
    down_rows = hidden_part // sections

    def columns_body(*refs):
        gate_ref, up_ref = refs[layers:]
        for l in range(layers):
            for s in range(sections):
                for ch in range(chunks):
                    target = gate_ref if ch < half else up_ref
                    at = ch % half
                    target[l, s * quarter : (s + 1) * quarter, at * lanes : (at + 1) * lanes] = refs[l][
                        0, s, ch * quarter : (ch + 1) * quarter
                    ].astype(f32)

    wide = jax.ShapeDtypeStruct((layers, sections * quarter, count * hidden_part), f32)
    gate, up = pl.pallas_call(
        columns_body,
        grid=(count,),
        out_shape=[wide, wide],
        in_specs=[pl.BlockSpec((1, sections, rows, lanes), lambda q: (q, 0, 0, 0))] * layers,
        out_specs=[pl.BlockSpec((layers, sections * quarter, hidden_part), lambda q: (0, 0, q))] * 2,
        compiler_params=pltpu.CompilerParams(vmem_limit_bytes=VMEM_LIMIT),
    )(*swapped)

    def rows_body(*refs):
        for l in range(layers):
            for ch in range(model // lanes):
                refs[layers][l, :, ch * lanes : (ch + 1) * lanes] = refs[l][
                    0, ch * down_rows : (ch + 1) * down_rows
                ].astype(f32)

    down = pl.pallas_call(
        rows_body,
        grid=(sections,),
        out_shape=jax.ShapeDtypeStruct((layers, hidden_part, model), f32),
        in_specs=[pl.BlockSpec((1,) + shared[0].shape[1:], lambda s: (s, 0, 0))] * layers,
        out_specs=pl.BlockSpec((layers, down_rows, model), lambda s: (0, s, 0)),
        compiler_params=pltpu.CompilerParams(vmem_limit_bytes=VMEM_LIMIT),
    )(*shared)
    return gate, up, down


def place_rec(swapped, shared, quarter, own_width, block_width, first_block, owner):
    layers = len(swapped)
    count, sections, _, lanes = swapped[0].shape
    chunks = 2 * own_width // lanes
    out_rows = own_width // sections
    padded = out_rows + 16
    model = shared[0].shape[1] // padded * lanes

    gate_rows = block_width // count // sections
    gate_chunks = block_width // lanes

    def body(*refs):
        in_ref, side_ref, out_ref, gate_ref = refs[2 * layers :]
        for l in range(layers):

            @pl.when(pl.program_id(0) == l)
            def _(l=l):
                for q in range(count):
                    for s in range(sections):
                        rows = slice(s * quarter, (s + 1) * quarter)
                        for ch in range(chunks):
                            value = refs[l][q, s, ch * quarter : (ch + 1) * quarter].astype(f32)
                            first, last = ch * lanes, (ch + 1) * lanes
                            base = q * own_width
                            if first < own_width:
                                end = min(last, own_width)
                                in_ref[0, rows, base + first : base + end] = value[:, : end - first]
                            if last > own_width:
                                begin = max(first, own_width)
                                side_ref[0, rows, base + begin - own_width : base + last - own_width] = value[
                                    :, begin - first :
                                ]
                for b, q in enumerate(owner):
                    for s in range(sections):
                        value = refs[l][q, s, chunks * quarter :].astype(f32)
                        for g in range(2):
                            for ch in range(gate_chunks):
                                at = ((2 * g + b - first_block[q]) * gate_chunks + ch) * gate_rows
                                gate_ref[
                                    g, 0, b, s * gate_rows : (s + 1) * gate_rows, ch * lanes : (ch + 1) * lanes
                                ] = value[at : at + gate_rows]
                for s in range(sections):
                    for ch in range(model // lanes):
                        out_ref[0, s * out_rows : (s + 1) * out_rows, ch * lanes : (ch + 1) * lanes] = refs[
                            layers + l
                        ][s, ch * padded : ch * padded + out_rows].astype(f32)

    wide = jax.ShapeDtypeStruct((layers, sections * quarter, count * own_width), f32)
    arrays = list(swapped) + list(shared)
    return pl.pallas_call(
        body,
        grid=(layers,),
        out_shape=[
            wide,
            wide,
            jax.ShapeDtypeStruct((layers, own_width, model), f32),
            jax.ShapeDtypeStruct((2, layers, len(owner), gate_rows * sections, block_width), f32),
        ],
        in_specs=[pl.BlockSpec(a.shape, lambda l, n=a.ndim: (0,) * n) for a in arrays],
        out_specs=[
            pl.BlockSpec((1, sections * quarter, count * own_width), lambda l: (l, 0, 0)),
            pl.BlockSpec((1, sections * quarter, count * own_width), lambda l: (l, 0, 0)),
            pl.BlockSpec((1, own_width, model), lambda l: (l, 0, 0)),
            pl.BlockSpec((2, 1, len(owner), gate_rows * sections, block_width), lambda l: (0, l, 0, 0, 0)),
        ],
        compiler_params=pltpu.CompilerParams(vmem_limit_bytes=VMEM_LIMIT),
    )(*arrays)


def stream_marks(starts, tokens):
    places = jnp.arange(tokens + 3, dtype=jnp.int32)

    def resets(p):
        return jnp.any(p[:, None] == starts[None, :], axis=1).astype(f32)

    first = 1.0 - resets(places)
    second = first * (1.0 - resets(places - 1))
    third = second * (1.0 - resets(places - 2))
    inside = (places < tokens).astype(f32)
    columns = [resets(places)[:tokens], first[:tokens], second[:tokens], third[:tokens]]
    for k, keep in ((1, first), (2, second), (3, third)):
        columns.append((keep * inside)[k : k + tokens])
    columns.append(jnp.zeros((tokens,), f32))
    return jnp.stack(columns, axis=1)


def on_device(
    inputs,
    doc_starts,
    valid_mask,
    cotangent,
    prev_state,
    prev_inputs,
    rec_gain,
    in_weight,
    side_weight,
    out_weight,
    rate_blocks,
    inflow_blocks,
    rate_bias,
    inflow_bias,
    conv_taps,
    conv_bias,
    lru_param,
    mlp_gain,
    gate_weight,
    up_weight,
    down_weight,
):
    sections = lax.axis_size("section")
    section = lax.axis_index("section")
    count = lax.axis_size("seq")
    place = lax.axis_index("seq")
    layers, d_rows, lru_width = in_weight.shape
    model = inputs.shape[2]
    tokens = inputs.shape[1] * count
    hidden_part = down_weight.shape[1]
    own_width = out_weight.shape[1]
    block_count, block_rows, block_width = rate_blocks.shape[1:]
    window = 2 * block_width
    quarter = d_rows // sections
    block_quarter = block_rows // sections
    first_block = [min(q * own_width // block_width, block_count - 2) for q in range(count)]
    owner = [min(q for q in range(count) if first_block[q] <= b <= first_block[q] + 1) for b in range(block_count)]
    block_start = jnp.asarray(first_block, jnp.int32)[place]
    offset = place * own_width - block_start * block_width
    window_start = block_start * block_width
    next_id = iter(range(64))

    def window_of(a, axis):
        return lax.dynamic_slice_in_dim(a, window_start, window, axis)

    x0 = lax.dynamic_index_in_dim(inputs, section, 0, False)
    cot = lax.dynamic_index_in_dim(cotangent, section, 0, False)
    valid = lax.dynamic_index_in_dim(valid_mask, section, 0, False)

    gate_blocks = jnp.stack([rate_blocks, inflow_blocks])

    def block_of(target):
        block = target * own_width // block_width
        return block - block // (block_count - 1)

    def rows_here():
        return pl.ds(pl.multiple_of(lax.axis_index("section") * quarter, quarter), quarter)

    def natural(out, source, s):
        return out.at[source, s]

    def by_piece(out, source, s):
        return out.at[s, source]

    wide_shape = (quarter, 2 * window)
    gates_shape = (block_rows, block_width)
    both_shape = (quarter, 2 * hidden_part)

    def wide_pieces(l):
        def cut(refs, target):
            lanes = pl.ds(pl.multiple_of(block_of(target) * block_width, block_width), window)
            return [ref.at[l, rows_here(), lanes] for ref in refs]

        def fill(view):
            return [view.at[:, pl.ds(i * window, window)] for i in range(2)]

        return cut, fill

    def gate_pieces(l):
        def cut(refs, target):
            s = lax.axis_index("section")
            return [refs[0].at[s // 2, l, block_of(target) + s % 2]]

        return cut, lambda view: [view]

    def line_rec(l):
        return [
            Line([in_weight, side_weight], (count,) + wide_shape, 2, *wide_pieces(l)),
            Line([gate_blocks], (count,) + gates_shape, 1, *gate_pieces(l)),
        ]

    def plane_rec(wide, gates):
        return [
            Plane(wide, (count, sections) + wide_shape, natural, lambda out, s: out.at[:, s]),
            Plane(gates, (sections, count) + gates_shape, by_piece, lambda out, s: out.at[s]),
        ]

    def spread_rec(l):
        return [
            Spread([in_weight, side_weight], (count, sections) + wide_shape, 2, *wide_pieces(l), natural),
            Spread([gate_blocks], (sections, count) + gates_shape, 1, *gate_pieces(l), by_piece),
        ]

    def line_mlp(l):
        if hidden_part % 128:
            pair = [
                lax.dynamic_slice_in_dim(a[l], section * quarter, quarter, 0).reshape(quarter, count, hidden_part)
                for a in (gate_weight, up_weight)
            ]
            packed = jnp.transpose(jnp.concatenate(pair, axis=2), (1, 0, 2))
            return [
                Line(
                    [packed],
                    (count,) + both_shape,
                    1,
                    lambda refs, target: [refs[0].at[target]],
                    lambda view: [view],
                )
            ]

        def cut(refs, target):
            lanes = pl.ds(pl.multiple_of(target * hidden_part, hidden_part), hidden_part)
            return [ref.at[l, rows_here(), lanes] for ref in refs]

        def fill(view):
            return [view.at[:, pl.ds(i * hidden_part, hidden_part)] for i in range(2)]

        return [Line([gate_weight, up_weight], (count,) + both_shape, 2, cut, fill)]

    def plane_mlp(both):
        return [Plane(both, (count, sections) + both_shape, natural, lambda out, s: out.at[:, s])]

    def unpack_rec(wide, gates):
        return wide.reshape(model, 2 * window), gates.reshape(2, 2, block_width, block_width)

    reach = window - own_width

    def out_window(strip, l):
        strip = jnp.concatenate([strip[0], out_weight[l], strip[1]], axis=0)
        return lax.dynamic_slice_in_dim(strip, reach - offset, window, 0)

    packed = jnp.concatenate(
        [rate_bias[:, None], inflow_bias[:, None], conv_taps, conv_bias[:, None], lru_param[:, None]], axis=1
    )
    gains_own = jnp.stack([rec_gain, mlp_gain], axis=1)
    flat = jnp.concatenate([packed.reshape(-1), gains_own.reshape(-1)]).reshape(16, -1)
    jobs = [Everyone(flat, count)] + spread_rec(0) + line_mlp(0)
    x_all, flat, *rec_got, mlp_line = comm("start", next(next_id), x=x0, jobs=jobs, groups=[(0, 3), (3, 4)])
    flat = flat.reshape(count, -1)
    small_all = flat[:, : packed.size].reshape(count, layers, 8, own_width)
    small_all = jnp.transpose(small_all, (1, 2, 0, 3)).reshape(layers, 8, lru_width)
    gains = flat[:, packed.size :].reshape(count, layers, 2, d_rows)
    gains = jnp.transpose(gains, (1, 2, 0, 3)).reshape(layers, 2, model)
    small = window_of(small_all, 2).astype(f32)
    x_wide = x_all.astype(f32)
    scale = lax.rsqrt(jnp.mean(x_wide * x_wide, axis=-1, keepdims=True) + epsilon)
    normed = (x_wide * scale * gains[0, 0].astype(f32)).astype(bf16)

    masked = (cot.astype(f32) * valid[:, None].astype(f32)).astype(bf16)
    marks = stream_marks(lax.dynamic_index_in_dim(doc_starts, section, 0, False), tokens)
    first_state = window_of(lax.dynamic_index_in_dim(prev_state, section, 0, False), 1).astype(f32)
    first_state = jnp.broadcast_to(first_state[:, None], (layers, 8, window))
    rim = window_of(lax.dynamic_index_in_dim(prev_inputs, section, 0, False), 2).astype(f32)
    rim = jnp.concatenate([jnp.zeros((layers, 5, window), f32), rim], axis=1)
    channel = jnp.arange(window, dtype=jnp.int32)
    own = jnp.logical_and(channel >= offset, channel < offset + own_width).astype(f32)
    own = jnp.broadcast_to(own[None], (8, window))
    pick = (channel[:, None] == jnp.arange(own_width, dtype=jnp.int32)[None] + offset).astype(bf16)

    x = x0
    kept = []
    rec_weights, mlp_weights = [], []
    for l in range(layers):
        wide_weight, gates = unpack_rec(*rec_got)
        rec_weights.append((wide_weight, gates))
        wide = dot(normed, wide_weight)
        gated, *saved = middle_forward(wide, marks, gates, small[l], rim[l], first_state[l], pick)
        part = dot(gated, out_weight[l]).astype(bf16)
        kept.append((x, normed, wide, gated, saved))
        jobs = plane_mlp(mlp_line)
        if l + 1 < layers:
            jobs += line_rec(l + 1)
        else:
            jobs += [Beside(out_weight, m, reach) for m in range(layers)]
        normed, x, both, *rec_line = comm("forward", next(next_id), part, x, gain=gains[l, 1], jobs=jobs)
        mlp_weights.append(both.reshape(model, 2 * hidden_part))
        both = dot(normed, mlp_weights[l])
        hidden = (jax.nn.gelu(both[:, :hidden_part]) * both[:, hidden_part:]).astype(bf16)
        part = dot(hidden, down_weight[l]).astype(bf16)
        kept.append((x, normed, both, hidden))
        if l + 1 < layers:
            jobs = plane_rec(*rec_line) + line_mlp(l + 1)
            normed, x, *rec_got, mlp_line = comm("forward", next(next_id), part, x, gain=gains[l + 1, 0], jobs=jobs)
            if l + 2 == layers:
                tied, normed = lax.optimization_barrier((masked, normed))
                masked_all = lax.all_gather(tied, "seq", axis=0, tiled=True)
        else:
            last_part, last_x = part, x

    strips = rec_line

    mlp_lanes = np.gcd(256, hidden_part).item()
    rec_lanes = np.gcd(128, 2 * own_width).item()

    def by_target(grad, lanes):
        chunks = grad.shape[1] // lanes
        grad = grad.astype(bf16).reshape(count, sections, quarter, chunks, lanes)
        return jnp.transpose(grad, (1, 0, 3, 2, 4)).reshape(sections, count, chunks * quarter, lanes)

    def by_section(grad, lanes):
        rows, chunks = grad.shape[0] // sections, grad.shape[1] // lanes
        grad = grad.astype(bf16).reshape(sections, rows, chunks, lanes)
        return jnp.transpose(grad, (0, 2, 1, 3)).reshape(sections, chunks * rows, lanes)

    def gates_by_target(grad, lanes):
        chunks = block_width // lanes
        grad = grad.astype(bf16).reshape(2, 2, count, sections, block_quarter, chunks, lanes)
        return jnp.transpose(grad, (3, 2, 0, 1, 5, 4, 6)).reshape(sections, count, -1, lanes)

    direct = hidden_part % 256 == 0 and rec_lanes == 128 and own_width % 64 == 0

    def bundle(swapped, shared):
        lanes = swapped.shape[3]
        return jnp.concatenate([swapped.reshape(sections, -1, lanes), shared], axis=1)

    def scatter(whole):
        return lax.psum_scatter(
            whole.reshape(-1, whole.shape[-1]), "section", scatter_dimension=0, tiled=True
        )

    rows_of = {
        "mlp": 2 * hidden_part // mlp_lanes * quarter,
        "rec": (2 * own_width * quarter + 4 * block_width * block_quarter) // rec_lanes,
    }

    def grad_jobs(mine, rows):
        def cut(refs, target):
            return [refs[0].at[pl.ds(pl.multiple_of(target * rows, 8), rows)]]

        return [
            Spread(
                [mine],
                (count, sections, rows, mine.shape[1]),
                1,
                cut,
                lambda view: [view],
                lambda out, source, s: out.at[source, s],
            ),
            Share(mine, count * rows, mine.shape[0] - count * rows),
        ]

    d_rows_own, d_all = masked, masked_all
    dgains = [[None, None] for _ in range(layers)]
    waiting, spread, sums_own = {}, {}, [None] * layers
    for l in reversed(range(layers)):
        x, normed, both, hidden = kept[2 * l + 1]
        d_hidden = dot_t(d_all, down_weight[l])
        gate, slope = gelu_pair(both[:, :hidden_part])
        d_gate = (d_hidden * both[:, hidden_part:] * slope).astype(bf16)
        d_up = (d_hidden * gate).astype(bf16)
        d_both = jnp.concatenate([d_gate, d_up], axis=1)
        part = dot_t(d_both, mlp_weights[l]).astype(bf16)
        if direct:
            whole = grads_mlp(normed, d_both, hidden, d_all, sections, count, mlp_lanes)
        else:
            down = by_section(dot_rows(hidden, d_all), mlp_lanes)
            whole = bundle(by_target(dot_rows(normed, d_both), mlp_lanes), down)
        part, whole = lax.optimization_barrier((part, whole))
        waiting["mlp", l] = scatter(whole)
        if l + 1 < layers:
            part, waiting["rec", l + 1] = lax.optimization_barrier((part, waiting["rec", l + 1]))
        d_all, d_rows_own, dgains[l][1] = comm("back", next(next_id), part, x, d_rows_own, gains[l, 1])

        x, normed, wide, gated, saved = kept[2 * l]
        wide_weight, gates = rec_weights[l]
        d_gated = dot_t(d_all, out_window(strips[l], l))
        dib, d_rate, d_inflow, sums = middle_backward(
            d_gated, wide, saved, marks, gates, small[l], rim[l], own
        )
        part = dot_t(dib, wide_weight).astype(bf16)
        if direct:
            whole = grads_rec(
                normed, dib, gated, d_all, saved[0], d_rate, d_inflow, pick, own_width, sections, count, rec_lanes
            )
        else:
            grad_out = dot_rows(gated, d_all)
            grad_wide = dot_rows(normed, dib)
            swapped = by_target(
                jnp.concatenate(
                    [
                        lax.dynamic_slice_in_dim(grad_wide, offset, own_width, 1),
                        lax.dynamic_slice_in_dim(grad_wide, offset + window, own_width, 1),
                    ],
                    axis=1,
                ),
                rec_lanes,
            )
            low = saved[0].astype(bf16).reshape(tokens, 2, block_width)
            d_gates = jnp.stack([d_rate, d_inflow]).reshape(2, tokens, 2, block_width)
            grad_gates = jnp.einsum("tbi,gtbj->gbij", low, d_gates, preferred_element_type=f32)
            swapped = jnp.concatenate([swapped, gates_by_target(grad_gates, rec_lanes)], axis=2)
            whole = bundle(swapped, by_section(grad_out, rec_lanes))
        sums_own[l] = lax.dynamic_slice_in_dim(sums, offset, own_width, 1)
        part, whole = lax.optimization_barrier((part, whole))
        waiting["rec", l] = scatter(whole)
        part, waiting["mlp", l] = lax.optimization_barrier((part, waiting["mlp", l]))
        if l > 0:
            d_all, d_rows_own, dgains[l][0] = comm("back", next(next_id), part, x, d_rows_own, gains[l, 0])
            continue
        names = [(kind, m) for m in range(1, layers) for kind in ("mlp", "rec")]
        jobs = [job for name in names for job in grad_jobs(waiting[name], rows_of[name[0]])]
        groups = [(2 * i, 2 * i + 2) for i in range(len(names))]
        input_grad, dgains[l][0], *got = comm("last", next(next_id), part, x, d_rows_own, gains[l, 0], jobs, groups)
        for i, name in enumerate(names):
            spread[name] = got[2 * i : 2 * i + 2]

    sums_lanes = -(-own_width // 256) * 256
    sums = jnp.pad(jnp.concatenate(sums_own, axis=0), ((0, 0), (0, sums_lanes - own_width)))
    sums = sums.reshape(-1, 256)
    dgain_all = jnp.concatenate([a for pair in dgains for a in pair], axis=0).reshape(2 * layers, count, d_rows)
    dgain_all = jnp.pad(jnp.transpose(dgain_all, (1, 0, 2)), ((0, 0), (0, 8 - 2 * layers), (0, 256 - d_rows)))
    tiny = jnp.concatenate([dgain_all.reshape(-1, 256), sums], axis=0)
    last_part, last_x, _ = lax.optimization_barrier((last_part, last_x, input_grad))
    jobs = [job for kind in ("mlp", "rec") for job in grad_jobs(waiting[kind, 0], rows_of[kind])]
    outputs, *got, dgain_all, sums = comm(
        "rows", next(next_id), last_part, last_x, jobs=jobs + grad_jobs(tiny, 8), groups=[(0, 2), (2, 4), (4, 6)]
    )
    spread["mlp", 0], spread["rec", 0] = got[:2], got[2:]
    sums = jnp.sum(sums, axis=0).reshape(layers, 8, sums_lanes)[:, :, :own_width]
    dgain_all = jnp.sum(dgain_all, axis=(0, 1))[: 2 * layers, :d_rows].reshape(layers, 2, d_rows)

    def both_layers(name):
        return [spread[name, l][0] for l in range(layers)], [spread[name, l][1] for l in range(layers)]

    def columns(parts, first, last, lanes):
        out = []
        for p in parts:
            chunks = p.shape[2] // quarter
            p = p[:, :, : chunks * quarter].reshape(count, sections, chunks, quarter, lanes)
            p = jnp.transpose(p, (1, 3, 0, 2, 4)).reshape(d_rows, count, chunks * lanes)
            out.append(p[:, :, first:last].reshape(d_rows, -1).astype(f32))
        return jnp.stack(out)

    def rows(parts, size, lanes):
        out = []
        for p in parts:
            p = jnp.transpose(p.reshape(sections, -1, size, lanes), (0, 2, 1, 3))
            out.append(p.reshape(sections * size, -1).astype(f32))
        return jnp.stack(out)

    mlp_swapped, mlp_shared = both_layers("mlp")
    rec_swapped, rec_shared = both_layers("rec")
    if direct:
        gate_grad, up_grad, down_grad = place_mlp(mlp_swapped, mlp_shared, quarter, hidden_part)
        in_grad, side_grad, out_grad, gate_out = place_rec(
            rec_swapped, rec_shared, quarter, own_width, block_width, first_block, owner
        )
    else:
        gate_grad = columns(mlp_swapped, 0, hidden_part, mlp_lanes)
        up_grad = columns(mlp_swapped, hidden_part, 2 * hidden_part, mlp_lanes)
        down_grad = rows(mlp_shared, hidden_part // sections, mlp_lanes)
        in_grad = columns(rec_swapped, 0, own_width, rec_lanes)
        side_grad = columns(rec_swapped, own_width, 2 * own_width, rec_lanes)
        out_grad = rows(rec_shared, own_width // sections, rec_lanes)

        gate_out = []
        for l in range(layers):
            got = rec_swapped[l][:, :, 2 * own_width // rec_lanes * quarter :]
            got = got.reshape(count, sections, 2, 2, block_width // rec_lanes, block_quarter, rec_lanes)
            blocks = jnp.stack([got[owner[b], :, :, b - first_block[owner[b]]] for b in range(block_count)])
            blocks = jnp.transpose(blocks, (2, 0, 1, 4, 3, 5))
            gate_out.append(blocks.reshape(2, block_count, block_rows, block_width))
        gate_out = jnp.stack(gate_out, axis=1).astype(f32)

    return (
        outputs[None],
        input_grad[None],
        dgain_all[:, 0],
        in_grad,
        side_grad,
        out_grad,
        gate_out[0],
        gate_out[1],
        sums[:, 0],
        sums[:, 1],
        sums[:, 2:6],
        sums[:, 6],
        sums[:, 7],
        dgain_all[:, 1],
        gate_grad,
        up_grad,
        down_grad,
    )


def solution(mesh):
    return jax.shard_map(
        on_device,
        mesh=mesh,
        in_specs=(
            P(None, "seq", None),
            P(),
            P(None, "seq"),
            P(None, "seq", None),
            P(),
            P(),
            P(None, "seq"),
            P(None, "seq", None),
            P(None, "seq", None),
            P(None, "seq", None),
            P(None, None, "seq", None),
            P(None, None, "seq", None),
            P(None, "seq"),
            P(None, "seq"),
            P(None, None, "seq"),
            P(None, "seq"),
            P(None, "seq"),
            P(None, "seq"),
            P(None, "seq", None),
            P(None, "seq", None),
            P(None, "seq", None),
        ),
        out_specs=(
            P("section", "seq", None),
            P("section", "seq", None),
            P(None, "seq"),
            P(None, "seq", None),
            P(None, "seq", None),
            P(None, "seq", None),
            P(None, None, "seq", None),
            P(None, None, "seq", None),
            P(None, "seq"),
            P(None, "seq"),
            P(None, None, "seq"),
            P(None, "seq"),
            P(None, "seq"),
            P(None, "seq"),
            P(None, "seq", None),
            P(None, "seq", None),
            P(None, "seq", None),
        ),
        check_vma=False,
    )
```
